32 devices in a mesh: dp: 32 (over z, y, x, core).
Axes of the slice: x: 2, y: 2, z: 4, core: 2. Of those that a mesh axis runs over, the one named last changes fastest.
Arguments:
- images: bfloat16 [768, 197, 384], P('dp'), may hold values from -40 to 40
- cotangent: bfloat16 [768, 197, 384], P('dp'), may hold values from -6 to 6
- master: float32 [1774080], P('dp'), may hold values from -1.5 to 1.5
- moment_one: float32 [1774080], P('dp'), may hold values from -240 to 240
- moment_two: float32 [1774080], P('dp'), may hold values from 20 to 2000
- batch_ends: int32 [32, 3], P('dp'), may hold values from 1 to 24, as said below
Outputs:
- block_out: bfloat16 [768, 197, 384], P('dp')
- input_grad: float32 [768, 197, 384], P('dp')
- weight_grad: float32 [1774080], P('dp')
- first_moment: float32 [1774080], P('dp')
- second_moment: float32 [1774080], P('dp')
- update: float32 [1774080], P('dp')
The draws below stay inside these ranges and needn't reach their ends.
Inputs may be any that keep to these rules, and one draw needn't show every extreme that they name: Micro-batch m of device d holds its image slots batch_ends[d, m - 1] (0 for m = 0) to batch_ends[d, m] - 1; each micro-batch holds 1 to 8 images, and some micro-batch of some device holds exactly 8. Slots from batch_ends[d, 2] on are empty.
All inputs are finite; a program needn't handle non-finite values.
Results may differ from the reference program's by a relative error of at most 0.0092.
Values may be sent and summed in bfloat16 or wider, within the bound.
A program may use at most 320 MiB of HBM per device.

```python
import math
import jax
import jax.numpy as jnp
from jax import lax

D = 384
FF = 1536
HEADS = 6
HEAD_DIM = 64
TOK_IMG = 197
MB = 3
MB_CAP = 8
STEP = 10
IMG_DEV = 24
IMAGES = 768
P_SIZE = 1774080
N_DP = 32


def draw_images(key, part):
    key_base, key_rows, key_cols = jax.random.split(key, 3)
    shape_all = (IMAGES, TOK_IMG, D)
    row_scale = jnp.exp(jax.random.uniform(key_rows, (IMAGES, TOK_IMG, 1), jnp.float32, math.log(0.3), math.log(3.0)))
    col_scale = jnp.exp(jax.random.uniform(key_cols, (1, 1, D), jnp.float32, math.log(0.3), math.log(3.0)))
    values = jax.random.truncated_normal(key_base, -4.0, 4.0, shape_all, jnp.float32)
    return (values * row_scale * col_scale).astype(jnp.bfloat16)


def draw_master(key, part):
    position = jnp.arange(P_SIZE, dtype=jnp.int32)
    noise = jax.random.truncated_normal(key, -4.0, 4.0, (P_SIZE,), jnp.float32)
    qkv_end = 3 * D * D
    out_end = qkv_end + D * D
    up_end = out_end + D * FF
    down_end = up_end + FF * D
    is_gain = (position >= down_end) & (position < down_end + D) | (position >= down_end + 2 * D) & (position < down_end + 3 * D)
    small_scale = jnp.where(is_gain, 0.1, 0.2)
    scale_vec = jnp.where(position < qkv_end, D ** (-0.5), jnp.where(position < out_end, 3.0 * D ** (-0.5), jnp.where(position < up_end, D ** (-0.5), jnp.where(position < down_end, FF ** (-0.5), small_scale))))
    return (noise * scale_vec + jnp.where(is_gain, 1.0, 0.0)).astype(jnp.float32)


def draw_batch_ends(key, part):
    key_sizes, key_device, key_micro = jax.random.split(key, 3)
    sizes_drawn = jax.random.randint(key_sizes, (N_DP, MB), 1, MB_CAP + 1)
    device_pick = jax.random.randint(key_device, (), 0, N_DP)
    micro_pick = jax.random.randint(key_micro, (), 0, MB)
    chosen = (jnp.arange(N_DP)[:, None] == device_pick) & (jnp.arange(MB)[None, :] == micro_pick)
    sizes_drawn = jnp.where(chosen, MB_CAP, sizes_drawn)
    return jnp.cumsum(sizes_drawn, axis=1).astype(jnp.int32)


def block_scale(own_key, extent, shards, low, high):
    factor_of = 1.0
    for dim, parts in shards:
        heights = jax.random.uniform(jax.random.fold_in(jax.random.fold_in(own_key, 6), dim), (parts,), jnp.float32, low / len(shards), high / len(shards))
        factor_of = factor_of * jnp.repeat(jnp.exp(heights), extent[dim] // parts).reshape((-1,) + (1,) * (len(extent) - 1 - dim))
    return factor_of


def scatter_about(rng, shape, scale, limit, cuts=(), kind=jnp.bfloat16):
    entries = jax.random.normal(rng, shape, jnp.float32) * scale
    if len(cuts) > 0:
        entries = block_scale(rng, shape, cuts, -0.22, 0.18) * entries
    return jnp.clip(entries, min=-limit, max=limit).astype(kind)


def setup_inputs(seed: int = 0) -> dict:
    keys = jax.random.split(jax.random.key(seed), 7)
    images = draw_images(jax.random.fold_in(keys[6], 71), 0)
    cotangent = scatter_about(keys[1], (IMAGES, TOK_IMG, D), 1.0, 6.0, ((0, 32),))
    master = draw_master(jax.random.fold_in(keys[6], 71), 0)
    moment_one = scatter_about(keys[3], (P_SIZE,), 40.0, 240.0, ((0, 32),), jnp.float32)
    moment_two = jnp.clip(jnp.exp(math.log(2000.0) - 4.6051702 * jax.random.uniform(keys[4], (P_SIZE,), jnp.float32) ** block_scale(keys[4], (P_SIZE,), ((0, 32),), -0.2, 0.2)), 20.0, 2000.0)
    batch_ends = draw_batch_ends(jax.random.fold_in(keys[6], 71), 0)
    return dict(images=images, cotangent=cotangent, master=master, moment_one=moment_one, moment_two=moment_two, batch_ends=batch_ends)


@jax.custom_vjp
def low(v):
    return lax.optimization_barrier(v.astype(jnp.bfloat16)).astype(jnp.float32)

@jax.custom_vjp
def low_back(v):
    return v

def low_keep(v):
    return (low(v), None)

def low_pass(kept, grad):
    return (grad,)

def back_keep(v):
    return (v, None)

def back_low(kept, grad):
    return (low(grad),)
low.defvjp(low_keep, low_pass)
low_back.defvjp(back_keep, back_low)
highest = lax.Precision.HIGHEST
beta_one = 0.9
beta_two = 0.999
learn_rate = 0.01
decay_rate = 0.05
adam_eps = 1e-08
norm_eps = 1e-06

def matmul(left, right):
    return jnp.dot(left, right, precision=highest, preferred_element_type=jnp.float32)

def layer_norm(values, gain_vec, shift_vec):
    centre = lax.optimization_barrier(jnp.mean(values, axis=-1, keepdims=True))
    centered = values - centre
    spread = lax.optimization_barrier(jnp.mean(centered * centered, axis=-1, keepdims=True))
    return centered * lax.rsqrt(spread + norm_eps) * gain_vec + shift_vec

def unpack(flat_vec):
    lengths = [3 * D * D, D * D, D * FF, FF * D, D, D, D, D, D, D, D, D, FF]
    pieces = []
    offset = 0
    for length_one in lengths:
        pieces.append(flat_vec[offset:offset + length_one])
        offset = offset + length_one
    shapes = [(D, 3 * D), (D, D), (D, FF), (FF, D)]
    return [pieces[number].reshape(shapes[number]) for number in range(4)] + pieces[4:]

def forward(theta, batch_images, live_mask):
    unpacked = unpack(low(theta))
    w_qkv, w_out, w_up, w_down = unpacked[:4]
    gain_one, shift_one, gain_two, shift_two, bias_query, bias_value, bias_out, bias_down, bias_up = unpacked[4:]
    count_img = batch_images.shape[0]
    rows_in = batch_images.reshape(count_img * TOK_IMG, D)
    normed_one = low(layer_norm(rows_in, gain_one, shift_one))
    bias_qkv = jnp.concatenate([bias_query, jnp.zeros_like(bias_query), bias_value])
    qkv = low_back(low(matmul(normed_one, w_qkv) + bias_qkv))
    qkv = qkv.reshape(count_img, TOK_IMG, 3, HEADS, HEAD_DIM)
    query_heads = qkv[:, :, 0]
    key_heads = qkv[:, :, 1]
    value_heads = qkv[:, :, 2]
    scores = low_back(jnp.einsum('nqhe,nkhe->nhqk', query_heads, key_heads, precision=highest) * HEAD_DIM ** (-0.5))
    soft_probs = jax.nn.softmax(scores, axis=-1)
    mixed_heads = jnp.einsum('nhqk,nkhe->nqhe', low(soft_probs), value_heads, precision=highest)
    mixed_rows = low_back(low(mixed_heads.reshape(count_img * TOK_IMG, D)))
    branch = low_back(matmul(mixed_rows, w_out) + bias_out)
    middle = rows_in + branch
    normed_two = low(layer_norm(middle, gain_two, shift_two))
    hidden_pre = low_back(matmul(normed_two, w_up) + bias_up)
    active = low(jax.nn.gelu(hidden_pre, approximate=False))
    result = middle + matmul(active, w_down) + bias_down
    return result.reshape(count_img, TOK_IMG, D) * live_mask[:, None, None]

def reference(images, cotangent, master, moment_one, moment_two, batch_ends):
    counts = batch_ends[:, MB - 1]
    slots = jnp.arange(IMG_DEV, dtype=jnp.int32)
    live = (slots[None, :] < counts[:, None]).astype(jnp.float32)
    group_images = images.reshape(N_DP, IMG_DEV, TOK_IMG, D)
    group_cot = cotangent.reshape(N_DP, IMG_DEV, TOK_IMG, D)

    def group_step(total, group):
        batch_images, upstream, live_mask = group

        def local_forward(theta, values):
            return forward(theta, values, live_mask)
        result, pull_back = jax.vjp(local_forward, master, batch_images.astype(jnp.float32))
        grad_theta, grad_images = pull_back(upstream.astype(jnp.float32))
        return (total + grad_theta, (result.astype(jnp.bfloat16), grad_images))
    weight_grad, (outputs, input_grads) = lax.scan(group_step, jnp.zeros_like(master), (group_images, group_cot, live))
    first_moment = beta_one * moment_one + (1.0 - beta_one) * weight_grad
    second_moment = beta_two * moment_two + (1.0 - beta_two) * weight_grad * weight_grad
    corrected_one = first_moment / (1.0 - beta_one ** STEP)
    corrected_two = second_moment / (1.0 - beta_two ** STEP)
    update = -learn_rate * (corrected_one / (jnp.sqrt(corrected_two) + adam_eps) + decay_rate * master)
    return (outputs.reshape(IMAGES, TOK_IMG, D), input_grads.reshape(IMAGES, TOK_IMG, D), weight_grad, first_moment, second_moment, update)
```

```python
import jax, jax.numpy as jnp, functools
from jax import lax
from jax.experimental import pallas as pl
from jax.experimental.pallas import tpu as pltpu
from jax.sharding import PartitionSpec as P

D = 384
FF = 1536
HEADS = 6
HEAD_DIM = 64
TOK = 197
TP = 208
G = 2
ROWS = G * TP
MB = 3
STEP = 10
CH = 32
FFC = 384

beta_one = 0.9
beta_two = 0.999
learn_rate = 0.01
decay_rate = 0.05
adam_eps = 1e-08
norm_eps = 1e-06
f32 = jnp.float32
bf16 = jnp.bfloat16

LANES = 128
TILE = 8 * LANES
MATS = ((0, D, 3 * D), (3456, D, D), (4608, D, FF), (9216, FF, D))
VEC_ROW = 13824
FLAT_ROWS = 13860
VMEM_LIMIT = 60 * 2**20


def dot(a, b, ca=1, cb=0):
    return lax.dot_general(a, b, (((ca,), (cb,)), ((), ())), preferred_element_type=f32)


def chunk_rows(shard):
    return ((shard + TILE - 1 + LANES - 1) // LANES + 15) // 16 * 16


def first_tile(shard, d):
    return (shard * d) // TILE


def compute_kernel(n, shard, cap, slots, meta, images, cot, p_images, p_cot, wbuf,
                   block_out, input_grad, p_out, p_grad, gbuf,
                   flat, w_qkv, w_o, w_1, w_2, vecs, g_qkv, g_o, g_1, g_2t, vsum,
                   xin, gin, oout, gout, x_s, n1_s, r1_s, a1_s, qkv_s, prob_s, o_s, m_s, n2_s, r2_s, a2_s,
                   g_s, u_s, act_s, du_s, acc_s, da_s, dm_s, db_s, do_s, dqkv_s, zero_b, zero_f,
                   in_sem, out_sem, zero_sem):
    rows_c = wbuf.shape[1]
    own_first = meta[0]
    own_n = meta[1]
    part_n = meta[2]
    live_n = meta[3]
    items = own_n + part_n
    steps = (items + G - 1) // G

    def fetch(step, slot, do):
        for i in range(G):
            item = jnp.minimum(step * G + i, items - 1)
            is_own = item < own_n

            @pl.when(is_own)
            def _():
                s = own_first + item
                for k, (src, dst) in enumerate(((images, xin), (cot, gin))):
                    c = pltpu.make_async_copy(src.at[s], dst.at[slot, i], in_sem.at[slot, i, k])
                    c.start() if do else c.wait()

            @pl.when(jnp.logical_not(is_own))
            def _():
                s = item - own_n
                for k, (src, dst) in enumerate(((p_images, xin), (p_cot, gin))):
                    c = pltpu.make_async_copy(src.at[s], dst.at[slot, i], in_sem.at[slot, i, k])
                    c.start() if do else c.wait()

    def flush(step, slot, do):
        for i in range(G):
            item = step * G + i
            is_own = item < own_n

            @pl.when(is_own)
            def _():
                s = own_first + item
                for k, (dst, src) in enumerate(((block_out, oout), (input_grad, gout))):
                    c = pltpu.make_async_copy(src.at[slot, i], dst.at[s], out_sem.at[slot, i, k])
                    c.start() if do else c.wait()

            @pl.when(jnp.logical_and(jnp.logical_not(is_own), item < items))
            def _():
                s = item - own_n
                for k, (dst, src) in enumerate(((p_out, oout), (p_grad, gout))):
                    c = pltpu.make_async_copy(src.at[slot, i], dst.at[s], out_sem.at[slot, i, k])
                    c.start() if do else c.wait()

    def zeros_copy(do):
        def one(s, carry):
            a = pltpu.make_async_copy(zero_b, block_out.at[s], zero_sem.at[0])
            b = pltpu.make_async_copy(zero_f, input_grad.at[s], zero_sem.at[1])
            a.start() if do else a.wait()
            b.start() if do else b.wait()
            return carry
        lax.fori_loop(live_n, slots, one, 0)

    fetch(0, 0, True)
    zero_b[...] = jnp.zeros(zero_b.shape, bf16)
    zero_f[...] = jnp.zeros(zero_f.shape, f32)
    zeros_copy(True)
    end = 0
    for d in range(n):
        top = 8 * first_tile(shard, d)
        if d == 0:
            flat[pl.ds(0, rows_c), :] = wbuf[0].astype(f32)
        else:
            shared = min(end - top, rows_c)
            flat[pl.ds(top, shared), :] += wbuf[d, pl.ds(0, shared), :].astype(f32)
            if shared < rows_c:
                flat[pl.ds(top + shared, rows_c - shared), :] = wbuf[d, pl.ds(shared, rows_c - shared), :].astype(f32)
        end = top + rows_c
    for ref, (row, height, width) in zip((w_qkv, w_o, w_1, w_2), MATS):
        blocks = width // LANES
        for j in range(blocks):
            ref[:, j * LANES:(j + 1) * LANES] = flat[pl.ds(row + j, height, stride=blocks), :].astype(bf16)
    for k in range(8):
        for j in range(3):
            vecs[k, j * LANES:(j + 1) * LANES] = flat[VEC_ROW + 3 * k + j, :]
    for j in range(12):
        vecs[8, j * LANES:(j + 1) * LANES] = flat[VEC_ROW + 24 + j, :]
    for ref in (g_qkv, g_o, g_1, g_2t, vsum):
        ref[...] = jnp.zeros(ref.shape, f32)
    for ref in (x_s, g_s):
        ref[...] = jnp.zeros(ref.shape, ref.dtype)

    g1 = vecs[0:1, :D]
    b1 = vecs[1:2, :D]
    g2 = vecs[2:3, :D]
    b2 = vecs[3:4, :D]
    cq = vecs[4:5, :D]
    cv = vecs[5:6, :D]
    co = vecs[6:7, :D]
    c2 = vecs[7:8, :D]

    lane = lax.broadcasted_iota(jnp.int32, (1, LANES), 1)
    low_half = lane < HEAD_DIM

    def colsum(v):
        return jnp.sum(v.reshape(v.shape[0] // 8, 8, v.shape[1]), axis=0)

    def mean(v):
        return jnp.sum(v, axis=-1, keepdims=True) * (1.0 / D)

    def body(step, carry):
        slot = lax.rem(step, 2)
        fetch(step, slot, False)

        @pl.when(step + 1 < steps)
        def _():
            fetch(step + 1, 1 - slot, True)

        for i in range(G):
            live = (step * G + i < items).astype(bf16)
            x_s[pl.ds(i * TP, TOK), :] = xin[slot, i].astype(f32)
            g_s[pl.ds(i * TP, TOK), :] = gin[slot, i] * live
        for r in range(0, ROWS, CH):
            rs = pl.ds(r, CH)
            v = x_s[rs, :]
            c = v - mean(v)
            inv = lax.rsqrt(mean(c * c) + norm_eps)
            nv = c * inv
            n1_s[rs, :] = nv
            r1_s[rs, :] = jnp.broadcast_to(inv, (CH, LANES))
            a1_s[rs, :] = (nv * g1 + b1).astype(bf16)
        a1 = a1_s[...]
        for k, bias in ((0, cq), (1, None), (2, cv)):
            cols = slice(k * D, (k + 1) * D)
            t = dot(a1, w_qkv[:, cols])
            qkv_s[:, cols] = (t if bias is None else t + bias).astype(bf16)
        key_live = lax.broadcasted_iota(jnp.int32, (1, TP), 1) < TOK
        for i in range(G):
            ir = pl.ds(i * TP, TP)
            for p in range(HEADS // 2):
                cols = slice(p * LANES, (p + 1) * LANES)
                q = qkv_s[ir, cols] * 0.125
                k = qkv_s[ir, slice(D + p * LANES, D + (p + 1) * LANES)]
                v = qkv_s[ir, slice(2 * D + p * LANES, 2 * D + (p + 1) * LANES)]
                zero = jnp.zeros_like(q)
                qm = jnp.concatenate([jnp.where(low_half, q, zero), jnp.where(low_half, zero, q)], axis=0)
                s = dot(qm, k, 1, 1)
                s = jnp.where(key_live, s, -1e30)
                e = jnp.exp(s - jnp.max(s, axis=-1, keepdims=True))
                pr = e / jnp.sum(e, axis=-1, keepdims=True)
                prob_s[i * 3 + p] = pr
                o2 = dot(pr.astype(bf16), v)
                o_s[ir, cols] = jnp.where(low_half, o2[:TP], o2[TP:]).astype(bf16)
        m_s[...] = dot(o_s[...], w_o[...])
        for r in range(0, ROWS, CH):
            rs = pl.ds(r, CH)
            v = x_s[rs, :] + m_s[rs, :] + co
            m_s[rs, :] = v
            c = v - mean(v)
            inv = lax.rsqrt(mean(c * c) + norm_eps)
            nv = c * inv
            n2_s[rs, :] = nv
            r2_s[rs, :] = jnp.broadcast_to(inv, (CH, LANES))
            a2_s[rs, :] = (nv * g2 + b2).astype(bf16)
        a2 = a2_s[...]
        gl = g_s[...]
        for j in range(FF // FFC):
            cols = slice(j * FFC, (j + 1) * FFC)
            b = j % 2
            u_s[b] = dot(a2, w_1[:, cols])
            da_s[b] = dot(gl, w_2[cols, :], 1, 1)
            c1 = vecs[8:9, cols]
            tot = None
            for r in range(0, ROWS, CH):
                rs = pl.ds(r, CH)
                u = u_s[b, rs, :] + c1
                phi = 0.5 + 0.5 * lax.erf(u * 0.7071067811865476)
                dens = jnp.exp(u * u * -0.5) * 0.3989422804014327
                act_s[b, rs, :] = (u * phi).astype(bf16)
                du = (da_s[b, rs, :] * (phi + u * dens)).astype(bf16)
                du_s[b, rs, :] = du
                part = colsum(du.astype(f32))
                tot = part if tot is None else tot + part
            vsum[8, :, cols] += tot
            act = act_s[b]
            du = du_s[b]
            if j == 0:
                acc_s[...] = dot(act, w_2[cols, :])
                dm_s[...] = dot(du, w_1[:, cols], 1, 1)
            else:
                acc_s[...] += dot(act, w_2[cols, :])
                dm_s[...] += dot(du, w_1[:, cols], 1, 1)
            g_1[:, cols] += dot(a2, du, 0, 0)
            g_2t[:, cols] += dot(gl, act, 0, 0)
        tg2 = tb2 = tco = tc2 = None
        for r in range(0, ROWS, CH):
            rs = pl.ds(r, CH)
            gw = g_s[rs, :].astype(f32)
            acc_s[rs, :] = m_s[rs, :] + acc_s[rs, :] + c2
            e2 = dm_s[rs, :]
            nv = n2_s[rs, :]
            en = e2 * nv
            eg = e2 * g2
            inv = r2_s[rs, :]
            inv = jnp.concatenate([inv, inv, inv], axis=1)
            dm = gw + inv * (eg - mean(eg) - nv * mean(en * g2))
            dm_s[rs, :] = dm
            db = dm.astype(bf16)
            db_s[rs, :] = db
            sums = (colsum(en), colsum(e2), colsum(db.astype(f32)), colsum(gw))
            if tg2 is None:
                tg2, tb2, tco, tc2 = sums
            else:
                tg2, tb2, tco, tc2 = tg2 + sums[0], tb2 + sums[1], tco + sums[2], tc2 + sums[3]
        vsum[2, :, :D] += tg2
        vsum[3, :, :D] += tb2
        vsum[6, :, :D] += tco
        vsum[7, :, :D] += tc2

        @pl.when(step >= 2)
        def _():
            flush(step - 2, slot, False)

        for i in range(G):
            oout[slot, i] = acc_s[pl.ds(i * TP, TOK), :].astype(bf16)
        db = db_s[...]
        g_o[...] += dot(o_s[...], db, 0, 0)
        do_s[...] = dot(db, w_o[...], 1, 1).astype(bf16)
        for i in range(G):
            ir = pl.ds(i * TP, TP)
            for p in range(HEADS // 2):
                cols = slice(p * LANES, (p + 1) * LANES)
                q = qkv_s[ir, cols] * 0.125
                k = qkv_s[ir, slice(D + p * LANES, D + (p + 1) * LANES)]
                v = qkv_s[ir, slice(2 * D + p * LANES, 2 * D + (p + 1) * LANES)]
                do = do_s[ir, cols]
                zero = jnp.zeros_like(q)
                qm = jnp.concatenate([jnp.where(low_half, q, zero), jnp.where(low_half, zero, q)], axis=0)
                dom = jnp.concatenate([jnp.where(low_half, do, zero), jnp.where(low_half, zero, do)], axis=0)
                pr = prob_s[i * 3 + p]
                dp = dot(dom, v, 1, 1)
                delta = jnp.sum(pr * dp, axis=-1, keepdims=True)
                ds = (pr * (dp - delta)).astype(bf16)
                dv = dot(pr.astype(bf16), dom, 0, 0)
                dk = dot(ds, qm, 0, 0)
                dq2 = dot(ds, k * 0.125)
                dq = jnp.where(low_half, dq2[:TP], dq2[TP:])
                dqkv_s[ir, cols] = dq.astype(bf16)
                dqkv_s[ir, slice(D + p * LANES, D + (p + 1) * LANES)] = dk.astype(bf16)
                dqkv_s[ir, slice(2 * D + p * LANES, 2 * D + (p + 1) * LANES)] = dv.astype(bf16)
        dqkv = dqkv_s[...]
        acc_s[...] = dot(dqkv, w_qkv[...], 1, 1)
        g_qkv[...] += dot(a1_s[...], dqkv, 0, 0)
        tg1 = tb1 = tcq = tcv = None
        for r in range(0, ROWS, CH):
            rs = pl.ds(r, CH)
            e1 = acc_s[rs, :]
            nv = n1_s[rs, :]
            en = e1 * nv
            eg = e1 * g1
            inv = r1_s[rs, :]
            inv = jnp.concatenate([inv, inv, inv], axis=1)
            dm_s[rs, :] += inv * (eg - mean(eg) - nv * mean(en * g1))
            sums = (colsum(en), colsum(e1), colsum(dqkv_s[rs, :D].astype(f32)), colsum(dqkv_s[rs, 2 * D:].astype(f32)))
            if tg1 is None:
                tg1, tb1, tcq, tcv = sums
            else:
                tg1, tb1, tcq, tcv = tg1 + sums[0], tb1 + sums[1], tcq + sums[2], tcv + sums[3]
        vsum[0, :, :D] += tg1
        vsum[1, :, :D] += tb1
        vsum[4, :, :D] += tcq
        vsum[5, :, :D] += tcv
        for i in range(G):
            gout[slot, i] = dm_s[pl.ds(i * TP, TOK), :]
        flush(step, slot, True)
        return carry

    lax.fori_loop(0, steps, body, 0)

    for ref, (row, height, width) in zip((g_qkv, g_o, g_1), MATS):
        blocks = width // LANES
        for j in range(blocks):
            flat[pl.ds(row + j, height, stride=blocks), :] = ref[:, j * LANES:(j + 1) * LANES]
    row = MATS[3][0]
    for c in range(FF // LANES):
        t = g_2t[:, c * LANES:(c + 1) * LANES].T
        for j in range(3):
            flat[pl.ds(row + 3 * LANES * c + j, LANES, stride=3), :] = t[:, j * LANES:(j + 1) * LANES]
    for k in range(9):
        t = jnp.sum(vsum[k], axis=0, keepdims=True)
        for j in range(12 if k == 8 else 3):
            flat[pl.ds(VEC_ROW + 3 * k + j, 1), :] = t[:, j * LANES:(j + 1) * LANES]
    flat[pl.ds(FLAT_ROWS, flat.shape[0] - FLAT_ROWS), :] = jnp.zeros((flat.shape[0] - FLAT_ROWS, LANES), f32)
    for d in range(n):
        gbuf[d] = flat[pl.ds(8 * first_tile(shard, d), rows_c), :].astype(bf16)

    @pl.when(steps >= 2)
    def _():
        flush(steps - 2, lax.rem(steps, 2), False)
    flush(steps - 1, lax.rem(steps + 1, 2), False)
    zeros_copy(False)


def flat_height(n, shard):
    return 8 * first_tile(shard, n - 1) + chunk_rows(shard)


def block_call(n, shard, cap, meta, images, cot, p_images, p_cot, wbuf):
    slots = images.shape[0]
    anyspace = pl.BlockSpec(memory_space=pl.ANY)
    vm = pl.BlockSpec(memory_space=pltpu.VMEM)
    rows_c = chunk_rows(shard)
    scratch = [
        pltpu.VMEM((flat_height(n, shard), LANES), f32),
        pltpu.VMEM((D, 3 * D), bf16), pltpu.VMEM((D, D), bf16), pltpu.VMEM((D, FF), bf16), pltpu.VMEM((FF, D), bf16),
        pltpu.VMEM((16, FF), f32),
        pltpu.VMEM((D, 3 * D), f32), pltpu.VMEM((D, D), f32), pltpu.VMEM((D, FF), f32), pltpu.VMEM((D, FF), f32),
        pltpu.VMEM((9, 8, FF), f32),
        pltpu.VMEM((2, G, TOK, D), bf16), pltpu.VMEM((2, G, TOK, D), bf16),
        pltpu.VMEM((2, G, TOK, D), bf16), pltpu.VMEM((2, G, TOK, D), f32),
        pltpu.VMEM((ROWS, D), f32),
        pltpu.VMEM((ROWS, D), f32), pltpu.VMEM((ROWS, LANES), f32), pltpu.VMEM((ROWS, D), bf16),
        pltpu.VMEM((ROWS, 3 * D), bf16),
        pltpu.VMEM((G * 3, 2 * TP, TP), f32),
        pltpu.VMEM((ROWS, D), bf16),
        pltpu.VMEM((ROWS, D), f32),
        pltpu.VMEM((ROWS, D), f32), pltpu.VMEM((ROWS, LANES), f32), pltpu.VMEM((ROWS, D), bf16),
        pltpu.VMEM((ROWS, D), bf16),
        pltpu.VMEM((2, ROWS, FFC), f32), pltpu.VMEM((2, ROWS, FFC), bf16), pltpu.VMEM((2, ROWS, FFC), bf16),
        pltpu.VMEM((ROWS, D), f32),
        pltpu.VMEM((2, ROWS, FFC), f32),
        pltpu.VMEM((ROWS, D), f32), pltpu.VMEM((ROWS, D), bf16), pltpu.VMEM((ROWS, D), bf16),
        pltpu.VMEM((ROWS, 3 * D), bf16),
        pltpu.VMEM((TOK, D), bf16), pltpu.VMEM((TOK, D), f32),
        pltpu.SemaphoreType.DMA((2, G, 2)), pltpu.SemaphoreType.DMA((2, G, 2)), pltpu.SemaphoreType.DMA((2,)),
    ]
    return pl.pallas_call(
        functools.partial(compute_kernel, n, shard, cap, slots),
        name="block",
        out_shape=(
            jax.ShapeDtypeStruct(images.shape, bf16),
            jax.ShapeDtypeStruct(images.shape, f32),
            jax.ShapeDtypeStruct((cap,) + images.shape[1:], bf16),
            jax.ShapeDtypeStruct((cap,) + images.shape[1:], f32),
            jax.ShapeDtypeStruct((n, rows_c, LANES), bf16),
        ),
        in_specs=[pl.BlockSpec(memory_space=pltpu.SMEM), anyspace, anyspace, anyspace, anyspace, vm],
        out_specs=(anyspace, anyspace, anyspace, anyspace, vm),
        scratch_shapes=scratch,
        compiler_params=pltpu.CompilerParams(vmem_limit_bytes=VMEM_LIMIT),
    )(meta, images, cot, p_images, p_cot, wbuf)


def pack_shard(n, shard, values):
    me = lax.axis_index("dp")
    offset = lax.rem(shard * me, TILE)
    padded = lax.dynamic_update_slice_in_dim(jnp.zeros((chunk_rows(shard) * LANES,), values.dtype), values, offset, 0)
    return padded.reshape(chunk_rows(shard), LANES)


def unpack_shard(n, shard, chunk):
    me = lax.axis_index("dp")
    offset = lax.rem(shard * me, TILE)
    return lax.dynamic_slice_in_dim(chunk.reshape(-1), offset, shard, 0)


def body(n, images, cotangent, master, moment_one, moment_two, batch_ends):
    shard = master.shape[0]
    cap = 2
    live_n = batch_ends[0, MB - 1]
    chunk = pack_shard(n, shard, master.astype(bf16))
    wbuf = lax.all_gather(chunk, "dp", axis=0)
    zero = jnp.zeros((), jnp.int32)
    meta = jnp.stack([zero, live_n, zero, live_n])
    block_out, input_grad, p_out, p_grad, gbuf = block_call(n, shard, cap, meta, images, cotangent, images[:cap], cotangent[:cap], wbuf)
    part = lax.psum_scatter(gbuf.astype(f32), "dp", scatter_dimension=0, tiled=False)
    weight_grad = unpack_shard(n, shard, part)
    first_moment = beta_one * moment_one + (1.0 - beta_one) * weight_grad
    second_moment = beta_two * moment_two + (1.0 - beta_two) * weight_grad * weight_grad
    corrected_one = first_moment / (1.0 - beta_one**STEP)
    corrected_two = second_moment / (1.0 - beta_two**STEP)
    update = -learn_rate * (corrected_one / (jnp.sqrt(corrected_two) + adam_eps) + decay_rate * master)
    return (block_out, input_grad, weight_grad, first_moment, second_moment, update)


def solution(mesh):
    n = mesh.shape["dp"]
    return jax.shard_map(
        functools.partial(body, n),
        mesh=mesh,
        in_specs=(P("dp", None, None), P("dp", None, None), P("dp"), P("dp"), P("dp"), P("dp", None)),
        out_specs=(P("dp", None, None), P("dp", None, None), P("dp"), P("dp"), P("dp"), P("dp")),
        check_vma=False,
    )
```

```python
import jax, jax.numpy as jnp, functools
from jax import lax
from jax.experimental import pallas as pl
from jax.experimental.pallas import tpu as pltpu
from jax.sharding import PartitionSpec as P

D = 384
FF = 1536
HEADS = 6
HEAD_DIM = 64
TOK = 197
TP = 208
G = 2
ROWS = G * TP
MB = 3
STEP = 10
CH = 32
FFC = 384

beta_one = 0.9
beta_two = 0.999
learn_rate = 0.01
decay_rate = 0.05
adam_eps = 1e-08
norm_eps = 1e-06
f32 = jnp.float32
bf16 = jnp.bfloat16

LANES = 128
TILE = 8 * LANES
MATS = ((0, D, 3 * D), (3456, D, D), (4608, D, FF), (9216, FF, D))
VEC_ROW = 13824
FLAT_ROWS = 13860
VMEM_LIMIT = 60 * 2**20
CAP = 6


def dot(a, b, ca=1, cb=0):
    return lax.dot_general(a, b, (((ca,), (cb,)), ((), ())), preferred_element_type=f32)


def chunk_rows(shard):
    return ((shard + TILE - 1 + LANES - 1) // LANES + 15) // 16 * 16


def first_tile(shard, d):
    return (shard * d) // TILE


def compute_kernel(n, shard, cap, slots, ends, other, images, cot, p_images, p_cot, wbuf,
                   block_out, input_grad, p_out, p_grad, gbuf,
                   flat, w_qkv, w_o, w_1, w_2, vecs, g_qkv, g_o, g_1, g_2t, vsum,
                   xin, gin, oout, gout, x_s, n1_s, r1_s, a1_s, qkv_s, prob_s, o_s, m_s, n2_s, r2_s, a2_s,
                   g_s, u_s, act_s, du_s, acc_s, da_s, dm_s, db_s, do_s, dqkv_s, zero_b, zero_f,
                   in_sem, out_sem, zero_sem):
    rows_c = wbuf.shape[1]
    live_n = ends[0, MB - 1]
    diff = live_n - other[0, 0]
    own_first = jnp.clip(diff // 2, 0, cap)
    own_n = live_n - own_first
    part_n = jnp.clip((0 - diff) // 2, 0, cap)
    items = own_n + part_n
    steps = (items + G - 1) // G

    def fetch(step, slot, do):
        for i in range(G):
            item = jnp.minimum(step * G + i, items - 1)
            is_own = item < own_n

            @pl.when(is_own)
            def _():
                s = own_first + item
                for k, (src, dst) in enumerate(((images, xin), (cot, gin))):
                    c = pltpu.make_async_copy(src.at[s], dst.at[slot, i], in_sem.at[slot, i, k])
                    c.start() if do else c.wait()

            @pl.when(jnp.logical_not(is_own))
            def _():
                s = item - own_n
                for k, (src, dst) in enumerate(((p_images, xin), (p_cot, gin))):
                    c = pltpu.make_async_copy(src.at[s], dst.at[slot, i], in_sem.at[slot, i, k])
                    c.start() if do else c.wait()

    def flush(step, slot, do):
        for i in range(G):
            item = step * G + i
            is_own = item < own_n

            @pl.when(is_own)
            def _():
                s = own_first + item
                for k, (dst, src) in enumerate(((block_out, oout), (input_grad, gout))):
                    c = pltpu.make_async_copy(src.at[slot, i], dst.at[s], out_sem.at[slot, i, k])
                    c.start() if do else c.wait()

            @pl.when(jnp.logical_and(jnp.logical_not(is_own), item < items))
            def _():
                s = item - own_n
                for k, (dst, src) in enumerate(((p_out, oout), (p_grad, gout))):
                    c = pltpu.make_async_copy(src.at[slot, i], dst.at[s], out_sem.at[slot, i, k])
                    c.start() if do else c.wait()

    def zeros_copy(do):
        def one(s, carry):
            a = pltpu.make_async_copy(zero_b, block_out.at[s], zero_sem.at[0])
            b = pltpu.make_async_copy(zero_f, input_grad.at[s], zero_sem.at[1])
            a.start() if do else a.wait()
            b.start() if do else b.wait()
            return carry
        lax.fori_loop(live_n, slots, one, 0)

    fetch(0, 0, True)
    zero_b[...] = jnp.zeros(zero_b.shape, bf16)
    zero_f[...] = jnp.zeros(zero_f.shape, f32)
    zeros_copy(True)
    end = 0
    places = chunk_places(n)
    for d in range(n):
        at = places[d]
        top = 8 * first_tile(shard, d)
        if d == 0:
            flat[pl.ds(0, rows_c), :] = wbuf[at].astype(f32)
        else:
            shared = min(end - top, rows_c)
            flat[pl.ds(top, shared), :] += wbuf[at, pl.ds(0, shared), :].astype(f32)
            if shared < rows_c:
                flat[pl.ds(top + shared, rows_c - shared), :] = wbuf[at, pl.ds(shared, rows_c - shared), :].astype(f32)
        end = top + rows_c
    for ref, (row, height, width) in zip((w_qkv, w_o, w_1, w_2), MATS):
        blocks = width // LANES
        for j in range(blocks):
            ref[:, j * LANES:(j + 1) * LANES] = flat[pl.ds(row + j, height, stride=blocks), :].astype(bf16)
    for k in range(8):
        for j in range(3):
            vecs[k, j * LANES:(j + 1) * LANES] = flat[VEC_ROW + 3 * k + j, :]
    for j in range(12):
        vecs[8, j * LANES:(j + 1) * LANES] = flat[VEC_ROW + 24 + j, :]
    for ref in (g_qkv, g_o, g_1, g_2t, vsum):
        ref[...] = jnp.zeros(ref.shape, f32)
    for ref in (x_s, g_s):
        ref[...] = jnp.zeros(ref.shape, ref.dtype)

    g1 = vecs[0:1, :D]
    b1 = vecs[1:2, :D]
    g2 = vecs[2:3, :D]
    b2 = vecs[3:4, :D]
    cq = vecs[4:5, :D]
    cv = vecs[5:6, :D]
    co = vecs[6:7, :D]
    c2 = vecs[7:8, :D]

    lane = lax.broadcasted_iota(jnp.int32, (1, LANES), 1)
    low_half = lane < HEAD_DIM

    def colsum(v):
        return jnp.sum(v.reshape(v.shape[0] // 8, 8, v.shape[1]), axis=0)

    def mean(v):
        return jnp.sum(v, axis=-1, keepdims=True) * (1.0 / D)

    def body(step, carry):
        slot = lax.rem(step, 2)
        fetch(step, slot, False)

        @pl.when(step + 1 < steps)
        def _():
            fetch(step + 1, 1 - slot, True)

        for i in range(G):
            live = (step * G + i < items).astype(bf16)
            x_s[pl.ds(i * TP, TOK), :] = xin[slot, i].astype(f32)
            g_s[pl.ds(i * TP, TOK), :] = gin[slot, i] * live
        for r in range(0, ROWS, CH):
            rs = pl.ds(r, CH)
            v = x_s[rs, :]
            c = v - mean(v)
            inv = lax.rsqrt(mean(c * c) + norm_eps)
            nv = c * inv
            n1_s[rs, :] = nv
            r1_s[rs, :] = jnp.broadcast_to(inv, (CH, LANES))
            a1_s[rs, :] = (nv * g1 + b1).astype(bf16)
        a1 = a1_s[...]
        for k, bias in ((0, cq), (1, None), (2, cv)):
            cols = slice(k * D, (k + 1) * D)
            t = dot(a1, w_qkv[:, cols])
            qkv_s[:, cols] = (t if bias is None else t + bias).astype(bf16)
        key_live = lax.broadcasted_iota(jnp.int32, (1, TP), 1) < TOK
        for i in range(G):
            ir = pl.ds(i * TP, TP)
            for p in range(HEADS // 2):
                cols = slice(p * LANES, (p + 1) * LANES)
                q = qkv_s[ir, cols] * 0.125
                k = qkv_s[ir, slice(D + p * LANES, D + (p + 1) * LANES)]
                v = qkv_s[ir, slice(2 * D + p * LANES, 2 * D + (p + 1) * LANES)]
                zero = jnp.zeros_like(q)
                qm = jnp.concatenate([jnp.where(low_half, q, zero), jnp.where(low_half, zero, q)], axis=0)
                s = dot(qm, k, 1, 1)
                s = jnp.where(key_live, s, -1e30)
                e = jnp.exp(s - jnp.max(s, axis=-1, keepdims=True))
                pr = e / jnp.sum(e, axis=-1, keepdims=True)
                prob_s[i * 3 + p] = pr
                o2 = dot(pr.astype(bf16), v)
                o_s[ir, cols] = jnp.where(low_half, o2[:TP], o2[TP:]).astype(bf16)
        m_s[...] = dot(o_s[...], w_o[...])
        for r in range(0, ROWS, CH):
            rs = pl.ds(r, CH)
            v = x_s[rs, :] + m_s[rs, :] + co
            m_s[rs, :] = v
            c = v - mean(v)
            inv = lax.rsqrt(mean(c * c) + norm_eps)
            nv = c * inv
            n2_s[rs, :] = nv
            r2_s[rs, :] = jnp.broadcast_to(inv, (CH, LANES))
            a2_s[rs, :] = (nv * g2 + b2).astype(bf16)
        a2 = a2_s[...]
        gl = g_s[...]
        for j in range(FF // FFC):
            cols = slice(j * FFC, (j + 1) * FFC)
            b = j % 2
            u_s[b] = dot(a2, w_1[:, cols])
            da_s[b] = dot(gl, w_2[cols, :], 1, 1)
            c1 = vecs[8:9, cols]
            tot = None
            for r in range(0, ROWS, CH):
                rs = pl.ds(r, CH)
                u = u_s[b, rs, :] + c1
                phi = 0.5 + 0.5 * lax.erf(u * 0.7071067811865476)
                dens = jnp.exp(u * u * -0.5) * 0.3989422804014327
                act_s[b, rs, :] = (u * phi).astype(bf16)
                du = (da_s[b, rs, :] * (phi + u * dens)).astype(bf16)
                du_s[b, rs, :] = du
                part = colsum(du.astype(f32))
                tot = part if tot is None else tot + part
            vsum[8, :, cols] += tot
            act = act_s[b]
            du = du_s[b]
            if j == 0:
                acc_s[...] = dot(act, w_2[cols, :])
                dm_s[...] = dot(du, w_1[:, cols], 1, 1)
            else:
                acc_s[...] += dot(act, w_2[cols, :])
                dm_s[...] += dot(du, w_1[:, cols], 1, 1)
            g_1[:, cols] += dot(a2, du, 0, 0)
            g_2t[:, cols] += dot(gl, act, 0, 0)
        tg2 = tb2 = tco = tc2 = None
        for r in range(0, ROWS, CH):
            rs = pl.ds(r, CH)
            gw = g_s[rs, :].astype(f32)
            acc_s[rs, :] = m_s[rs, :] + acc_s[rs, :] + c2
            e2 = dm_s[rs, :]
            nv = n2_s[rs, :]
            en = e2 * nv
            eg = e2 * g2
            inv = r2_s[rs, :]
            inv = jnp.concatenate([inv, inv, inv], axis=1)
            dm = gw + inv * (eg - mean(eg) - nv * mean(en * g2))
            dm_s[rs, :] = dm
            db = dm.astype(bf16)
            db_s[rs, :] = db
            sums = (colsum(en), colsum(e2), colsum(db.astype(f32)), colsum(gw))
            if tg2 is None:
                tg2, tb2, tco, tc2 = sums
            else:
                tg2, tb2, tco, tc2 = tg2 + sums[0], tb2 + sums[1], tco + sums[2], tc2 + sums[3]
        vsum[2, :, :D] += tg2
        vsum[3, :, :D] += tb2
        vsum[6, :, :D] += tco
        vsum[7, :, :D] += tc2

        @pl.when(step >= 2)
        def _():
            flush(step - 2, slot, False)

        for i in range(G):
            oout[slot, i] = acc_s[pl.ds(i * TP, TOK), :].astype(bf16)
        db = db_s[...]
        g_o[...] += dot(o_s[...], db, 0, 0)
        do_s[...] = dot(db, w_o[...], 1, 1).astype(bf16)
        for i in range(G):
            ir = pl.ds(i * TP, TP)
            for p in range(HEADS // 2):
                cols = slice(p * LANES, (p + 1) * LANES)
                q = qkv_s[ir, cols] * 0.125
                k = qkv_s[ir, slice(D + p * LANES, D + (p + 1) * LANES)]
                v = qkv_s[ir, slice(2 * D + p * LANES, 2 * D + (p + 1) * LANES)]
                do = do_s[ir, cols]
                zero = jnp.zeros_like(q)
                qm = jnp.concatenate([jnp.where(low_half, q, zero), jnp.where(low_half, zero, q)], axis=0)
                dom = jnp.concatenate([jnp.where(low_half, do, zero), jnp.where(low_half, zero, do)], axis=0)
                pr = prob_s[i * 3 + p]
                dp = dot(dom, v, 1, 1)
                delta = jnp.sum(pr * dp, axis=-1, keepdims=True)
                ds = (pr * (dp - delta)).astype(bf16)
                dv = dot(pr.astype(bf16), dom, 0, 0)
                dk = dot(ds, qm, 0, 0)
                dq2 = dot(ds, k * 0.125)
                dq = jnp.where(low_half, dq2[:TP], dq2[TP:])
                dqkv_s[ir, cols] = dq.astype(bf16)
                dqkv_s[ir, slice(D + p * LANES, D + (p + 1) * LANES)] = dk.astype(bf16)
                dqkv_s[ir, slice(2 * D + p * LANES, 2 * D + (p + 1) * LANES)] = dv.astype(bf16)
        dqkv = dqkv_s[...]
        acc_s[...] = dot(dqkv, w_qkv[...], 1, 1)
        g_qkv[...] += dot(a1_s[...], dqkv, 0, 0)
        tg1 = tb1 = tcq = tcv = None
        for r in range(0, ROWS, CH):
            rs = pl.ds(r, CH)
            e1 = acc_s[rs, :]
            nv = n1_s[rs, :]
            en = e1 * nv
            eg = e1 * g1
            inv = r1_s[rs, :]
            inv = jnp.concatenate([inv, inv, inv], axis=1)
            dm_s[rs, :] += inv * (eg - mean(eg) - nv * mean(en * g1))
            sums = (colsum(en), colsum(e1), colsum(dqkv_s[rs, :D].astype(f32)), colsum(dqkv_s[rs, 2 * D:].astype(f32)))
            if tg1 is None:
                tg1, tb1, tcq, tcv = sums
            else:
                tg1, tb1, tcq, tcv = tg1 + sums[0], tb1 + sums[1], tcq + sums[2], tcv + sums[3]
        vsum[0, :, :D] += tg1
        vsum[1, :, :D] += tb1
        vsum[4, :, :D] += tcq
        vsum[5, :, :D] += tcv
        for i in range(G):
            gout[slot, i] = dm_s[pl.ds(i * TP, TOK), :]
        flush(step, slot, True)
        return carry

    lax.fori_loop(0, steps, body, 0)

    for ref, (row, height, width) in zip((g_qkv, g_o, g_1), MATS):
        blocks = width // LANES
        for j in range(blocks):
            flat[pl.ds(row + j, height, stride=blocks), :] = ref[:, j * LANES:(j + 1) * LANES]
    row = MATS[3][0]
    for c in range(FF // LANES):
        t = g_2t[:, c * LANES:(c + 1) * LANES].T
        for j in range(3):
            flat[pl.ds(row + 3 * LANES * c + j, LANES, stride=3), :] = t[:, j * LANES:(j + 1) * LANES]
    for k in range(9):
        t = jnp.sum(vsum[k], axis=0, keepdims=True)
        for j in range(12 if k == 8 else 3):
            flat[pl.ds(VEC_ROW + 3 * k + j, 1), :] = t[:, j * LANES:(j + 1) * LANES]
    flat[pl.ds(FLAT_ROWS, flat.shape[0] - FLAT_ROWS), :] = jnp.zeros((flat.shape[0] - FLAT_ROWS, LANES), f32)
    for d in range(n):
        gbuf[places[d]] = flat[pl.ds(8 * first_tile(shard, d), rows_c), :].astype(bf16)

    @pl.when(steps >= 2)
    def _():
        flush(steps - 2, lax.rem(steps, 2), False)
    flush(steps - 1, lax.rem(steps + 1, 2), False)
    zeros_copy(False)


def flat_height(n, shard):
    return 8 * first_tile(shard, n - 1) + chunk_rows(shard)


def block_call(n, shard, cap, ends, other, images, cot, p_images, p_cot, wbuf):
    slots = images.shape[0]
    anyspace = pl.BlockSpec(memory_space=pl.ANY)
    vm = pl.BlockSpec(memory_space=pltpu.VMEM)
    rows_c = chunk_rows(shard)
    scratch = [
        pltpu.VMEM((flat_height(n, shard), LANES), f32),
        pltpu.VMEM((D, 3 * D), bf16), pltpu.VMEM((D, D), bf16), pltpu.VMEM((D, FF), bf16), pltpu.VMEM((FF, D), bf16),
        pltpu.VMEM((16, FF), f32),
        pltpu.VMEM((D, 3 * D), f32), pltpu.VMEM((D, D), f32), pltpu.VMEM((D, FF), f32), pltpu.VMEM((D, FF), f32),
        pltpu.VMEM((9, 8, FF), f32),
        pltpu.VMEM((2, G, TOK, D), bf16), pltpu.VMEM((2, G, TOK, D), bf16),
        pltpu.VMEM((2, G, TOK, D), bf16), pltpu.VMEM((2, G, TOK, D), f32),
        pltpu.VMEM((ROWS, D), f32),
        pltpu.VMEM((ROWS, D), f32), pltpu.VMEM((ROWS, LANES), f32), pltpu.VMEM((ROWS, D), bf16),
        pltpu.VMEM((ROWS, 3 * D), bf16),
        pltpu.VMEM((G * 3, 2 * TP, TP), f32),
        pltpu.VMEM((ROWS, D), bf16),
        pltpu.VMEM((ROWS, D), f32),
        pltpu.VMEM((ROWS, D), f32), pltpu.VMEM((ROWS, LANES), f32), pltpu.VMEM((ROWS, D), bf16),
        pltpu.VMEM((ROWS, D), bf16),
        pltpu.VMEM((2, ROWS, FFC), f32), pltpu.VMEM((2, ROWS, FFC), bf16), pltpu.VMEM((2, ROWS, FFC), bf16),
        pltpu.VMEM((ROWS, D), f32),
        pltpu.VMEM((2, ROWS, FFC), f32),
        pltpu.VMEM((ROWS, D), f32), pltpu.VMEM((ROWS, D), bf16), pltpu.VMEM((ROWS, D), bf16),
        pltpu.VMEM((ROWS, 3 * D), bf16),
        pltpu.VMEM((TOK, D), bf16), pltpu.VMEM((TOK, D), f32),
        pltpu.SemaphoreType.DMA((2, G, 2)), pltpu.SemaphoreType.DMA((2, G, 2)), pltpu.SemaphoreType.DMA((2,)),
    ]
    return pl.pallas_call(
        functools.partial(compute_kernel, n, shard, cap, slots),
        name="block",
        out_shape=(
            jax.ShapeDtypeStruct(images.shape, bf16),
            jax.ShapeDtypeStruct(images.shape, f32),
            jax.ShapeDtypeStruct((cap,) + images.shape[1:], bf16),
            jax.ShapeDtypeStruct((cap,) + images.shape[1:], f32),
            jax.ShapeDtypeStruct((n, rows_c, LANES), bf16),
        ),
        in_specs=[pl.BlockSpec(memory_space=pltpu.SMEM), pl.BlockSpec(memory_space=pltpu.SMEM), anyspace, anyspace, anyspace, anyspace, vm],
        out_specs=(anyspace, anyspace, anyspace, anyspace, vm),
        scratch_shapes=scratch,
        compiler_params=pltpu.CompilerParams(vmem_limit_bytes=VMEM_LIMIT),
    )(ends, other, images, cot, p_images, p_cot, wbuf)


def chip_axes(n):
    chips = n // 2
    if chips % 16 == 0:
        rest = chips // 4
        side = 2 if rest == 4 else 4
        return (4, rest // side, side)
    return (chips, 1, 1)


class Place:
    def __init__(self, n):
        self.size = chip_axes(n)
        self.stride = (self.size[1] * self.size[2] * 2, self.size[2] * 2, 2)
        self.me = lax.axis_index("dp")
        self.core = lax.rem(self.me, 2)
        self.at = [lax.rem(self.me // self.stride[k], self.size[k]) for k in range(3)]

    def peer(self, axis, hop):
        to = lax.rem(self.at[axis] + hop, self.size[axis])
        return self.me + (to - self.at[axis]) * self.stride[axis]

    def partner(self):
        return self.me + 1 - 2 * self.core

    def slot(self, core, a, b, c):
        return ((core * self.size[1] + b) * self.size[2] + c) * self.size[0] + a

    def everyone(self):
        return [self.peer(k, h) for k in range(3) for h in range(1, self.size[k])] + [self.partner()]


def chunk_order(n):
    A, B, C = chip_axes(n)
    return [((a * B + b) * C + c) * 2 + core for core in range(2) for b in range(B) for c in range(C) for a in range(A)]


def chunk_places(n):
    order = chunk_order(n)
    return [order.index(d) for d in range(n)]


def greet(place):
    barrier = pltpu.get_barrier_semaphore()
    everyone = place.everyone()
    for other in everyone:
        pl.semaphore_signal(barrier, inc=1, device_id=(other,), device_id_type=pl.DeviceIdType.MESH)
    pl.semaphore_wait(barrier, len(everyone))


class Sender:
    def __init__(self, send_sem, recv_sem):
        self.send_sem, self.recv_sem, self.count, self.all = send_sem, recv_sem, 0, []

    def go(self, src, dst, device):
        copy = pltpu.make_async_remote_copy(
            src_ref=src, dst_ref=dst, send_sem=self.send_sem.at[self.count], recv_sem=self.recv_sem.at[self.count],
            device_id=(device,), device_id_type=pl.DeviceIdType.MESH)
        copy.start()
        self.count += 1
        self.all.append(copy)
        return copy


def row_parts(rows, parts):
    tiles = rows // 16
    cuts = [tiles * k // parts * 16 for k in range(parts + 1)]
    return [(cuts[k], cuts[k + 1] - cuts[k]) for k in range(parts)]


PARTS = 4


def gather_kernel(n, cap, chunk, count, images, cot, wbuf, other, images_r, cot_r, p_images, p_cot,
                  xin, wide, relay, send_sem, recv_sem, in_sem, out_sem):
    place = Place(n)
    A, B, C = place.size
    a, b, c = place.at
    core = place.core
    loads = [pltpu.make_async_copy(src, xin.at[k], in_sem.at[k]) for k, src in enumerate((images, cot))]
    for copy in loads:
        copy.start()
    mine = place.slot(core, a, b, c)
    wbuf[mine] = chunk[...]
    greet(place)
    sender = Sender(send_sem, recv_sem)
    parts = row_parts(chunk.shape[0], PARTS)

    def run(start, length, part):
        return wbuf.at[pl.ds(start, length), pl.ds(part[0], part[1]), :]

    def spread(axis, runs, part):
        return [sender.go(run(s, l, part), run(s, l, part), place.peer(axis, hop))
                for hop in range(1, place.size[axis]) for s, l in runs]

    def pass_on(runs, part):
        return [sender.go(run(s, l, part), run(s, l, part), place.partner()) for s, l in runs]

    tell = sender.go(count, other, place.partner())
    one = [spread(0, [(mine, 1)], part) for part in parts]
    slots = images.shape[1]
    toks = images.shape[0]

    def relayout(k):
        loads[k].wait()
        for t in range(0, toks, 50):
            m = min(50, toks - t)
            v = xin[k, pl.ds(t, m)].reshape(m * slots, D).astype(f32)
            for j in range(D // LANES):
                wide[k, j, pl.ds(t * slots, m * slots), :] = v[:, j * LANES:(j + 1) * LANES]

        def one_slot(s, carry):
            for j in range(D // LANES):
                relay[k, s, :, j * LANES:(j + 1) * LANES] = wide[k, j, pl.ds(s, toks, stride=slots), :].astype(bf16)
            return carry
        lax.fori_loop(0, slots, one_slot, 0)

    relayout(0)
    pair = [sender.go(relay.at[0, pl.ds(0, cap)], p_images, place.partner())]
    stores = [pltpu.make_async_copy(relay.at[0], images_r, out_sem.at[0])]
    stores[0].start()
    forwards = []
    two = []
    for k, part in enumerate(parts):
        for copy in one[k]:
            copy.wait_recv()
        runs = [(place.slot(core, 0, b, c), A)]
        two.append(spread(2 if k % 2 == 0 else 1, runs, part))
        forwards += pass_on(runs, part)
    relayout(1)
    pair.append(sender.go(relay.at[1, pl.ds(0, cap)], p_cot, place.partner()))
    stores.append(pltpu.make_async_copy(relay.at[1], cot_r, out_sem.at[1]))
    stores[1].start()
    three = []
    for k, part in enumerate(parts):
        for copy in two[k]:
            copy.wait_recv()
        if k % 2 == 0:
            runs = [(place.slot(core, 0, b, 0), C * A)]
            others = [(place.slot(core, 0, b, lax.rem(c + h, C)), A) for h in range(1, C)]
        else:
            runs = [(place.slot(core, 0, y, c), A) for y in range(B)]
            others = [(place.slot(core, 0, lax.rem(b + h, B), c), A) for h in range(1, B)]
        three.append(spread(1 if k % 2 == 0 else 2, runs, part))
        forwards += pass_on(others, part)
    for k, part in enumerate(parts):
        for copy in three[k]:
            copy.wait_recv()
        if k % 2 == 0:
            others = [(place.slot(core, 0, lax.rem(b + h, B), 0), C * A) for h in range(1, B)]
        else:
            others = [(place.slot(core, 0, y, lax.rem(c + h, C)), A) for h in range(1, C) for y in range(B)]
        forwards += pass_on(others, part)
    for copy in forwards + pair + [tell]:
        copy.wait_recv()
    for copy in sender.all:
        copy.wait_send()
    for copy in stores:
        copy.wait()


def gather_call(n, cap, chunk, count, images, cot):
    toks, slots, _ = images.shape
    anyspace = pl.BlockSpec(memory_space=pl.ANY)
    vm = pl.BlockSpec(memory_space=pltpu.VMEM)
    sems = 160
    return pl.pallas_call(
        functools.partial(gather_kernel, n, cap),
        name="gather",
        out_shape=(
            jax.ShapeDtypeStruct((n,) + chunk.shape, bf16), jax.ShapeDtypeStruct(count.shape, jnp.int32),
            jax.ShapeDtypeStruct((slots, toks, D), bf16), jax.ShapeDtypeStruct((slots, toks, D), bf16),
            jax.ShapeDtypeStruct((cap, toks, D), bf16), jax.ShapeDtypeStruct((cap, toks, D), bf16),
        ),
        in_specs=[vm, vm, anyspace, anyspace],
        out_specs=(vm, vm, anyspace, anyspace, anyspace, anyspace),
        scratch_shapes=[
            pltpu.VMEM((2, toks, slots, D), bf16), pltpu.VMEM((2, D // LANES, toks * slots, LANES), f32), pltpu.VMEM((2, slots, toks, D), bf16),
            pltpu.SemaphoreType.DMA((sems,)), pltpu.SemaphoreType.DMA((sems,)),
            pltpu.SemaphoreType.DMA((2,)), pltpu.SemaphoreType.DMA((2,)),
        ],
        compiler_params=pltpu.CompilerParams(collective_id=0, has_side_effects=True, vmem_limit_bytes=VMEM_LIMIT),
    )(chunk, count, images, cot)


def scatter_kernel(n, gbuf, p_out, p_grad, total, r_out, r_grad, half, got0, got1, got2, got3, send_sem, recv_sem):
    place = Place(n)
    A, B, C = place.size
    a, b, c = place.at
    core = place.core
    greet(place)
    sender = Sender(send_sem, recv_sem)
    parts = row_parts(gbuf.shape[1], PARTS)
    chips = n // 2
    zero = [sender.go(gbuf.at[pl.ds((1 - core) * chips, chips), pl.ds(*part), :], got0.at[:, pl.ds(*part), :], place.partner())
            for part in parts]
    back = [sender.go(p_out, r_out, place.partner()), sender.go(p_grad, r_grad, place.partner())]

    def rows(ref, start, length, part):
        return ref.at[pl.ds(start, length), pl.ds(*part), :]

    def slot(bb, cc):
        return (bb * C + cc) * A

    one, two, three = [], [], []
    for k, part in enumerate(parts):
        zero[k].wait_recv()
        pr = pl.ds(*part)

        def add(i, carry):
            half[i, pr, :] = (gbuf[core * chips + i, pr, :].astype(f32) + got0[i, pr, :].astype(f32)).astype(bf16)
            return carry
        lax.fori_loop(0, chips, add, 0)
        sent = []
        if k % 2 == 0:
            for h in range(1, B):
                to = lax.rem(b + h, B)
                sent.append(sender.go(rows(half, slot(to, 0), C * A, part), rows(got1, (h - 1) * C * A, C * A, part), place.peer(1, h)))
        else:
            for h in range(1, C):
                to = lax.rem(c + h, C)
                for y in range(B):
                    sent.append(sender.go(rows(half, slot(y, to), A, part), rows(got1, ((h - 1) * B + y) * A, A, part), place.peer(2, h)))
        one.append(sent)
    for k, part in enumerate(parts):
        for copy in one[k]:
            copy.wait_recv()
        pr = pl.ds(*part)
        sent = []
        if k % 2 == 0:
            def add(i, carry):
                v = half[slot(b, 0) + i, pr, :].astype(f32)
                for h in range(1, B):
                    v = v + got1[(h - 1) * C * A + i, pr, :].astype(f32)
                half[slot(b, 0) + i, pr, :] = v.astype(bf16)
                return carry
            lax.fori_loop(0, C * A, add, 0)
            for h in range(1, C):
                to = lax.rem(c + h, C)
                sent.append(sender.go(rows(half, slot(b, to), A, part), rows(got2, (h - 1) * A, A, part), place.peer(2, h)))
        else:
            def add(i, carry):
                y = i // A
                z = lax.rem(i, A)
                v = half[slot(y, c) + z, pr, :].astype(f32)
                for h in range(1, C):
                    v = v + got1[((h - 1) * B + y) * A + z, pr, :].astype(f32)
                half[slot(y, c) + z, pr, :] = v.astype(bf16)
                return carry
            lax.fori_loop(0, B * A, add, 0)
            for h in range(1, B):
                to = lax.rem(b + h, B)
                sent.append(sender.go(rows(half, slot(to, c), A, part), rows(got2, (h - 1) * A, A, part), place.peer(1, h)))
        two.append(sent)
    for k, part in enumerate(parts):
        for copy in two[k]:
            copy.wait_recv()
        pr = pl.ds(*part)
        last = (C if k % 2 == 0 else B) - 1

        def add(i, carry):
            v = half[slot(b, c) + i, pr, :].astype(f32)
            for h in range(last):
                v = v + got2[h * A + i, pr, :].astype(f32)
            half[slot(b, c) + i, pr, :] = v.astype(bf16)
            return carry
        lax.fori_loop(0, A, add, 0)
        sent = []
        for h in range(1, A):
            to = lax.rem(a + h, A)
            sent.append(sender.go(rows(half, slot(b, c) + to, 1, part), rows(got3, h - 1, 1, part), place.peer(0, h)))
        three.append(sent)
    for k, part in enumerate(parts):
        for copy in three[k]:
            copy.wait_recv()
        pr = pl.ds(*part)
        v = half[slot(b, c) + a, pr, :].astype(f32)
        for h in range(A - 1):
            v = v + got3[h, pr, :].astype(f32)
        total[pr, :] = v
    for copy in back:
        copy.wait_recv()
    for copy in sender.all:
        copy.wait_send()


def scatter_call(n, gbuf, p_out, p_grad):
    A, B, C = chip_axes(n)
    rows_c = gbuf.shape[1]
    anyspace = pl.BlockSpec(memory_space=pl.ANY)
    vm = pl.BlockSpec(memory_space=pltpu.VMEM)
    count = 160
    big = max((B - 1) * C * A, (C - 1) * B * A)
    return pl.pallas_call(
        functools.partial(scatter_kernel, n),
        name="scatter",
        out_shape=(jax.ShapeDtypeStruct((rows_c, LANES), f32), jax.ShapeDtypeStruct(p_out.shape, p_out.dtype),
                   jax.ShapeDtypeStruct(p_grad.shape, p_grad.dtype)),
        in_specs=[vm, anyspace, anyspace],
        out_specs=(vm, anyspace, anyspace),
        scratch_shapes=[
            pltpu.VMEM((n // 2, rows_c, LANES), bf16), pltpu.VMEM((n // 2, rows_c, LANES), bf16),
            pltpu.VMEM((big, rows_c, LANES), bf16), pltpu.VMEM((max(B, C) * A, rows_c, LANES), bf16),
            pltpu.VMEM((A, rows_c, LANES), bf16),
            pltpu.SemaphoreType.DMA((count,)), pltpu.SemaphoreType.DMA((count,)),
        ],
        compiler_params=pltpu.CompilerParams(collective_id=1, has_side_effects=True, vmem_limit_bytes=VMEM_LIMIT),
    )(gbuf, p_out, p_grad)


def pack_shard(n, shard, values):
    me = lax.axis_index("dp")
    offset = lax.rem(shard * me, TILE)
    padded = lax.dynamic_update_slice_in_dim(jnp.zeros((chunk_rows(shard) * LANES,), values.dtype), values, offset, 0)
    return padded.reshape(chunk_rows(shard), LANES)


def unpack_shard(n, shard, chunk):
    me = lax.axis_index("dp")
    offset = lax.rem(shard * me, TILE)
    return lax.dynamic_slice_in_dim(chunk.reshape(-1), offset, shard, 0)


def body(n, images, cotangent, master, moment_one, moment_two, batch_ends):
    shard = master.shape[0]
    cap = CAP
    slots = images.shape[0]
    chunk = pack_shard(n, shard, master.astype(bf16))
    count = jnp.broadcast_to(batch_ends[0, MB - 1], (8, LANES))
    wbuf, other, images_r, cot_r, p_images, p_cot = gather_call(
        n, cap, chunk, count, images.transpose(1, 0, 2), cotangent.transpose(1, 0, 2))
    block_out, input_grad, p_out, p_grad, gbuf = block_call(
        n, shard, cap, batch_ends, other, images_r, cot_r, p_images, p_cot, wbuf)
    part, r_out, r_grad = scatter_call(n, gbuf, p_out, p_grad)
    given = jnp.clip((batch_ends[0, MB - 1] - other[0, 0]) // 2, 0, cap)
    use = (jnp.arange(slots) < given)[:, None, None]
    pad = ((0, slots - cap), (0, 0), (0, 0))
    block_out = jnp.where(use, jnp.pad(r_out, pad), block_out)
    input_grad = jnp.where(use, jnp.pad(r_grad, pad), input_grad)
    weight_grad = unpack_shard(n, shard, part)
    first_moment = beta_one * moment_one + (1.0 - beta_one) * weight_grad
    second_moment = beta_two * moment_two + (1.0 - beta_two) * weight_grad * weight_grad
    corrected_one = first_moment / (1.0 - beta_one**STEP)
    corrected_two = second_moment / (1.0 - beta_two**STEP)
    update = -learn_rate * (corrected_one / (jnp.sqrt(corrected_two) + adam_eps) + decay_rate * master)
    return (block_out, input_grad, weight_grad, first_moment, second_moment, update)


def solution(mesh):
    n = mesh.shape["dp"]
    return jax.shard_map(
        functools.partial(body, n),
        mesh=mesh,
        in_specs=(P("dp", None, None), P("dp", None, None), P("dp"), P("dp"), P("dp"), P("dp", None)),
        out_specs=(P("dp", None, None), P("dp", None, None), P("dp"), P("dp"), P("dp"), P("dp")),
        check_vma=False,
    )
```

```python
import jax, jax.numpy as jnp, functools
from jax import lax
from jax.experimental import pallas as pl
from jax.experimental.pallas import tpu as pltpu
from jax.sharding import PartitionSpec as P

D = 384
FF = 1536
HEADS = 6
HEAD_DIM = 64
TOK = 197
TP = 208
G = 2
ROWS = G * TP
MB = 3
STEP = 10
CH = 32
FFC = 1536

beta_one = 0.9
beta_two = 0.999
learn_rate = 0.01
decay_rate = 0.05
adam_eps = 1e-08
norm_eps = 1e-06
f32 = jnp.float32
bf16 = jnp.bfloat16

LANES = 128
TILE = 8 * LANES
MATS = ((0, D, 3 * D), (3456, D, D), (4608, D, FF), (9216, FF, D))
VEC_ROW = 13824
FLAT_ROWS = 13860
VMEM_LIMIT = 60 * 2**20
CAP = 6


def dot(a, b, ca=1, cb=0):
    return lax.dot_general(a, b, (((ca,), (cb,)), ((), ())), preferred_element_type=f32)


def chunk_rows(shard):
    return ((shard + TILE - 1 + LANES - 1) // LANES + 15) // 16 * 16


def first_tile(shard, d):
    return (shard * d) // TILE


def compute_kernel(n, shard, cap, slots, ends, other, images, cot, p_images, p_cot, wbuf,
                   block_out, input_grad, p_out, p_grad, gbuf,
                   flat, w_qkv, w_o, w_1, w_2, vecs, g_qkv, g_o, g_1, g_2t, vsum,
                   xin, gin, oout, gout, x_s, n1_s, r1_s, a1_s, qkv_s, prob_s, ve_s, inv_s, of_s, o_s, m_s, n2_s, r2_s, a2_s,
                   g_s, u_s, act_s, du_s, acc_s, da_s, dm_s, db_s, do_s, dqkv_s, zero_b, zero_f,
                   in_sem, out_sem, zero_sem):
    rows_c = wbuf.shape[1]
    live_n = ends[0, MB - 1]
    diff = live_n - other[0, MB - 1]
    own_first = jnp.clip(diff // 2, 0, cap)
    own_n = live_n - own_first
    part_n = jnp.clip((0 - diff) // 2, 0, cap)
    items = own_n + part_n
    steps = (items + G - 1) // G

    def fetch(step, slot, do):
        for i in range(G):
            item = jnp.minimum(step * G + i, items - 1)
            is_own = item < own_n

            @pl.when(is_own)
            def _():
                s = own_first + item
                for k, (src, dst) in enumerate(((images, xin), (cot, gin))):
                    c = pltpu.make_async_copy(src.at[s], dst.at[slot, i], in_sem.at[slot, i, k])
                    c.start() if do else c.wait()

            @pl.when(jnp.logical_not(is_own))
            def _():
                s = item - own_n
                for k, (src, dst) in enumerate(((p_images, xin), (p_cot, gin))):
                    c = pltpu.make_async_copy(src.at[s], dst.at[slot, i], in_sem.at[slot, i, k])
                    c.start() if do else c.wait()

    def flush(step, slot, do):
        for i in range(G):
            item = step * G + i
            is_own = item < own_n

            @pl.when(is_own)
            def _():
                s = own_first + item
                for k, (dst, src) in enumerate(((block_out, oout), (input_grad, gout))):
                    c = pltpu.make_async_copy(src.at[slot, i], dst.at[s], out_sem.at[slot, i, k])
                    c.start() if do else c.wait()

            @pl.when(jnp.logical_and(jnp.logical_not(is_own), item < items))
            def _():
                s = item - own_n
                for k, (dst, src) in enumerate(((p_out, oout), (p_grad, gout))):
                    c = pltpu.make_async_copy(src.at[slot, i], dst.at[s], out_sem.at[slot, i, k])
                    c.start() if do else c.wait()

    def zeros_copy(do):
        def one(s, carry):
            a = pltpu.make_async_copy(zero_b, block_out.at[s], zero_sem.at[0])
            b = pltpu.make_async_copy(zero_f, input_grad.at[s], zero_sem.at[1])
            a.start() if do else a.wait()
            b.start() if do else b.wait()
            return carry
        lax.fori_loop(live_n, slots, one, 0)

    fetch(0, 0, True)
    zero_b[...] = jnp.zeros(zero_b.shape, bf16)
    zero_f[...] = jnp.zeros(zero_f.shape, f32)
    zeros_copy(True)
    end = 0
    places = chunk_places(n)
    for d in range(n):
        at = places[d]
        top = 8 * first_tile(shard, d)
        if d == 0:
            flat[pl.ds(0, rows_c), :] = wbuf[at].astype(f32)
        else:
            shared = min(end - top, rows_c)
            flat[pl.ds(top, shared), :] += wbuf[at, pl.ds(0, shared), :].astype(f32)
            if shared < rows_c:
                flat[pl.ds(top + shared, rows_c - shared), :] = wbuf[at, pl.ds(shared, rows_c - shared), :].astype(f32)
        end = top + rows_c
    for ref, (row, height, width) in zip((w_qkv, w_o, w_1, w_2), MATS):
        blocks = width // LANES
        for j in range(blocks):
            ref[:, j * LANES:(j + 1) * LANES] = flat[pl.ds(row + j, height, stride=blocks), :].astype(bf16)
    for k in range(8):
        for j in range(3):
            vecs[k, j * LANES:(j + 1) * LANES] = flat[VEC_ROW + 3 * k + j, :]
    for j in range(12):
        vecs[8, j * LANES:(j + 1) * LANES] = flat[VEC_ROW + 24 + j, :]
    for ref in (g_qkv, g_o, g_1, g_2t, vsum):
        ref[...] = jnp.zeros(ref.shape, f32)
    g_s[...] = jnp.zeros(g_s.shape, bf16)
    real = lax.broadcasted_iota(jnp.int32, (TP, LANES), 0) < TOK
    ve_s[:, :, LANES:] = jnp.broadcast_to(real.astype(f32).astype(bf16), (G * 3, TP, LANES))

    g1 = vecs[0:1, :D]
    b1 = vecs[1:2, :D]
    g2 = vecs[2:3, :D]
    b2 = vecs[3:4, :D]
    cq = vecs[4:5, :D]
    cv = vecs[5:6, :D]
    co = vecs[6:7, :D]
    c2 = vecs[7:8, :D]

    bqkv = jnp.concatenate([cq, jnp.zeros_like(cq), cv], axis=1)

    lane = lax.broadcasted_iota(jnp.int32, (1, LANES), 1)
    low_half = lane < HEAD_DIM

    def colsum(v):
        return jnp.sum(v.reshape(v.shape[0] // 8, 8, v.shape[1]), axis=0)

    def mean(v):
        return jnp.sum(v, axis=-1, keepdims=True) * (1.0 / D)

    def body(step, carry):
        slot = lax.rem(step, 2)
        fetch(step, slot, False)

        @pl.when(step + 1 < steps)
        def _():
            fetch(step + 1, 1 - slot, True)

        for i in range(G):
            live = (step * G + i < items).astype(bf16)
            x = xin[slot, i].astype(f32)
            x_s[pl.ds(i * TP, TOK), :] = x
            x_s[pl.ds(i * TP + TOK, TP - TOK), :] = jnp.broadcast_to(x[TOK - 1:], (TP - TOK, D))
            g_s[pl.ds(i * TP, TOK), :] = gin[slot, i] * live
        for r in range(0, ROWS, CH):
            rs = pl.ds(r, CH)
            v = x_s[rs, :]
            c = v - mean(v)
            inv = lax.rsqrt(mean(c * c) + norm_eps)
            nv = c * inv
            n1_s[rs, :] = nv
            r1_s[rs, :] = jnp.broadcast_to(inv, (CH, LANES))
            a1_s[rs, :] = (nv * g1 + b1).astype(bf16)
        a1 = a1_s[...]
        qkv_s[...] = (dot(a1, w_qkv[...]) + bqkv).astype(bf16)
        tail = lax.broadcasted_iota(jnp.int32, (16, 1), 0) < TOK - (TP - 16)
        for i in range(G):
            ir = pl.ds(i * TP, TP)
            for p in range(HEADS // 2):
                at = i * 3 + p
                cols = slice(p * LANES, (p + 1) * LANES)
                vcols = slice(2 * D + p * LANES, 2 * D + (p + 1) * LANES)
                ve_s[at, :TP - 16, :LANES] = qkv_s[pl.ds(i * TP, TP - 16), vcols]
                last = qkv_s[pl.ds((i + 1) * TP - 16, 16), vcols]
                ve_s[at, TP - 16:, :LANES] = jnp.where(tail, last, jnp.zeros_like(last))
                q = qkv_s[ir, cols] * 0.125
                k = qkv_s[ir, slice(D + p * LANES, D + (p + 1) * LANES)]
                zero = jnp.zeros_like(q)
                qm = jnp.concatenate([jnp.where(low_half, q, zero), jnp.where(low_half, zero, q)], axis=0)
                s = dot(qm, k, 1, 1)
                e = jnp.exp(s - jnp.max(s, axis=-1, keepdims=True)).astype(bf16)
                prob_s[at] = e
                oe = dot(e, ve_s[at])
                inv = 1.0 / jnp.where(low_half, oe[:TP, LANES:], oe[TP:, LANES:])
                o = jnp.where(low_half, oe[:TP, :LANES], oe[TP:, :LANES]) * inv
                inv_s[at] = inv
                of_s[at] = o
                o_s[ir, cols] = o.astype(bf16)
        m_s[...] = dot(o_s[...], w_o[...])
        for r in range(0, ROWS, CH):
            rs = pl.ds(r, CH)
            v = x_s[rs, :] + m_s[rs, :] + co
            m_s[rs, :] = v
            c = v - mean(v)
            inv = lax.rsqrt(mean(c * c) + norm_eps)
            nv = c * inv
            n2_s[rs, :] = nv
            r2_s[rs, :] = jnp.broadcast_to(inv, (CH, LANES))
            a2_s[rs, :] = (nv * g2 + b2).astype(bf16)
        a2 = a2_s[...]
        gl = g_s[...]
        for j in range(FF // FFC):
            cols = slice(j * FFC, (j + 1) * FFC)
            b = j
            u_s[b] = dot(a2, w_1[:, cols])
            da_s[b] = dot(gl, w_2[cols, :], 1, 1)
            c1 = vecs[8:9, cols]
            tot = None
            for r in range(0, ROWS, CH):
                rs = pl.ds(r, CH)
                u = u_s[b, rs, :] + c1
                phi = 0.5 + 0.5 * lax.erf(u * 0.7071067811865476)
                dens = jnp.exp(u * u * -0.5) * 0.3989422804014327
                act_s[b, rs, :] = (u * phi).astype(bf16)
                du = (da_s[b, rs, :] * (phi + u * dens)).astype(bf16)
                du_s[b, rs, :] = du
                part = colsum(du.astype(f32))
                tot = part if tot is None else tot + part
            vsum[8, :, cols] += tot
            act = act_s[b]
            du = du_s[b]
            if j == 0:
                acc_s[...] = dot(act, w_2[cols, :])
                dm_s[...] = dot(du, w_1[:, cols], 1, 1)
            else:
                acc_s[...] += dot(act, w_2[cols, :])
                dm_s[...] += dot(du, w_1[:, cols], 1, 1)
        tg2 = tb2 = tco = tc2 = None
        for r in range(0, ROWS, CH):
            rs = pl.ds(r, CH)
            gw = g_s[rs, :].astype(f32)
            acc_s[rs, :] = m_s[rs, :] + acc_s[rs, :] + c2
            e2 = dm_s[rs, :]
            nv = n2_s[rs, :]
            en = e2 * nv
            eg = e2 * g2
            inv = r2_s[rs, :]
            inv = jnp.concatenate([inv, inv, inv], axis=1)
            dm = gw + inv * (eg - mean(eg) - nv * mean(en * g2))
            dm_s[rs, :] = dm
            db = dm.astype(bf16)
            db_s[rs, :] = db
            sums = (colsum(en), colsum(e2), colsum(db.astype(f32)), colsum(gw))
            if tg2 is None:
                tg2, tb2, tco, tc2 = sums
            else:
                tg2, tb2, tco, tc2 = tg2 + sums[0], tb2 + sums[1], tco + sums[2], tc2 + sums[3]
        vsum[2, :, :D] += tg2
        vsum[3, :, :D] += tb2
        vsum[6, :, :D] += tco
        vsum[7, :, :D] += tc2

        @pl.when(step >= 2)
        def _():
            flush(step - 2, slot, False)

        for i in range(G):
            oout[slot, i] = acc_s[pl.ds(i * TP, TOK), :].astype(bf16)
        db = db_s[...]
        g_o[...] += dot(o_s[...], db, 0, 0)
        do_s[...] = dot(db, w_o[...], 1, 1).astype(bf16)
        for i in range(G):
            ir = pl.ds(i * TP, TP)
            for p in range(HEADS // 2):
                at = i * 3 + p
                cols = slice(p * LANES, (p + 1) * LANES)
                q = qkv_s[ir, cols] * 0.125
                k = qkv_s[ir, slice(D + p * LANES, D + (p + 1) * LANES)]
                zero = jnp.zeros_like(q)
                qm = jnp.concatenate([jnp.where(low_half, q, zero), jnp.where(low_half, zero, q)], axis=0)
                do = (do_s[ir, cols].astype(f32) * inv_s[at]).astype(bf16)
                dom0 = jnp.where(low_half, do, zero)
                dom1 = jnp.where(low_half, zero, do)
                dom = jnp.concatenate([dom0, dom1], axis=0)
                t = of_s[at] * do.astype(f32) * -1.0
                hi = t.astype(bf16)
                lo = pltpu.roll(t - hi.astype(f32), HEAD_DIM, 1).astype(bf16)
                x0 = jnp.where(low_half, hi, lo)
                x1 = jnp.where(low_half, lo, hi)
                left = jnp.concatenate([dom, jnp.concatenate([x0, x1], axis=0)], axis=1)
                e = prob_s[at]
                dp = dot(left, ve_s[at], 1, 1)
                fc = slice(at * 256, (at + 1) * 256)
                g_1[:, fc] += dot(a2_s[...], du_s[0, :, fc], 0, 0)
                ds = (e.astype(f32) * dp).astype(bf16)
                dv = dot(dom, e, 0, 0).T
                dk = dot(qm, ds, 0, 0).T
                g_2t[:, fc] += dot(g_s[...], act_s[0, :, fc], 0, 0)
                dq2 = dot(ds, k * 0.125)
                dq = jnp.where(low_half, dq2[:TP], dq2[TP:])
                dqkv_s[ir, cols] = dq.astype(bf16)
                dqkv_s[ir, slice(D + p * LANES, D + (p + 1) * LANES)] = dk.astype(bf16)
                vcols = slice(2 * D + p * LANES, 2 * D + (p + 1) * LANES)
                dqkv_s[pl.ds(i * TP, TP - 16), vcols] = dv[:TP - 16].astype(bf16)
                dqkv_s[pl.ds((i + 1) * TP - 16, 16), vcols] = jnp.where(tail, dv[TP - 16:], 0.0).astype(bf16)
        dqkv = dqkv_s[...]
        acc_s[...] = dot(dqkv, w_qkv[...], 1, 1)
        g_qkv[...] += dot(a1_s[...], dqkv, 0, 0)
        tg1 = tb1 = tcq = tcv = None
        for r in range(0, ROWS, CH):
            rs = pl.ds(r, CH)
            e1 = acc_s[rs, :]
            nv = n1_s[rs, :]
            en = e1 * nv
            eg = e1 * g1
            inv = r1_s[rs, :]
            inv = jnp.concatenate([inv, inv, inv], axis=1)
            dm_s[rs, :] += inv * (eg - mean(eg) - nv * mean(en * g1))
            sums = (colsum(en), colsum(e1), colsum(dqkv_s[rs, :D].astype(f32)), colsum(dqkv_s[rs, 2 * D:].astype(f32)))
            if tg1 is None:
                tg1, tb1, tcq, tcv = sums
            else:
                tg1, tb1, tcq, tcv = tg1 + sums[0], tb1 + sums[1], tcq + sums[2], tcv + sums[3]
        vsum[0, :, :D] += tg1
        vsum[1, :, :D] += tb1
        vsum[4, :, :D] += tcq
        vsum[5, :, :D] += tcv
        for i in range(G):
            gout[slot, i] = dm_s[pl.ds(i * TP, TOK), :]
        flush(step, slot, True)
        return carry

    lax.fori_loop(0, steps, body, 0)

    for ref, (row, height, width) in zip((g_qkv, g_o, g_1), MATS):
        blocks = width // LANES
        for j in range(blocks):
            flat[pl.ds(row + j, height, stride=blocks), :] = ref[:, j * LANES:(j + 1) * LANES]
    row = MATS[3][0]
    for c in range(FF // LANES):
        t = g_2t[:, c * LANES:(c + 1) * LANES].T
        for j in range(3):
            flat[pl.ds(row + 3 * LANES * c + j, LANES, stride=3), :] = t[:, j * LANES:(j + 1) * LANES]
    for k in range(9):
        t = jnp.sum(vsum[k], axis=0, keepdims=True)
        for j in range(12 if k == 8 else 3):
            flat[pl.ds(VEC_ROW + 3 * k + j, 1), :] = t[:, j * LANES:(j + 1) * LANES]
    flat[pl.ds(FLAT_ROWS, flat.shape[0] - FLAT_ROWS), :] = jnp.zeros((flat.shape[0] - FLAT_ROWS, LANES), f32)
    for d in range(n):
        gbuf[places[d]] = flat[pl.ds(8 * first_tile(shard, d), rows_c), :].astype(bf16)

    @pl.when(steps >= 2)
    def _():
        flush(steps - 2, lax.rem(steps, 2), False)
    flush(steps - 1, lax.rem(steps + 1, 2), False)
    zeros_copy(False)


def flat_height(n, shard):
    return 8 * first_tile(shard, n - 1) + chunk_rows(shard)


def block_call(n, shard, cap, ends, other, images, cot, p_images, p_cot, wbuf):
    slots = images.shape[0]
    anyspace = pl.BlockSpec(memory_space=pl.ANY)
    vm = pl.BlockSpec(memory_space=pltpu.VMEM)
    rows_c = chunk_rows(shard)
    scratch = [
        pltpu.VMEM((flat_height(n, shard), LANES), f32),
        pltpu.VMEM((D, 3 * D), bf16), pltpu.VMEM((D, D), bf16), pltpu.VMEM((D, FF), bf16), pltpu.VMEM((FF, D), bf16),
        pltpu.VMEM((16, FF), f32),
        pltpu.VMEM((D, 3 * D), f32), pltpu.VMEM((D, D), f32), pltpu.VMEM((D, FF), f32), pltpu.VMEM((D, FF), f32),
        pltpu.VMEM((9, 8, FF), f32),
        pltpu.VMEM((2, G, TOK, D), bf16), pltpu.VMEM((2, G, TOK, D), bf16),
        pltpu.VMEM((2, G, TOK, D), bf16), pltpu.VMEM((2, G, TOK, D), f32),
        pltpu.VMEM((ROWS, D), f32),
        pltpu.VMEM((ROWS, D), f32), pltpu.VMEM((ROWS, LANES), f32), pltpu.VMEM((ROWS, D), bf16),
        pltpu.VMEM((ROWS, 3 * D), bf16),
        pltpu.VMEM((G * 3, 2 * TP, TP), bf16), pltpu.VMEM((G * 3, TP, 2 * LANES), bf16),
        pltpu.VMEM((G * 3, TP, LANES), f32), pltpu.VMEM((G * 3, TP, LANES), f32),
        pltpu.VMEM((ROWS, D), bf16),
        pltpu.VMEM((ROWS, D), f32),
        pltpu.VMEM((ROWS, D), f32), pltpu.VMEM((ROWS, LANES), f32), pltpu.VMEM((ROWS, D), bf16),
        pltpu.VMEM((ROWS, D), bf16),
        pltpu.VMEM((FF // FFC, ROWS, FFC), f32), pltpu.VMEM((FF // FFC, ROWS, FFC), bf16), pltpu.VMEM((FF // FFC, ROWS, FFC), bf16),
        pltpu.VMEM((ROWS, D), f32),
        pltpu.VMEM((FF // FFC, ROWS, FFC), f32),
        pltpu.VMEM((ROWS, D), f32), pltpu.VMEM((ROWS, D), bf16), pltpu.VMEM((ROWS, D), bf16),
        pltpu.VMEM((ROWS, 3 * D), bf16),
        pltpu.VMEM((TOK, D), bf16), pltpu.VMEM((TOK, D), f32),
        pltpu.SemaphoreType.DMA((2, G, 2)), pltpu.SemaphoreType.DMA((2, G, 2)), pltpu.SemaphoreType.DMA((2,)),
    ]
    return pl.pallas_call(
        functools.partial(compute_kernel, n, shard, cap, slots),
        name="block",
        out_shape=(
            jax.ShapeDtypeStruct(images.shape, bf16),
            jax.ShapeDtypeStruct(images.shape, f32),
            jax.ShapeDtypeStruct((cap,) + images.shape[1:], bf16),
            jax.ShapeDtypeStruct((cap,) + images.shape[1:], f32),
            jax.ShapeDtypeStruct((n, rows_c, LANES), bf16),
        ),
        in_specs=[pl.BlockSpec(memory_space=pltpu.SMEM), pl.BlockSpec(memory_space=pltpu.SMEM), anyspace, anyspace, anyspace, anyspace, vm],
        out_specs=(anyspace, anyspace, anyspace, anyspace, vm),
        scratch_shapes=scratch,
        compiler_params=pltpu.CompilerParams(vmem_limit_bytes=VMEM_LIMIT),
    )(ends, other, images, cot, p_images, p_cot, wbuf)


def chip_axes(n):
    chips = n // 2
    if chips % 16 == 0:
        rest = chips // 4
        side = 2 if rest == 4 else 4
        return (4, rest // side, side)
    return (chips, 1, 1)


class Place:
    def __init__(self, n):
        self.size = chip_axes(n)
        self.stride = (self.size[1] * self.size[2] * 2, self.size[2] * 2, 2)
        self.me = lax.axis_index("dp")
        self.core = lax.rem(self.me, 2)
        self.at = [lax.rem(self.me // self.stride[k], self.size[k]) for k in range(3)]

    def peer(self, axis, hop):
        to = lax.rem(self.at[axis] + hop, self.size[axis])
        return self.me + (to - self.at[axis]) * self.stride[axis]

    def partner(self):
        return self.me + 1 - 2 * self.core

    def slot(self, core, a, b, c):
        return ((core * self.size[1] + b) * self.size[2] + c) * self.size[0] + a

    def everyone(self):
        return [self.peer(k, h) for k in range(3) for h in range(1, self.size[k])] + [self.partner()]


def chunk_places(n):
    A, B, C = chip_axes(n)
    order = [((a * B + b) * C + c) * 2 + core for core in range(2) for b in range(B) for c in range(C) for a in range(A)]
    return [order.index(d) for d in range(n)]


def greet(place):
    barrier = pltpu.get_barrier_semaphore()
    everyone = place.everyone()
    for other in everyone:
        pl.semaphore_signal(barrier, inc=1, device_id=(other,), device_id_type=pl.DeviceIdType.MESH)
    pl.semaphore_wait(barrier, len(everyone))


class Sender:
    def __init__(self, send_sem, recv_sem):
        self.send_sem, self.recv_sem, self.all = send_sem, recv_sem, []

    def go(self, src, dst, device):
        k = len(self.all)
        copy = pltpu.make_async_remote_copy(
            src_ref=src, dst_ref=dst, send_sem=self.send_sem.at[k], recv_sem=self.recv_sem.at[k],
            device_id=(device,), device_id_type=pl.DeviceIdType.MESH)
        copy.start()
        self.all.append([copy, False])
        return copy

    def sent(self, copies):
        for entry in self.all:
            if any(entry[0] is copy for copy in copies) and not entry[1]:
                entry[0].wait_send()
                entry[1] = True

    def finish(self):
        self.sent([entry[0] for entry in self.all])


def arrive(copies):
    for copy in copies:
        copy.wait_recv()


def row_parts(rows, parts):
    tiles = rows // 16
    parts = min(parts, tiles)
    cuts = [tiles * k // parts * 16 for k in range(parts + 1)]
    return [(cuts[k], cuts[k + 1] - cuts[k]) for k in range(parts)]


PARTS = 4
SEMS = 192


def gather_kernel(n, cap, chunk, count, images, cot, wbuf, other, images_r, cot_r, p_images, p_cot,
                  xin, wide, relay, send_sem, recv_sem, in_sem, out_sem):
    place = Place(n)
    A, B, C = place.size
    a, b, c = place.at
    core = place.core
    loads = [pltpu.make_async_copy(src, xin.at[k], in_sem.at[k]) for k, src in enumerate((images, cot))]
    for copy in loads:
        copy.start()
    mine = place.slot(core, a, b, c)
    wbuf[mine] = chunk[...]
    greet(place)
    sender = Sender(send_sem, recv_sem)
    parts = row_parts(chunk.shape[0], PARTS)
    last = len(parts) - 1
    slots = images.shape[1]
    toks = images.shape[0]

    def run(start, length, part):
        return wbuf.at[pl.ds(start, length), pl.ds(part[0], part[1]), :]

    def spread(axis, runs, part):
        return [sender.go(run(s, l, part), run(s, l, part), place.peer(axis, hop))
                for hop in range(1, place.size[axis]) for s, l in runs]

    def pass_on(runs, part):
        return [sender.go(run(s, l, part), run(s, l, part), place.partner()) for s, l in runs]

    def widen(k, t, m):
        v = xin[k, pl.ds(t, m)].reshape(m * slots, D).astype(f32)
        for j in range(D // LANES):
            wide[k, j, pl.ds(t * slots, m * slots), :] = v[:, j * LANES:(j + 1) * LANES]

    def one_slot(k, s, carry):
        for j in range(D // LANES):
            relay[k, s, :, j * LANES:(j + 1) * LANES] = wide[k, j, pl.ds(s, toks, stride=slots), :].astype(bf16)
        return carry

    def chores():
        for k in range(2):
            loads[k].wait()
            for t in range(0, toks, 100):
                widen(k, t, min(100, toks - t))
                yield
            step = -(-slots // 4)
            for s in range(0, slots, step):
                lax.fori_loop(s, min(s + step, slots), functools.partial(one_slot, k), 0)
                yield
            pair.append(sender.go(relay.at[k, pl.ds(0, cap)], (p_images, p_cot)[k], place.partner()))
            stores.append(pltpu.make_async_copy(relay.at[k], (images_r, cot_r)[k], out_sem.at[k]))
            stores[-1].start()
        while True:
            yield

    one, two, three, forwards, stores = {}, {}, {}, [], []
    one[0] = spread(0, [(mine, 1)], parts[0])
    pair = [sender.go(count, other, place.partner())]

    def second(k):
        arrive(one[k])
        runs = [(place.slot(core, 0, b, c), A)]
        two[k] = spread(2 if k % 2 == 0 else 1, runs, parts[k])
        forwards.extend(pass_on(runs, parts[k]))

    def third(k):
        arrive(two[k])
        if k % 2 == 0:
            runs = [(place.slot(core, 0, b, 0), C * A)]
            others = [(place.slot(core, 0, b, lax.rem(c + h, C)), A) for h in range(1, C)]
        else:
            runs = [(place.slot(core, 0, y, c), A) for y in range(B)]
            others = [(place.slot(core, 0, lax.rem(b + h, B), c), A) for h in range(1, B)]
        three[k] = spread(1 if k % 2 == 0 else 2, runs, parts[k])
        forwards.extend(pass_on(others, parts[k]))

    def ending(k):
        arrive(three[k])
        if k % 2 == 0:
            others = [(place.slot(core, 0, lax.rem(b + h, B), 0), C * A) for h in range(1, B)]
        else:
            others = [(place.slot(core, 0, y, lax.rem(c + h, C)), A) for h in range(1, C) for y in range(B)]
        forwards.extend(pass_on(others, parts[k]))

    chore = chores()
    next(chore)
    for k in range(len(parts)):
        sender.sent(one[k])
        if k < last:
            one[k + 1] = spread(0, [(mine, 1)], parts[k + 1])
        second(k)
        next(chore)
        if k >= 1:
            third(k - 1)
        next(chore)
    third(last)
    for _ in range(4):
        next(chore)
    for k in range(len(parts)):
        ending(k)
    arrive(forwards + pair)
    sender.finish()
    for copy in stores:
        copy.wait()


def gather_call(n, cap, chunk, count, images, cot):
    toks, slots, _ = images.shape
    anyspace = pl.BlockSpec(memory_space=pl.ANY)
    vm = pl.BlockSpec(memory_space=pltpu.VMEM)
    return pl.pallas_call(
        functools.partial(gather_kernel, n, cap),
        name="gather",
        out_shape=(
            jax.ShapeDtypeStruct((n,) + chunk.shape, bf16), jax.ShapeDtypeStruct(count.shape, jnp.int32),
            jax.ShapeDtypeStruct((slots, toks, D), bf16), jax.ShapeDtypeStruct((slots, toks, D), bf16),
            jax.ShapeDtypeStruct((cap, toks, D), bf16), jax.ShapeDtypeStruct((cap, toks, D), bf16),
        ),
        in_specs=[vm, vm, anyspace, anyspace],
        out_specs=(vm, vm, anyspace, anyspace, anyspace, anyspace),
        scratch_shapes=[
            pltpu.VMEM((2, toks, slots, D), bf16), pltpu.VMEM((2, D // LANES, toks * slots, LANES), f32), pltpu.VMEM((2, slots, toks, D), bf16),
            pltpu.SemaphoreType.DMA((SEMS,)), pltpu.SemaphoreType.DMA((SEMS,)),
            pltpu.SemaphoreType.DMA((2,)), pltpu.SemaphoreType.DMA((2,)),
        ],
        compiler_params=pltpu.CompilerParams(collective_id=0, has_side_effects=True, vmem_limit_bytes=VMEM_LIMIT),
    )(chunk, count, images, cot)


def scatter_kernel(n, cap, gbuf, ends, other, p_out, p_grad, block_out, input_grad, total, out_t, grad_t,
                   half, got0, got1, got2, got3, r_out, r_grad, own_out, own_grad, wide, out16,
                   send_sem, recv_sem, in_sem, out_sem):
    place = Place(n)
    A, B, C = place.size
    a, b, c = place.at
    core = place.core
    slots, toks, _ = block_out.shape
    loads = [pltpu.make_async_copy(src, dst, in_sem.at[k])
             for k, (src, dst) in enumerate(((block_out, own_out), (input_grad, own_grad)))]
    for copy in loads:
        copy.start()
    greet(place)
    sender = Sender(send_sem, recv_sem)
    parts = row_parts(gbuf.shape[1], PARTS)
    last = len(parts) - 1
    chips = n // 2
    zero = [sender.go(gbuf.at[pl.ds((1 - core) * chips, chips), pl.ds(*part), :], got0.at[:, pl.ds(*part), :], place.partner())
            for part in parts]
    back = [sender.go(p_out, r_out, place.partner()), sender.go(p_grad, r_grad, place.partner())]
    given = jnp.maximum(ends[0, MB - 1] - other[0, MB - 1], 0) // 2
    stores = []

    def shared(own, sent, k, s, carry):
        for j in range(D // LANES):
            cols = slice(j * LANES, (j + 1) * LANES)
            v = jnp.where(s < given, sent[s, :, cols], own[s, :, cols])
            wide[k, j, pl.ds(s, toks, stride=slots), :] = v.astype(f32)
        return carry

    def single(own, k, s, carry):
        for j in range(D // LANES):
            wide[k, j, pl.ds(s, toks, stride=slots), :] = own[s, :, j * LANES:(j + 1) * LANES].astype(f32)
        return carry

    def chores():
        for k, (own, sent, dst) in enumerate(((own_out, r_out, out_t), (own_grad, r_grad, grad_t))):
            loads[k].wait()
            step = -(-(slots - cap) // 3)
            for s in range(cap, slots, step):
                lax.fori_loop(s, min(s + step, slots), functools.partial(single, own, k), 0)
                yield
            arrive(back[k:k + 1])
            lax.fori_loop(0, cap, functools.partial(shared, own, sent, k), 0)
            yield
            for j in range(D // LANES):
                cols = slice(j * LANES, (j + 1) * LANES)
                src = wide.at[k, j]
                if k == 0:
                    out16[:, cols] = wide[k, j].astype(bf16)
                    src = out16.at[:, cols]
                stores.append(pltpu.make_async_copy(src, dst.at[:, cols], out_sem.at[k, j]))
                stores[-1].start()
            yield
        while True:
            yield

    def rows(ref, start, length, part):
        return ref.at[pl.ds(start, length), pl.ds(*part), :]

    def slot(bb, cc):
        return (bb * C + cc) * A

    one, two, three = {}, {}, {}

    def first(k):
        arrive([zero[k]])
        part = parts[k]
        pr = pl.ds(*part)

        def add(i, carry):
            half[i, pr, :] = (gbuf[core * chips + i, pr, :].astype(f32) + got0[i, pr, :].astype(f32)).astype(bf16)
            return carry
        lax.fori_loop(0, chips, add, 0)
        sent = []
        if k % 2 == 0:
            for h in range(1, B):
                to = lax.rem(b + h, B)
                sent.append(sender.go(rows(half, slot(to, 0), C * A, part), rows(got1, (h - 1) * C * A, C * A, part), place.peer(1, h)))
        else:
            for h in range(1, C):
                to = lax.rem(c + h, C)
                for y in range(B):
                    sent.append(sender.go(rows(half, slot(y, to), A, part), rows(got1, ((h - 1) * B + y) * A, A, part), place.peer(2, h)))
        one[k] = sent

    def second(k):
        arrive(one[k])
        part = parts[k]
        pr = pl.ds(*part)
        sent = []
        if k % 2 == 0:
            def add(i, carry):
                v = half[slot(b, 0) + i, pr, :].astype(f32)
                for h in range(1, B):
                    v = v + got1[(h - 1) * C * A + i, pr, :].astype(f32)
                half[slot(b, 0) + i, pr, :] = v.astype(bf16)
                return carry
            lax.fori_loop(0, C * A, add, 0)
            for h in range(1, C):
                to = lax.rem(c + h, C)
                sent.append(sender.go(rows(half, slot(b, to), A, part), rows(got2, (h - 1) * A, A, part), place.peer(2, h)))
        else:
            def add(i, carry):
                y = i // A
                z = lax.rem(i, A)
                v = half[slot(y, c) + z, pr, :].astype(f32)
                for h in range(1, C):
                    v = v + got1[((h - 1) * B + y) * A + z, pr, :].astype(f32)
                half[slot(y, c) + z, pr, :] = v.astype(bf16)
                return carry
            lax.fori_loop(0, B * A, add, 0)
            for h in range(1, B):
                to = lax.rem(b + h, B)
                sent.append(sender.go(rows(half, slot(to, c), A, part), rows(got2, (h - 1) * A, A, part), place.peer(1, h)))
        two[k] = sent

    def third(k):
        arrive(two[k])
        part = parts[k]
        pr = pl.ds(*part)
        others = (C if k % 2 == 0 else B) - 1

        def add(i, carry):
            v = half[slot(b, c) + i, pr, :].astype(f32)
            for h in range(others):
                v = v + got2[h * A + i, pr, :].astype(f32)
            half[slot(b, c) + i, pr, :] = v.astype(bf16)
            return carry
        lax.fori_loop(0, A, add, 0)
        sent = []
        for h in range(1, A):
            to = lax.rem(a + h, A)
            sent.append(sender.go(rows(half, slot(b, c) + to, 1, part), rows(got3, h - 1, 1, part), place.peer(0, h)))
        three[k] = sent

    def ending(k):
        arrive(three[k])
        pr = pl.ds(*parts[k])
        v = half[slot(b, c) + a, pr, :].astype(f32)
        for h in range(A - 1):
            v = v + got3[h, pr, :].astype(f32)
        total[pr, :] = v

    chore = chores()
    first(0)
    first(1)
    next(chore)
    for k in range(0, len(parts), 2):
        pair = [j for j in (k, k + 1) if j <= last]
        nxt = [j for j in (k + 2, k + 3) if j <= last]
        for j in pair:
            sender.sent(one[j])
        for j in nxt:
            first(j)
        next(chore)
        for j in pair:
            second(j)
            next(chore)
        for j in pair:
            third(j)
            next(chore)
    for k in range(len(parts)):
        ending(k)
        if k == 0:
            for _ in range(3):
                next(chore)
    sender.finish()
    for copy in stores:
        copy.wait()


def scatter_call(n, cap, gbuf, ends, other, p_out, p_grad, block_out, input_grad):
    A, B, C = chip_axes(n)
    rows_c = gbuf.shape[1]
    slots, toks, _ = block_out.shape
    anyspace = pl.BlockSpec(memory_space=pl.ANY)
    vm = pl.BlockSpec(memory_space=pltpu.VMEM)
    sm = pl.BlockSpec(memory_space=pltpu.SMEM)
    big = max((B - 1) * C * A, (C - 1) * B * A)
    return pl.pallas_call(
        functools.partial(scatter_kernel, n, cap),
        name="scatter",
        out_shape=(jax.ShapeDtypeStruct((rows_c, LANES), f32), jax.ShapeDtypeStruct((toks * slots, D), bf16),
                   jax.ShapeDtypeStruct((toks * slots, D), f32)),
        in_specs=[vm, sm, sm, anyspace, anyspace, anyspace, anyspace],
        out_specs=(vm, anyspace, anyspace),
        scratch_shapes=[
            pltpu.VMEM((n // 2, rows_c, LANES), bf16), pltpu.VMEM((n // 2, rows_c, LANES), bf16),
            pltpu.VMEM((big, rows_c, LANES), bf16), pltpu.VMEM((max(B, C) * A, rows_c, LANES), bf16),
            pltpu.VMEM((A, rows_c, LANES), bf16),
            pltpu.VMEM((cap, toks, D), bf16), pltpu.VMEM((cap, toks, D), f32),
            pltpu.VMEM((slots, toks, D), bf16), pltpu.VMEM((slots, toks, D), f32),
            pltpu.VMEM((2, D // LANES, toks * slots, LANES), f32), pltpu.VMEM((toks * slots, D), bf16),
            pltpu.SemaphoreType.DMA((SEMS,)), pltpu.SemaphoreType.DMA((SEMS,)),
            pltpu.SemaphoreType.DMA((2,)), pltpu.SemaphoreType.DMA((2, D // LANES)),
        ],
        compiler_params=pltpu.CompilerParams(collective_id=1, has_side_effects=True, vmem_limit_bytes=VMEM_LIMIT),
    )(gbuf, ends, other, p_out, p_grad, block_out, input_grad)


def pack_shard(n, shard, values):
    me = lax.axis_index("dp")
    offset = lax.rem(shard * me, TILE)
    size = chunk_rows(shard) * LANES
    padded = jnp.pad(values, (TILE, size - shard))
    return lax.dynamic_slice_in_dim(padded, TILE - offset, size, 0).reshape(chunk_rows(shard), LANES)


def unpack_shard(n, shard, chunk):
    me = lax.axis_index("dp")
    offset = lax.rem(shard * me, TILE)
    return lax.dynamic_slice_in_dim(chunk.reshape(-1), offset, shard, 0)


def body(n, images, cotangent, master, moment_one, moment_two, batch_ends):
    shard = master.shape[0]
    cap = CAP
    slots, toks, _ = images.shape
    chunk = pack_shard(n, shard, master.astype(bf16))
    wbuf, other, images_r, cot_r, p_images, p_cot = gather_call(
        n, cap, chunk, batch_ends, images.transpose(1, 0, 2), cotangent.transpose(1, 0, 2))
    block_out, input_grad, p_out, p_grad, gbuf = block_call(
        n, shard, cap, batch_ends, other, images_r, cot_r, p_images, p_cot, wbuf)
    part, out_t, grad_t = scatter_call(n, cap, gbuf, batch_ends, other, p_out, p_grad, block_out, input_grad)
    block_out = out_t.reshape(toks, slots, D).transpose(1, 0, 2)
    input_grad = grad_t.reshape(toks, slots, D).transpose(1, 0, 2)
    weight_grad = unpack_shard(n, shard, part)
    first_moment = beta_one * moment_one + (1.0 - beta_one) * weight_grad
    second_moment = beta_two * moment_two + (1.0 - beta_two) * weight_grad * weight_grad
    corrected_one = first_moment / (1.0 - beta_one**STEP)
    corrected_two = second_moment / (1.0 - beta_two**STEP)
    update = -learn_rate * (
        corrected_one / (jnp.sqrt(corrected_two) + adam_eps) + decay_rate * master
    )
    return (block_out, input_grad, weight_grad, first_moment, second_moment, update)


def solution(mesh):
    n = mesh.shape["dp"]
    return jax.shard_map(
        functools.partial(body, n),
        mesh=mesh,
        in_specs=(P("dp", None, None), P("dp", None, None), P("dp"), P("dp"), P("dp"), P("dp", None)),
        out_specs=(P("dp", None, None), P("dp", None, None), P("dp"), P("dp"), P("dp"), P("dp")),
        check_vma=False,
    )
```

```python
import jax, jax.numpy as jnp, functools
from jax import lax
from jax.experimental import pallas as pl
from jax.experimental.pallas import tpu as pltpu
from jax.sharding import PartitionSpec as P

D = 384
FF = 1536
HEADS = 6
HEAD_DIM = 64
TOK = 197
TP = 208
G = 2
ROWS = G * TP
MB = 3
STEP = 10
CAP = 6
FRONT = 8
CH = 32
FFC = 256

beta_one = 0.9
beta_two = 0.999
learn_rate = 0.01
decay_rate = 0.05
adam_eps = 1e-08
norm_eps = 1e-06
f32 = jnp.float32
bf16 = jnp.bfloat16

LANES = 128
TILE = 8 * LANES
MATS = ((0, D, 3 * D), (3456, D, D), (4608, D, FF), (9216, FF, D))
VEC_ROW = 13824
FLAT_ROWS = 13860
VMEM_LIMIT = 60 * 2**20


def dot(a, b, ca=1, cb=0):
    return lax.dot_general(a, b, (((ca,), (cb,)), ((), ())), preferred_element_type=f32)


def chunk_rows(shard):
    return ((shard + TILE - 1 + LANES - 1) // LANES + 15) // 16 * 16


def first_tile(shard, d):
    return (shard * d) // TILE


def compute_kernel(n, shard, cap, slots, ends, other, images, cot, p_images, p_cot, wbuf_h,
                   out_t, grad_t, f_out, f_grad, p_out, p_grad, gbuf_h,
                   flat, w_qkv, w_o, w_1, w_2, vecs, g_qkv, g_o, g_1, g_2t, vsum,
                   xin, gin, oout, gout, x_s, n1_s, r1_s, a1_s, qkv_s, prob_s, ve_s, inv_s, of_s, o_s, m_s, n2_s, r2_s, a2_s,
                   g_s, u_s, act_s, du_s, acc_s, da_s, dm_s, db_s, do_s, dqkv_s, zero_b, zero_f, wbuf, wide_o, wide_g, out16,
                   in_sem, out_sem, zero_sem, w_sem, end_sem):
    load = pltpu.make_async_copy(wbuf_h, wbuf, w_sem.at[0])
    load.start()
    rows_c = wbuf.shape[1]
    live_n = ends[0, MB - 1]
    diff = live_n - other[0, MB - 1]
    own_first = jnp.clip(diff // 2, 0, cap)
    own_n = live_n - own_first
    part_n = jnp.clip((0 - diff) // 2, 0, cap)
    groups = slots // FRONT - 1
    items = own_n + part_n
    steps = (items + G - 1) // G

    def fetch(step, slot, do):
        for i in range(G):
            item = jnp.minimum(step * G + i, items - 1)
            is_own = item < own_n

            @pl.when(is_own)
            def _():
                s = own_first + item
                for k, (src, dst) in enumerate(((images, xin), (cot, gin))):
                    c = pltpu.make_async_copy(src.at[s], dst.at[slot, i], in_sem.at[slot, i, k])
                    c.start() if do else c.wait()

            @pl.when(jnp.logical_not(is_own))
            def _():
                s = item - own_n
                for k, (src, dst) in enumerate(((p_images, xin), (p_cot, gin))):
                    c = pltpu.make_async_copy(src.at[s], dst.at[slot, i], in_sem.at[slot, i, k])
                    c.start() if do else c.wait()

    def flush(step, slot, do):
        for i in range(G):
            item = step * G + i
            is_own = item < own_n
            s_own = own_first + item

            @pl.when(jnp.logical_and(is_own, s_own < FRONT))
            def _():
                for k, (dst, src) in enumerate(((f_out, oout), (f_grad, gout))):
                    c = pltpu.make_async_copy(src.at[slot, i], dst.at[s_own], out_sem.at[slot, i, k])
                    c.start() if do else c.wait()

            @pl.when(jnp.logical_and(jnp.logical_not(is_own), item < items))
            def _():
                s = item - own_n
                for k, (dst, src) in enumerate(((p_out, oout), (p_grad, gout))):
                    c = pltpu.make_async_copy(src.at[slot, i], dst.at[s], out_sem.at[slot, i, k])
                    c.start() if do else c.wait()

    def keep(step, slot, ref, wide, staged):
        for i in range(G):
            item = step * G + i
            s_own = own_first + item
            far = jnp.logical_and(item < own_n, s_own >= FRONT)

            @pl.when(far)
            def _():
                group = s_own // FRONT - 1
                for j in range(D // LANES):
                    wide[group, j, pl.ds(lax.rem(s_own, FRONT), TOK, stride=FRONT), :] = ref[pl.ds(i * TP, TOK), j * LANES:(j + 1) * LANES]

            @pl.when(jnp.logical_not(far))
            def _():
                staged[slot, i] = ref[pl.ds(i * TP, TOK), :].astype(staged.dtype)

    def zeros_copy(do):
        def one(s, carry):
            a = pltpu.make_async_copy(zero_b, f_out.at[s], zero_sem.at[0])
            b = pltpu.make_async_copy(zero_f, f_grad.at[s], zero_sem.at[1])
            a.start() if do else a.wait()
            b.start() if do else b.wait()
            return carry
        lax.fori_loop(jnp.minimum(live_n, FRONT), FRONT, one, 0)

    def zero_slot(s, carry):
        for j in range(D // LANES):
            for ref in (wide_o, wide_g):
                ref[s // FRONT - 1, j, pl.ds(lax.rem(s, FRONT), TOK, stride=FRONT), :] = jnp.zeros((TOK, LANES), f32)
        return carry

    def group_copies(group):
        first = (group + 1) * FRONT
        copies = []
        for j in range(D // LANES):
            cols = slice(j * LANES, (j + 1) * LANES)
            copies.append(pltpu.make_async_copy(
                wide_g.at[group, j].reshape(TOK, FRONT, LANES), grad_t.at[:, pl.ds(first, FRONT), cols], end_sem.at[group, 0, j]))
            copies.append(pltpu.make_async_copy(out16.at[group, j], out_t.at[:, pl.ds(first, FRONT), cols], end_sem.at[group, 1, j]))
        return copies

    def group_leaves(group):
        for j in range(D // LANES):
            out16[group, j] = wide_o[group, j].astype(bf16).reshape(TOK, FRONT, LANES)
        for copy in group_copies(group):
            copy.start()

    def last_step(group):
        by_slot = ((group + 2) * FRONT - own_first + G - 1) // G
        by_count = (own_n + G - 1) // G
        return jnp.maximum(jnp.minimum(by_slot, by_count), 1) - 1

    fetch(0, 0, True)
    zero_b[...] = jnp.zeros(zero_b.shape, bf16)
    zero_f[...] = jnp.zeros(zero_f.shape, f32)
    zeros_copy(True)
    lax.fori_loop(jnp.maximum(live_n, FRONT), slots, zero_slot, 0)
    for ref in (g_qkv, g_o, g_1, g_2t, vsum):
        ref[...] = jnp.zeros(ref.shape, f32)
    load.wait()
    end = 0
    places = chunk_places(n)
    for d in range(n):
        at = places[d]
        top = 8 * first_tile(shard, d)
        if d == 0:
            flat[pl.ds(0, rows_c), :] = wbuf[at].astype(f32)
        else:
            shared = min(end - top, rows_c)
            flat[pl.ds(top, shared), :] += wbuf[at, pl.ds(0, shared), :].astype(f32)
            if shared < rows_c:
                flat[pl.ds(top + shared, rows_c - shared), :] = wbuf[at, pl.ds(shared, rows_c - shared), :].astype(f32)
        end = top + rows_c
    for ref, (row, height, width) in zip((w_qkv, w_o, w_1, w_2), MATS):
        blocks = width // LANES
        for j in range(blocks):
            ref[:, j * LANES:(j + 1) * LANES] = flat[pl.ds(row + j, height, stride=blocks), :].astype(bf16)
    for k in range(8):
        for j in range(3):
            vecs[k, j * LANES:(j + 1) * LANES] = flat[VEC_ROW + 3 * k + j, :]
    for j in range(12):
        vecs[8, j * LANES:(j + 1) * LANES] = flat[VEC_ROW + 24 + j, :]
    g_s[...] = jnp.zeros(g_s.shape, bf16)
    real = lax.broadcasted_iota(jnp.int32, (TP, LANES), 0) < TOK
    ve_s[:, :, LANES:] = jnp.broadcast_to(real.astype(f32).astype(bf16), (G * 3, TP, LANES))

    g1 = vecs[0:1, :D]
    b1 = vecs[1:2, :D]
    g2 = vecs[2:3, :D]
    b2 = vecs[3:4, :D]
    cq = vecs[4:5, :D]
    cv = vecs[5:6, :D]
    co = vecs[6:7, :D]
    c2 = vecs[7:8, :D]

    bqkv = jnp.concatenate([cq, jnp.zeros_like(cq), cv], axis=1)

    lane = lax.broadcasted_iota(jnp.int32, (1, LANES), 1)
    low_half = lane < HEAD_DIM

    def colsum(v):
        return jnp.sum(v.reshape(v.shape[0] // 8, 8, v.shape[1]), axis=0)

    def mean(v):
        return jnp.sum(v, axis=-1, keepdims=True) * (1.0 / D)

    def body(step, carry):
        slot = lax.rem(step, 2)
        fetch(step, slot, False)

        @pl.when(step + 1 < steps)
        def _():
            fetch(step + 1, 1 - slot, True)

        for i in range(G):
            live = (step * G + i < items).astype(bf16)
            x = xin[slot, i].astype(f32)
            x_s[pl.ds(i * TP, TOK), :] = x
            x_s[pl.ds(i * TP + TOK, TP - TOK), :] = jnp.broadcast_to(x[TOK - 1:], (TP - TOK, D))
            g_s[pl.ds(i * TP, TOK), :] = gin[slot, i] * live
        for r in range(0, ROWS, CH):
            rs = pl.ds(r, CH)
            v = x_s[rs, :]
            c = v - mean(v)
            inv = lax.rsqrt(mean(c * c) + norm_eps)
            nv = c * inv
            n1_s[rs, :] = nv
            r1_s[rs, :] = jnp.broadcast_to(inv, (CH, LANES))
            a1_s[rs, :] = (nv * g1 + b1).astype(bf16)
        a1 = a1_s[...]
        qkv_s[...] = (dot(a1, w_qkv[...]) + bqkv).astype(bf16)
        tail = lax.broadcasted_iota(jnp.int32, (16, 1), 0) < TOK - (TP - 16)
        pairs = [(i, p) for i in range(G) for p in range(HEADS // 2)]

        def masked_q(i, p):
            q = qkv_s[pl.ds(i * TP, TP), slice(p * LANES, (p + 1) * LANES)] * 0.125
            zero = jnp.zeros_like(q)
            return jnp.concatenate([jnp.where(low_half, q, zero), jnp.where(low_half, zero, q)], axis=0)

        def keys(i, p):
            return qkv_s[pl.ds(i * TP, TP), slice(D + p * LANES, D + (p + 1) * LANES)]

        def scores(i, p):
            return dot(masked_q(i, p), keys(i, p), 1, 1)

        s = scores(*pairs[0])
        for at, (i, p) in enumerate(pairs):
            ahead = scores(*pairs[at + 1]) if at + 1 < len(pairs) else None
            cols = slice(p * LANES, (p + 1) * LANES)
            vcols = slice(2 * D + p * LANES, 2 * D + (p + 1) * LANES)
            ve_s[at, :TP - 16, :LANES] = qkv_s[pl.ds(i * TP, TP - 16), vcols]
            last = qkv_s[pl.ds((i + 1) * TP - 16, 16), vcols]
            ve_s[at, TP - 16:, :LANES] = jnp.where(tail, last, jnp.zeros_like(last))
            e = jnp.exp(s - jnp.max(s, axis=-1, keepdims=True)).astype(bf16)
            prob_s[at] = e
            oe = dot(e, ve_s[at])
            inv = 1.0 / jnp.where(low_half, oe[:TP, LANES:], oe[TP:, LANES:])
            o = jnp.where(low_half, oe[:TP, :LANES], oe[TP:, :LANES]) * inv
            inv_s[at] = inv
            of_s[at] = o
            o_s[pl.ds(i * TP, TP), cols] = o.astype(bf16)
            s = ahead
        m_s[...] = dot(o_s[...], w_o[...])
        for r in range(0, ROWS, CH):
            rs = pl.ds(r, CH)
            v = x_s[rs, :] + m_s[rs, :] + co
            m_s[rs, :] = v
            c = v - mean(v)
            inv = lax.rsqrt(mean(c * c) + norm_eps)
            nv = c * inv
            n2_s[rs, :] = nv
            r2_s[rs, :] = jnp.broadcast_to(inv, (CH, LANES))
            a2_s[rs, :] = (nv * g2 + b2).astype(bf16)
        a2 = a2_s[...]
        gl = g_s[...]
        def hidden(j):
            fc = slice(j * FFC, (j + 1) * FFC)
            u_s[0, :, fc] = dot(a2, w_1[:, fc])
            da_s[0, :, fc] = dot(gl, w_2[fc, :], 1, 1)
        hidden(0)
        for j in range(FF // FFC):
            if (j + 1) * FFC < FF:
                hidden(j + 1)
            fc = slice(j * FFC, (j + 1) * FFC)
            c1 = vecs[8:9, fc]
            tot = None
            for r in range(0, ROWS, CH):
                rs = pl.ds(r, CH)
                u = u_s[0, rs, fc] + c1
                phi = 0.5 + 0.5 * lax.erf(u * 0.7071067811865476)
                dens = jnp.exp(u * u * -0.5) * 0.3989422804014327
                act_s[0, rs, fc] = (u * phi).astype(bf16)
                du = (da_s[0, rs, fc] * (phi + u * dens)).astype(bf16)
                du_s[0, rs, fc] = du
                part = colsum(du.astype(f32))
                tot = part if tot is None else tot + part
            vsum[8, :, fc] += tot
        dm_s[...] = dot(du_s[0], w_1[...], 1, 1)
        tg2 = tb2 = tco = tc2 = None
        for r in range(0, ROWS, CH):
            rs = pl.ds(r, CH)
            gw = g_s[rs, :].astype(f32)
            if r == 0:
                acc_s[:, :256] = dot(act_s[0], w_2[:, :256])
            if r == 6 * CH:
                acc_s[:, 256:] = dot(act_s[0], w_2[:, 256:])
            e2 = dm_s[rs, :]
            nv = n2_s[rs, :]
            en = e2 * nv
            eg = e2 * g2
            inv = r2_s[rs, :]
            inv = jnp.concatenate([inv, inv, inv], axis=1)
            dm = gw + inv * (eg - mean(eg) - nv * mean(en * g2))
            dm_s[rs, :] = dm
            db = dm.astype(bf16)
            db_s[rs, :] = db
            sums = (colsum(en), colsum(e2), colsum(db.astype(f32)), colsum(gw))
            if tg2 is None:
                tg2, tb2, tco, tc2 = sums
            else:
                tg2, tb2, tco, tc2 = tg2 + sums[0], tb2 + sums[1], tco + sums[2], tc2 + sums[3]
        vsum[2, :, :D] += tg2
        vsum[3, :, :D] += tb2
        vsum[6, :, :D] += tco
        vsum[7, :, :D] += tc2
        m_s[...] = m_s[...] + acc_s[...] + c2

        db = db_s[...]
        g_o[...] += dot(o_s[...], db, 0, 0)
        do_s[...] = dot(db, w_o[...], 1, 1).astype(bf16)
        def slopes(at):
            i, p = pairs[at]
            do = (do_s[pl.ds(i * TP, TP), slice(p * LANES, (p + 1) * LANES)].astype(f32) * inv_s[at]).astype(bf16)
            zero = jnp.zeros_like(do)
            dom = jnp.concatenate([jnp.where(low_half, do, zero), jnp.where(low_half, zero, do)], axis=0)
            t = of_s[at] * do.astype(f32) * -1.0
            hi = t.astype(bf16)
            lo = pltpu.roll(t - hi.astype(f32), HEAD_DIM, 1).astype(bf16)
            rest = jnp.concatenate([jnp.where(low_half, hi, lo), jnp.where(low_half, lo, hi)], axis=0)
            return dom, dot(jnp.concatenate([dom, rest], axis=1), ve_s[at], 1, 1)

        dom, dp = slopes(0)
        for at, (i, p) in enumerate(pairs):
            ir = pl.ds(i * TP, TP)
            fc = slice(at * 256, (at + 1) * 256)
            g_1[:, fc] += dot(a2_s[...], du_s[0, :, fc], 0, 0)
            e = prob_s[at]
            ds = (e.astype(f32) * dp).astype(bf16)
            dv = dot(dom, e, 0, 0).T
            dk = dot(masked_q(i, p), ds, 0, 0).T
            g_2t[:, fc] += dot(g_s[...], act_s[0, :, fc], 0, 0)
            dq2 = dot(ds, keys(i, p) * 0.125)
            dqkv_s[ir, slice(p * LANES, (p + 1) * LANES)] = jnp.where(low_half, dq2[:TP], dq2[TP:]).astype(bf16)
            dqkv_s[ir, slice(D + p * LANES, D + (p + 1) * LANES)] = dk.astype(bf16)
            vcols = slice(2 * D + p * LANES, 2 * D + (p + 1) * LANES)
            dqkv_s[pl.ds(i * TP, TP - 16), vcols] = dv[:TP - 16].astype(bf16)
            dqkv_s[pl.ds((i + 1) * TP - 16, 16), vcols] = jnp.where(tail, dv[TP - 16:], 0.0).astype(bf16)
            dom, dp = slopes(at + 1) if at + 1 < len(pairs) else (None, None)
        dqkv = dqkv_s[...]
        acc_s[...] = dot(dqkv, w_qkv[...], 1, 1)
        g_qkv[...] += dot(a1_s[...], dqkv, 0, 0)
        tg1 = tb1 = tcq = tcv = None
        for r in range(0, ROWS, CH):
            rs = pl.ds(r, CH)
            e1 = acc_s[rs, :]
            nv = n1_s[rs, :]
            en = e1 * nv
            eg = e1 * g1
            inv = r1_s[rs, :]
            inv = jnp.concatenate([inv, inv, inv], axis=1)
            dm_s[rs, :] += inv * (eg - mean(eg) - nv * mean(en * g1))
            sums = (colsum(en), colsum(e1), colsum(dqkv_s[rs, :D].astype(f32)), colsum(dqkv_s[rs, 2 * D:].astype(f32)))
            if tg1 is None:
                tg1, tb1, tcq, tcv = sums
            else:
                tg1, tb1, tcq, tcv = tg1 + sums[0], tb1 + sums[1], tcq + sums[2], tcv + sums[3]
        vsum[0, :, :D] += tg1
        vsum[1, :, :D] += tb1
        vsum[4, :, :D] += tcq
        vsum[5, :, :D] += tcv

        @pl.when(step >= 2)
        def _():
            flush(step - 2, slot, False)

        keep(step, slot, m_s, wide_o, oout)
        keep(step, slot, dm_s, wide_g, gout)
        flush(step, slot, True)
        for group in range(groups):
            @pl.when(step == last_step(group))
            def _():
                group_leaves(group)
        return carry

    lax.fori_loop(0, steps, body, 0)

    ends_copies = []
    for ref, (row, height, width) in zip((g_qkv, g_o, g_1), MATS):
        blocks = width // LANES
        for j in range(blocks):
            flat[pl.ds(row + j, height, stride=blocks), :] = ref[:, j * LANES:(j + 1) * LANES]
    row = MATS[3][0]
    for c in range(FF // LANES):
        t = g_2t[:, c * LANES:(c + 1) * LANES].T
        for j in range(3):
            flat[pl.ds(row + 3 * LANES * c + j, LANES, stride=3), :] = t[:, j * LANES:(j + 1) * LANES]
    for k in range(9):
        t = jnp.sum(vsum[k], axis=0, keepdims=True)
        for j in range(12 if k == 8 else 3):
            flat[pl.ds(VEC_ROW + 3 * k + j, 1), :] = t[:, j * LANES:(j + 1) * LANES]
    flat[pl.ds(FLAT_ROWS, flat.shape[0] - FLAT_ROWS), :] = jnp.zeros((flat.shape[0] - FLAT_ROWS, LANES), f32)
    for d in range(n):
        wbuf[places[d]] = flat[pl.ds(8 * first_tile(shard, d), rows_c), :].astype(bf16)
        copy = pltpu.make_async_copy(wbuf.at[places[d]], gbuf_h.at[places[d]], w_sem.at[d])
        copy.start()
        ends_copies.append(copy)

    @pl.when(steps >= 2)
    def _():
        flush(steps - 2, lax.rem(steps, 2), False)
    flush(steps - 1, lax.rem(steps + 1, 2), False)
    zeros_copy(False)
    for group in range(groups):
        ends_copies.extend(group_copies(group))
    for copy in ends_copies:
        copy.wait()


def flat_height(n, shard):
    return 8 * first_tile(shard, n - 1) + chunk_rows(shard)


def block_call(n, shard, cap, ends, other, images, cot, p_images, p_cot, wbuf):
    slots = images.shape[0]
    anyspace = pl.BlockSpec(memory_space=pl.ANY)
    rows_c = chunk_rows(shard)
    groups = slots // FRONT - 1
    scratch = [
        pltpu.VMEM((flat_height(n, shard), LANES), f32),
        pltpu.VMEM((D, 3 * D), bf16), pltpu.VMEM((D, D), bf16), pltpu.VMEM((D, FF), bf16), pltpu.VMEM((FF, D), bf16),
        pltpu.VMEM((16, FF), f32),
        pltpu.VMEM((D, 3 * D), f32), pltpu.VMEM((D, D), f32), pltpu.VMEM((D, FF), f32), pltpu.VMEM((D, FF), f32),
        pltpu.VMEM((9, 8, FF), f32),
        pltpu.VMEM((2, G, TOK, D), bf16), pltpu.VMEM((2, G, TOK, D), bf16),
        pltpu.VMEM((2, G, TOK, D), bf16), pltpu.VMEM((2, G, TOK, D), f32),
        pltpu.VMEM((ROWS, D), f32),
        pltpu.VMEM((ROWS, D), f32), pltpu.VMEM((ROWS, LANES), f32), pltpu.VMEM((ROWS, D), bf16),
        pltpu.VMEM((ROWS, 3 * D), bf16),
        pltpu.VMEM((G * 3, 2 * TP, TP), bf16), pltpu.VMEM((G * 3, TP, 2 * LANES), bf16),
        pltpu.VMEM((G * 3, TP, LANES), f32), pltpu.VMEM((G * 3, TP, LANES), f32),
        pltpu.VMEM((ROWS, D), bf16),
        pltpu.VMEM((ROWS, D), f32),
        pltpu.VMEM((ROWS, D), f32), pltpu.VMEM((ROWS, LANES), f32), pltpu.VMEM((ROWS, D), bf16),
        pltpu.VMEM((ROWS, D), bf16),
        pltpu.VMEM((1, ROWS, FF), f32), pltpu.VMEM((1, ROWS, FF), bf16), pltpu.VMEM((1, ROWS, FF), bf16),
        pltpu.VMEM((ROWS, D), f32),
        pltpu.VMEM((1, ROWS, FF), f32),
        pltpu.VMEM((ROWS, D), f32), pltpu.VMEM((ROWS, D), bf16), pltpu.VMEM((ROWS, D), bf16),
        pltpu.VMEM((ROWS, 3 * D), bf16),
        pltpu.VMEM((TOK, D), bf16), pltpu.VMEM((TOK, D), f32),
        pltpu.VMEM((n, rows_c, LANES), bf16),
        pltpu.VMEM((groups, D // LANES, TOK * FRONT, LANES), f32), pltpu.VMEM((groups, D // LANES, TOK * FRONT, LANES), f32),
        pltpu.VMEM((groups, D // LANES, TOK, FRONT, LANES), bf16),
        pltpu.SemaphoreType.DMA((2, G, 2)), pltpu.SemaphoreType.DMA((2, G, 2)), pltpu.SemaphoreType.DMA((2,)),
        pltpu.SemaphoreType.DMA((n,)), pltpu.SemaphoreType.DMA((groups, 2, D // LANES)),
    ]
    return pl.pallas_call(
        functools.partial(compute_kernel, n, shard, cap, slots),
        name="block",
        out_shape=(
            jax.ShapeDtypeStruct((TOK, slots, D), bf16),
            jax.ShapeDtypeStruct((TOK, slots, D), f32),
            jax.ShapeDtypeStruct((FRONT, TOK, D), bf16),
            jax.ShapeDtypeStruct((FRONT, TOK, D), f32),
            jax.ShapeDtypeStruct((cap,) + images.shape[1:], bf16),
            jax.ShapeDtypeStruct((cap,) + images.shape[1:], f32),
            jax.ShapeDtypeStruct((n, rows_c, LANES), bf16),
        ),
        in_specs=[pl.BlockSpec(memory_space=pltpu.SMEM), pl.BlockSpec(memory_space=pltpu.SMEM)] + [anyspace] * 5,
        out_specs=(anyspace,) * 7,
        scratch_shapes=scratch,
        compiler_params=pltpu.CompilerParams(vmem_limit_bytes=VMEM_LIMIT),
    )(ends, other, images, cot, p_images, p_cot, wbuf)


def chip_axes(n):
    chips = n // 2
    if chips % 16 == 0:
        rest = chips // 4
        side = 2 if rest == 4 else 4
        return (4, rest // side, side)
    return (chips, 1, 1)


class Place:
    def __init__(self, n):
        self.size = chip_axes(n)
        self.stride = (self.size[1] * self.size[2] * 2, self.size[2] * 2, 2)
        self.me = lax.axis_index("dp")
        self.core = lax.rem(self.me, 2)
        self.at = [lax.rem(self.me // self.stride[k], self.size[k]) for k in range(3)]

    def peer(self, axis, hop):
        to = lax.rem(self.at[axis] + hop, self.size[axis])
        return self.me + (to - self.at[axis]) * self.stride[axis]

    def partner(self):
        return self.me + 1 - 2 * self.core

    def slot(self, core, a, b, c):
        return ((core * self.size[1] + b) * self.size[2] + c) * self.size[0] + a

    def everyone(self):
        return [self.peer(k, h) for k in range(3) for h in range(1, self.size[k])] + [self.partner()]


def chunk_places(n):
    A, B, C = chip_axes(n)
    order = [((a * B + b) * C + c) * 2 + core for core in range(2) for b in range(B) for c in range(C) for a in range(A)]
    return [order.index(d) for d in range(n)]


def greet(place):
    barrier = pltpu.get_barrier_semaphore()
    everyone = place.everyone()
    for other in everyone:
        pl.semaphore_signal(barrier, inc=1, device_id=(other,), device_id_type=pl.DeviceIdType.MESH)
    pl.semaphore_wait(barrier, len(everyone))


class Sender:
    def __init__(self, send_sem, recv_sem):
        self.send_sem, self.recv_sem, self.all = send_sem, recv_sem, []

    def go(self, src, dst, device):
        k = len(self.all)
        copy = pltpu.make_async_remote_copy(
            src_ref=src, dst_ref=dst, send_sem=self.send_sem.at[k], recv_sem=self.recv_sem.at[k],
            device_id=(device,), device_id_type=pl.DeviceIdType.MESH)
        copy.start()
        self.all.append([copy, False])
        return copy

    def sent(self, copies):
        for entry in self.all:
            if any(entry[0] is copy for copy in copies) and not entry[1]:
                entry[0].wait_send()
                entry[1] = True

    def finish(self):
        self.sent([entry[0] for entry in self.all])


def arrive(copies):
    for copy in copies:
        copy.wait_recv()


def row_parts(rows, parts):
    tiles = rows // 16
    parts = min(parts, tiles)
    cuts = [tiles * k // parts * 16 for k in range(parts + 1)]
    return [(cuts[k], cuts[k + 1] - cuts[k]) for k in range(parts)]


PARTS = 4
SEMS = 192


def gather_kernel(n, cap, chunk, count, images, cot, wbuf_h, other, images_r, cot_r, p_images, p_cot,
                  wbuf, xin, wide, relay, send_sem, recv_sem, in_sem, out_sem, w_sem):
    place = Place(n)
    A, B, C = place.size
    a, b, c = place.at
    core = place.core
    loads = [pltpu.make_async_copy(src, xin.at[k], in_sem.at[k]) for k, src in enumerate((images, cot))]
    for copy in loads:
        copy.start()
    mine = place.slot(core, a, b, c)
    wbuf[mine] = chunk[...]
    greet(place)
    sender = Sender(send_sem, recv_sem)
    parts = row_parts(chunk.shape[0], PARTS)
    last = len(parts) - 1
    slots = images.shape[1]
    toks = images.shape[0]

    def run(start, length, part):
        return wbuf.at[pl.ds(start, length), pl.ds(part[0], part[1]), :]

    def spread(axis, runs, part):
        return [sender.go(run(s, l, part), run(s, l, part), place.peer(axis, hop))
                for hop in range(1, place.size[axis]) for s, l in runs]

    def pass_on(runs, part):
        return [sender.go(run(s, l, part), run(s, l, part), place.partner()) for s, l in runs]

    def widen(k, t, m):
        v = xin[k, pl.ds(t, m)].reshape(m * slots, D).astype(f32)
        for j in range(D // LANES):
            wide[k, j, pl.ds(t * slots, m * slots), :] = v[:, j * LANES:(j + 1) * LANES]

    def one_slot(k, s, carry):
        for j in range(D // LANES):
            relay[k, s, :, j * LANES:(j + 1) * LANES] = wide[k, j, pl.ds(s, toks, stride=slots), :].astype(bf16)
        return carry

    def chores():
        for k in range(2):
            loads[k].wait()
            for t in range(0, toks, 100):
                widen(k, t, min(100, toks - t))
                yield
            step = -(-slots // 4)
            for s in range(0, slots, step):
                lax.fori_loop(s, min(s + step, slots), functools.partial(one_slot, k), 0)
                yield
            pair.append(sender.go(relay.at[k, pl.ds(0, cap)], (p_images, p_cot)[k], place.partner()))
            stores.append(pltpu.make_async_copy(relay.at[k], (images_r, cot_r)[k], out_sem.at[k]))
            stores[-1].start()
        while True:
            yield

    one, two, three, stores = {}, {}, {}, []
    forwards = [[] for _ in parts]
    one[0] = spread(0, [(mine, 1)], parts[0])
    pair = [sender.go(count, other, place.partner())]

    def second(k):
        arrive(one[k])
        runs = [(place.slot(core, 0, b, c), A)]
        two[k] = spread(2 if k % 2 == 0 else 1, runs, parts[k])
        forwards[k].extend(pass_on(runs, parts[k]))

    def third(k):
        arrive(two[k])
        if k % 2 == 0:
            runs = [(place.slot(core, 0, b, 0), C * A)]
            others = [(place.slot(core, 0, b, lax.rem(c + h, C)), A) for h in range(1, C)]
        else:
            runs = [(place.slot(core, 0, y, c), A) for y in range(B)]
            others = [(place.slot(core, 0, lax.rem(b + h, B), c), A) for h in range(1, B)]
        three[k] = spread(1 if k % 2 == 0 else 2, runs, parts[k])
        forwards[k].extend(pass_on(others, parts[k]))

    def ending(k):
        arrive(three[k])
        if k % 2 == 0:
            others = [(place.slot(core, 0, lax.rem(b + h, B), 0), C * A) for h in range(1, B)]
        else:
            others = [(place.slot(core, 0, y, lax.rem(c + h, C)), A) for h in range(1, C) for y in range(B)]
        forwards[k].extend(pass_on(others, parts[k]))

    chore = chores()
    next(chore)
    for k in range(len(parts)):
        sender.sent(one[k])
        if k < last:
            one[k + 1] = spread(0, [(mine, 1)], parts[k + 1])
        second(k)
        next(chore)
        if k >= 1:
            third(k - 1)
        next(chore)
    third(last)
    for _ in range(4):
        next(chore)
    for k in range(len(parts)):
        ending(k)
    for k, part in enumerate(parts):
        arrive(forwards[k])
        stores.append(pltpu.make_async_copy(wbuf.at[:, pl.ds(*part), :], wbuf_h.at[:, pl.ds(*part), :], w_sem.at[k]))
        stores[-1].start()
    arrive(pair)
    sender.finish()
    for copy in stores:
        copy.wait()


def gather_call(n, cap, chunk, count, images, cot):
    toks, slots, _ = images.shape
    anyspace = pl.BlockSpec(memory_space=pl.ANY)
    vm = pl.BlockSpec(memory_space=pltpu.VMEM)
    return pl.pallas_call(
        functools.partial(gather_kernel, n, cap),
        name="gather",
        out_shape=(
            jax.ShapeDtypeStruct((n,) + chunk.shape, bf16), jax.ShapeDtypeStruct(count.shape, jnp.int32),
            jax.ShapeDtypeStruct((slots, toks, D), bf16), jax.ShapeDtypeStruct((slots, toks, D), bf16),
            jax.ShapeDtypeStruct((cap, toks, D), bf16), jax.ShapeDtypeStruct((cap, toks, D), bf16),
        ),
        in_specs=[vm, vm, anyspace, anyspace],
        out_specs=(anyspace, vm, anyspace, anyspace, anyspace, anyspace),
        scratch_shapes=[
            pltpu.VMEM((n,) + chunk.shape, bf16),
            pltpu.VMEM((2, toks, slots, D), bf16), pltpu.VMEM((2, D // LANES, toks * slots, LANES), f32), pltpu.VMEM((2, slots, toks, D), bf16),
            pltpu.SemaphoreType.DMA((SEMS,)), pltpu.SemaphoreType.DMA((SEMS,)),
            pltpu.SemaphoreType.DMA((2,)), pltpu.SemaphoreType.DMA((2,)), pltpu.SemaphoreType.DMA((PARTS,)),
        ],
        compiler_params=pltpu.CompilerParams(collective_id=0, has_side_effects=True, vmem_limit_bytes=VMEM_LIMIT),
    )(chunk, count, images, cot)


def scatter_kernel(n, cap, gbuf, ends, other, p_out, p_grad, f_out, f_grad, total, out_f, grad_f,
                   half, got0, got1, got2, got3, r_out, r_grad, own_out, own_grad, wide,
                   send_sem, recv_sem, in_sem, half_sem):
    place = Place(n)
    A, B, C = place.size
    a, b, c = place.at
    core = place.core
    slots, toks, _ = f_out.shape
    loads = [pltpu.make_async_copy(src, dst, in_sem.at[k])
             for k, (src, dst) in enumerate(((f_out, own_out), (f_grad, own_grad)))]
    for copy in loads:
        copy.start()
    greet(place)
    sender = Sender(send_sem, recv_sem)
    parts = row_parts(gbuf.shape[1], PARTS)
    last = len(parts) - 1
    chips = n // 2
    halves = [pltpu.make_async_copy(gbuf.at[pl.ds(core * chips, chips), pl.ds(*part), :], half.at[:, pl.ds(*part), :], half_sem.at[k])
              for k, part in enumerate(parts)]
    zero = [sender.go(gbuf.at[pl.ds((1 - core) * chips, chips), pl.ds(*part), :], got0.at[:, pl.ds(*part), :], place.partner())
            for part in parts]
    back = [sender.go(p_out, r_out, place.partner()), sender.go(p_grad, r_grad, place.partner())]
    for copy in halves:
        copy.start()
    given = jnp.maximum(ends[0, MB - 1] - other[0, MB - 1], 0) // 2

    def shared(own, sent, k, s, carry):
        for j in range(D // LANES):
            cols = slice(j * LANES, (j + 1) * LANES)
            v = jnp.where(s < given, sent[s, :, cols], own[s, :, cols])
            wide[k, j, pl.ds(s, toks, stride=slots), :] = v.astype(f32)
        return carry

    def single(own, k, s, carry):
        for j in range(D // LANES):
            wide[k, j, pl.ds(s, toks, stride=slots), :] = own[s, :, j * LANES:(j + 1) * LANES].astype(f32)
        return carry

    def chores():
        for k, (own, sent, dst) in enumerate(((own_out, r_out, out_f), (own_grad, r_grad, grad_f))):
            loads[k].wait()
            arrive(back[k:k + 1])
            lax.fori_loop(0, cap, functools.partial(shared, own, sent, k), 0)
            yield
            lax.fori_loop(cap, slots, functools.partial(single, own, k), 0)
            for j in range(D // LANES):
                dst[:, j * LANES:(j + 1) * LANES] = wide[k, j].astype(dst.dtype)
            yield
        while True:
            yield

    def rows(ref, start, length, part):
        return ref.at[pl.ds(start, length), pl.ds(*part), :]

    def slot(bb, cc):
        return (bb * C + cc) * A

    one, two, three = {}, {}, {}

    def first(k):
        arrive([zero[k]])
        halves[k].wait()
        part = parts[k]
        pr = pl.ds(*part)

        def add(i, carry):
            half[i, pr, :] = (half[i, pr, :].astype(f32) + got0[i, pr, :].astype(f32)).astype(bf16)
            return carry
        lax.fori_loop(0, chips, add, 0)
        sent = []
        if k % 2 == 0:
            for h in range(1, B):
                to = lax.rem(b + h, B)
                sent.append(sender.go(rows(half, slot(to, 0), C * A, part), rows(got1, (h - 1) * C * A, C * A, part), place.peer(1, h)))
        else:
            for h in range(1, C):
                to = lax.rem(c + h, C)
                for y in range(B):
                    sent.append(sender.go(rows(half, slot(y, to), A, part), rows(got1, ((h - 1) * B + y) * A, A, part), place.peer(2, h)))
        one[k] = sent

    def second(k):
        arrive(one[k])
        part = parts[k]
        pr = pl.ds(*part)
        sent = []
        if k % 2 == 0:
            def add(i, carry):
                v = half[slot(b, 0) + i, pr, :].astype(f32)
                for h in range(1, B):
                    v = v + got1[(h - 1) * C * A + i, pr, :].astype(f32)
                half[slot(b, 0) + i, pr, :] = v.astype(bf16)
                return carry
            lax.fori_loop(0, C * A, add, 0)
            for h in range(1, C):
                to = lax.rem(c + h, C)
                sent.append(sender.go(rows(half, slot(b, to), A, part), rows(got2, (h - 1) * A, A, part), place.peer(2, h)))
        else:
            def add(i, carry):
                y = i // A
                z = lax.rem(i, A)
                v = half[slot(y, c) + z, pr, :].astype(f32)
                for h in range(1, C):
                    v = v + got1[((h - 1) * B + y) * A + z, pr, :].astype(f32)
                half[slot(y, c) + z, pr, :] = v.astype(bf16)
                return carry
            lax.fori_loop(0, B * A, add, 0)
            for h in range(1, B):
                to = lax.rem(b + h, B)
                sent.append(sender.go(rows(half, slot(to, c), A, part), rows(got2, (h - 1) * A, A, part), place.peer(1, h)))
        two[k] = sent

    def third(k):
        arrive(two[k])
        part = parts[k]
        pr = pl.ds(*part)
        others = (C if k % 2 == 0 else B) - 1

        def add(i, carry):
            v = half[slot(b, c) + i, pr, :].astype(f32)
            for h in range(others):
                v = v + got2[h * A + i, pr, :].astype(f32)
            half[slot(b, c) + i, pr, :] = v.astype(bf16)
            return carry
        lax.fori_loop(0, A, add, 0)
        sent = []
        for h in range(1, A):
            to = lax.rem(a + h, A)
            sent.append(sender.go(rows(half, slot(b, c) + to, 1, part), rows(got3, h - 1, 1, part), place.peer(0, h)))
        three[k] = sent

    def ending(k):
        arrive(three[k])
        pr = pl.ds(*parts[k])
        v = half[slot(b, c) + a, pr, :].astype(f32)
        for h in range(A - 1):
            v = v + got3[h, pr, :].astype(f32)
        total[pr, :] = v

    chore = chores()
    first(0)
    first(1)
    next(chore)
    for k in range(0, len(parts), 2):
        pair = [j for j in (k, k + 1) if j <= last]
        nxt = [j for j in (k + 2, k + 3) if j <= last]
        for j in pair:
            sender.sent(one[j])
        for j in nxt:
            first(j)
        next(chore)
        for j in pair:
            second(j)
            next(chore)
        for j in pair:
            third(j)
            next(chore)
    for k in range(len(parts)):
        ending(k)
        if k == 0:
            for _ in range(3):
                next(chore)
    sender.finish()


def scatter_call(n, cap, gbuf, ends, other, p_out, p_grad, f_out, f_grad):
    A, B, C = chip_axes(n)
    rows_c = gbuf.shape[1]
    slots, toks, _ = f_out.shape
    anyspace = pl.BlockSpec(memory_space=pl.ANY)
    vm = pl.BlockSpec(memory_space=pltpu.VMEM)
    sm = pl.BlockSpec(memory_space=pltpu.SMEM)
    big = max((B - 1) * C * A, (C - 1) * B * A)
    return pl.pallas_call(
        functools.partial(scatter_kernel, n, cap),
        name="scatter",
        out_shape=(jax.ShapeDtypeStruct((rows_c, LANES), f32), jax.ShapeDtypeStruct((toks * slots, D), bf16),
                   jax.ShapeDtypeStruct((toks * slots, D), f32)),
        in_specs=[anyspace, sm, sm, anyspace, anyspace, anyspace, anyspace],
        out_specs=(vm, vm, vm),
        scratch_shapes=[
            pltpu.VMEM((n // 2, rows_c, LANES), bf16), pltpu.VMEM((n // 2, rows_c, LANES), bf16),
            pltpu.VMEM((big, rows_c, LANES), bf16), pltpu.VMEM((max(B, C) * A, rows_c, LANES), bf16),
            pltpu.VMEM((A, rows_c, LANES), bf16),
            pltpu.VMEM((cap, toks, D), bf16), pltpu.VMEM((cap, toks, D), f32),
            pltpu.VMEM((slots, toks, D), bf16), pltpu.VMEM((slots, toks, D), f32),
            pltpu.VMEM((2, D // LANES, toks * slots, LANES), f32),
            pltpu.SemaphoreType.DMA((SEMS,)), pltpu.SemaphoreType.DMA((SEMS,)),
            pltpu.SemaphoreType.DMA((2,)), pltpu.SemaphoreType.DMA((PARTS,)),
        ],
        compiler_params=pltpu.CompilerParams(collective_id=1, has_side_effects=True, vmem_limit_bytes=VMEM_LIMIT),
    )(gbuf, ends, other, p_out, p_grad, f_out, f_grad)


def pack_shard(n, shard, values):
    me = lax.axis_index("dp")
    offset = lax.rem(shard * me, TILE)
    size = chunk_rows(shard) * LANES
    padded = jnp.pad(values, (TILE, size - shard))
    return lax.dynamic_slice_in_dim(padded, TILE - offset, size, 0).reshape(chunk_rows(shard), LANES)


def unpack_shard(n, shard, chunk):
    me = lax.axis_index("dp")
    offset = lax.rem(shard * me, TILE)
    return lax.dynamic_slice_in_dim(chunk.reshape(-1), offset, shard, 0)


def body(n, images, cotangent, master, moment_one, moment_two, batch_ends):
    shard = master.shape[0]
    cap = CAP
    slots, toks, _ = images.shape
    chunk = pack_shard(n, shard, master.astype(bf16))
    wbuf, other, images_r, cot_r, p_images, p_cot = gather_call(
        n, cap, chunk, batch_ends, images.transpose(1, 0, 2), cotangent.transpose(1, 0, 2))
    out_t, grad_t, f_out, f_grad, p_out, p_grad, gbuf = block_call(
        n, shard, cap, batch_ends, other, images_r, cot_r, p_images, p_cot, wbuf)
    part, out_f, grad_f = scatter_call(n, cap, gbuf, batch_ends, other, p_out, p_grad, f_out, f_grad)
    block_out = lax.dynamic_update_slice(out_t, out_f.reshape(toks, FRONT, D), (0, 0, 0)).transpose(1, 0, 2)
    input_grad = lax.dynamic_update_slice(grad_t, grad_f.reshape(toks, FRONT, D), (0, 0, 0)).transpose(1, 0, 2)
    weight_grad = unpack_shard(n, shard, part)
    first_moment = beta_one * moment_one + (1.0 - beta_one) * weight_grad
    second_moment = beta_two * moment_two + (1.0 - beta_two) * weight_grad * weight_grad
    corrected_one = first_moment / (1.0 - beta_one**STEP)
    corrected_two = second_moment / (1.0 - beta_two**STEP)
    update = -learn_rate * (
        corrected_one / (jnp.sqrt(corrected_two) + adam_eps) + decay_rate * master
    )
    return (block_out, input_grad, weight_grad, first_moment, second_moment, update)


def solution(mesh):
    n = mesh.shape["dp"]
    return jax.shard_map(
        functools.partial(body, n),
        mesh=mesh,
        in_specs=(P("dp", None, None), P("dp", None, None), P("dp"), P("dp"), P("dp"), P("dp", None)),
        out_specs=(P("dp", None, None), P("dp", None, None), P("dp"), P("dp"), P("dp"), P("dp")),
        check_vma=False,
    )
```

```python
import jax, jax.numpy as jnp, functools
from jax import lax
from jax.experimental import pallas as pl
from jax.experimental.pallas import tpu as pltpu
from jax.sharding import PartitionSpec as P

D = 384
FF = 1536
HEADS = 6
HEAD_DIM = 64
TOK = 197
TP = 208
G = 2
ROWS = G * TP
MB = 3
STEP = 10
CAP = 6
FRONT = 8
CH = 32
FFC = 256

beta_one = 0.9
beta_two = 0.999
learn_rate = 0.01
decay_rate = 0.05
adam_eps = 1e-08
norm_eps = 1e-06
f32 = jnp.float32
bf16 = jnp.bfloat16

LANES = 128
TILE = 8 * LANES
MATS = ((0, D, 3 * D), (3456, D, D), (4608, D, FF), (9216, FF, D))
VEC_ROW = 13824
FLAT_ROWS = 13860
VMEM_LIMIT = 60 * 2**20


def dot(a, b, ca=1, cb=0):
    return lax.dot_general(a, b, (((ca,), (cb,)), ((), ())), preferred_element_type=f32)


def chunk_rows(shard):
    return ((shard + TILE - 1 + LANES - 1) // LANES + 15) // 16 * 16


def first_tile(shard, d):
    return (shard * d) // TILE


def compute_kernel(n, shard, cap, slots, ends, other, images, cot, p_images, p_cot, wbuf_h,
                   out_t, grad_t, f_out, f_grad, p_out, p_grad, gbuf_h,
                   flat, w_qkv, w_o, w_1, w_2, vecs, g_qkv, g_o, g_1, g_2t, vsum,
                   xin, gin, oout, gout, x_s, n1_s, r1_s, a1_s, qkv_s, prob_s, ve_s, inv_s, of_s, o_s, m_s, n2_s, r2_s, a2_s,
                   g_s, u_s, act_s, du_s, acc_s, da_s, dm_s, db_s, do_s, dqkv_s, zero_b, zero_f, wbuf, wide_o, wide_g, out16,
                   in_sem, out_sem, zero_sem, w_sem, end_sem):
    places = chunk_places(n)
    loads = [pltpu.make_async_copy(wbuf_h.at[places[d]], wbuf.at[places[d]], w_sem.at[d]) for d in range(n)]
    for copy in loads:
        copy.start()
    rows_c = wbuf.shape[1]
    live_n = ends[0, MB - 1]
    diff = live_n - other[0, MB - 1]
    own_first = jnp.clip(diff // 2, 0, cap)
    own_n = live_n - own_first
    part_n = jnp.clip((0 - diff) // 2, 0, cap)
    groups = slots // FRONT - 1
    items = own_n + part_n
    steps = (items + G - 1) // G

    def fetch(step, slot, do):
        for i in range(G):
            item = jnp.minimum(step * G + i, items - 1)
            is_own = item < own_n

            @pl.when(is_own)
            def _():
                s = own_first + item
                for k, (src, dst) in enumerate(((images, xin), (cot, gin))):
                    c = pltpu.make_async_copy(src.at[s], dst.at[slot, i], in_sem.at[slot, i, k])
                    c.start() if do else c.wait()

            @pl.when(jnp.logical_not(is_own))
            def _():
                s = item - own_n
                for k, (src, dst) in enumerate(((p_images, xin), (p_cot, gin))):
                    c = pltpu.make_async_copy(src.at[s], dst.at[slot, i], in_sem.at[slot, i, k])
                    c.start() if do else c.wait()

    def flush(step, slot, do):
        for i in range(G):
            item = step * G + i
            is_own = item < own_n
            s_own = own_first + item

            @pl.when(jnp.logical_and(is_own, s_own < FRONT))
            def _():
                for k, (dst, src) in enumerate(((f_out, oout), (f_grad, gout))):
                    c = pltpu.make_async_copy(src.at[slot, i], dst.at[s_own], out_sem.at[slot, i, k])
                    c.start() if do else c.wait()

            @pl.when(jnp.logical_and(jnp.logical_not(is_own), item < items))
            def _():
                s = item - own_n
                for k, (dst, src) in enumerate(((p_out, oout), (p_grad, gout))):
                    c = pltpu.make_async_copy(src.at[slot, i], dst.at[s], out_sem.at[slot, i, k])
                    c.start() if do else c.wait()

    def keep(step, slot, ref, wide, staged):
        for i in range(G):
            item = step * G + i
            s_own = own_first + item
            far = jnp.logical_and(item < own_n, s_own >= FRONT)

            @pl.when(far)
            def _():
                group = s_own // FRONT - 1
                for j in range(D // LANES):
                    wide[group, j, pl.ds(lax.rem(s_own, FRONT), TOK, stride=FRONT), :] = ref[pl.ds(i * TP, TOK), j * LANES:(j + 1) * LANES]

            @pl.when(jnp.logical_not(far))
            def _():
                staged[slot, i] = ref[pl.ds(i * TP, TOK), :].astype(staged.dtype)

    def zeros_copy(do):
        def one(s, carry):
            a = pltpu.make_async_copy(zero_b, f_out.at[s], zero_sem.at[0])
            b = pltpu.make_async_copy(zero_f, f_grad.at[s], zero_sem.at[1])
            a.start() if do else a.wait()
            b.start() if do else b.wait()
            return carry
        lax.fori_loop(jnp.minimum(live_n, FRONT), FRONT, one, 0)

    def zero_slot(s, carry):
        for j in range(D // LANES):
            for ref in (wide_o, wide_g):
                ref[s // FRONT - 1, j, pl.ds(lax.rem(s, FRONT), TOK, stride=FRONT), :] = jnp.zeros((TOK, LANES), f32)
        return carry

    def group_copies(group):
        first = (group + 1) * FRONT
        copies = []
        for j in range(D // LANES):
            cols = slice(j * LANES, (j + 1) * LANES)
            copies.append(pltpu.make_async_copy(
                wide_g.at[group, j].reshape(TOK, FRONT, LANES), grad_t.at[:, pl.ds(first, FRONT), cols], end_sem.at[group, 0, j]))
            copies.append(pltpu.make_async_copy(out16.at[group, j], out_t.at[:, pl.ds(first, FRONT), cols], end_sem.at[group, 1, j]))
        return copies

    def group_leaves(group):
        for j in range(D // LANES):
            out16[group, j] = wide_o[group, j].astype(bf16).reshape(TOK, FRONT, LANES)
        for copy in group_copies(group):
            copy.start()

    def last_step(group):
        by_slot = ((group + 2) * FRONT - own_first + G - 1) // G
        by_count = (own_n + G - 1) // G
        return jnp.maximum(jnp.minimum(by_slot, by_count), 1) - 1

    fetch(0, 0, True)
    zero_b[...] = jnp.zeros(zero_b.shape, bf16)
    zero_f[...] = jnp.zeros(zero_f.shape, f32)
    zeros_copy(True)
    lax.fori_loop(jnp.maximum(live_n, FRONT), slots, zero_slot, 0)
    for ref in (g_qkv, g_o, g_1, g_2t, vsum):
        ref[...] = jnp.zeros(ref.shape, f32)
    end = 0
    for d in range(n):
        at = places[d]
        loads[d].wait()
        top = 8 * first_tile(shard, d)
        if d == 0:
            flat[pl.ds(0, rows_c), :] = wbuf[at].astype(f32)
        else:
            shared = min(end - top, rows_c)
            flat[pl.ds(top, shared), :] += wbuf[at, pl.ds(0, shared), :].astype(f32)
            if shared < rows_c:
                flat[pl.ds(top + shared, rows_c - shared), :] = wbuf[at, pl.ds(shared, rows_c - shared), :].astype(f32)
        end = top + rows_c
    for ref, (row, height, width) in zip((w_qkv, w_o, w_1, w_2), MATS):
        blocks = width // LANES
        for j in range(blocks):
            ref[:, j * LANES:(j + 1) * LANES] = flat[pl.ds(row + j, height, stride=blocks), :].astype(bf16)
    for k in range(8):
        for j in range(3):
            vecs[k, j * LANES:(j + 1) * LANES] = flat[VEC_ROW + 3 * k + j, :]
    for j in range(12):
        vecs[8, j * LANES:(j + 1) * LANES] = flat[VEC_ROW + 24 + j, :]
    g_s[...] = jnp.zeros(g_s.shape, bf16)
    real = lax.broadcasted_iota(jnp.int32, (TP, LANES), 0) < TOK
    ve_s[:, :, LANES:] = jnp.broadcast_to(real.astype(f32).astype(bf16), (G * 3, TP, LANES))

    g1 = vecs[0:1, :D]
    b1 = vecs[1:2, :D]
    g2 = vecs[2:3, :D]
    b2 = vecs[3:4, :D]
    cq = vecs[4:5, :D]
    cv = vecs[5:6, :D]
    co = vecs[6:7, :D]
    c2 = vecs[7:8, :D]

    bqkv = jnp.concatenate([cq, jnp.zeros_like(cq), cv], axis=1)

    lane = lax.broadcasted_iota(jnp.int32, (1, LANES), 1)
    low_half = lane < HEAD_DIM

    def colsum(v):
        return jnp.sum(v.reshape(v.shape[0] // 8, 8, v.shape[1]), axis=0)

    def mean(v):
        return jnp.sum(v, axis=-1, keepdims=True) * (1.0 / D)

    def body(step, carry):
        slot = lax.rem(step, 2)
        fetch(step, slot, False)

        @pl.when(step + 1 < steps)
        def _():
            fetch(step + 1, 1 - slot, True)

        for i in range(G):
            live = (step * G + i < items).astype(bf16)
            x = xin[slot, i].astype(f32)
            x_s[pl.ds(i * TP, TOK), :] = x
            x_s[pl.ds(i * TP + TOK, TP - TOK), :] = jnp.broadcast_to(x[TOK - 1:], (TP - TOK, D))
            g_s[pl.ds(i * TP, TOK), :] = gin[slot, i] * live
        for r in range(0, ROWS, CH):
            rs = pl.ds(r, CH)
            v = x_s[rs, :]
            c = v - mean(v)
            inv = lax.rsqrt(mean(c * c) + norm_eps)
            nv = c * inv
            n1_s[rs, :] = nv
            r1_s[rs, :] = jnp.broadcast_to(inv, (CH, LANES))
            a1_s[rs, :] = (nv * g1 + b1).astype(bf16)
        a1 = a1_s[...]
        qkv_s[...] = (dot(a1, w_qkv[...]) + bqkv).astype(bf16)
        tail = lax.broadcasted_iota(jnp.int32, (16, 1), 0) < TOK - (TP - 16)
        pairs = [(i, p) for i in range(G) for p in range(HEADS // 2)]

        def masked_q(i, p):
            q = qkv_s[pl.ds(i * TP, TP), slice(p * LANES, (p + 1) * LANES)] * 0.125
            zero = jnp.zeros_like(q)
            return jnp.concatenate([jnp.where(low_half, q, zero), jnp.where(low_half, zero, q)], axis=0)

        def keys(i, p):
            return qkv_s[pl.ds(i * TP, TP), slice(D + p * LANES, D + (p + 1) * LANES)]

        def scores(i, p):
            return dot(masked_q(i, p), keys(i, p), 1, 1)

        s = scores(*pairs[0])
        for at, (i, p) in enumerate(pairs):
            ahead = scores(*pairs[at + 1]) if at + 1 < len(pairs) else None
            cols = slice(p * LANES, (p + 1) * LANES)
            vcols = slice(2 * D + p * LANES, 2 * D + (p + 1) * LANES)
            ve_s[at, :TP - 16, :LANES] = qkv_s[pl.ds(i * TP, TP - 16), vcols]
            last = qkv_s[pl.ds((i + 1) * TP - 16, 16), vcols]
            ve_s[at, TP - 16:, :LANES] = jnp.where(tail, last, jnp.zeros_like(last))
            e = jnp.exp(s - jnp.max(s, axis=-1, keepdims=True)).astype(bf16)
            prob_s[at] = e
            oe = dot(e, ve_s[at])
            inv = 1.0 / jnp.where(low_half, oe[:TP, LANES:], oe[TP:, LANES:])
            o = jnp.where(low_half, oe[:TP, :LANES], oe[TP:, :LANES]) * inv
            inv_s[at] = inv
            of_s[at] = o
            o_s[pl.ds(i * TP, TP), cols] = o.astype(bf16)
            s = ahead
        m_s[...] = dot(o_s[...], w_o[...])
        for r in range(0, ROWS, CH):
            rs = pl.ds(r, CH)
            v = x_s[rs, :] + m_s[rs, :] + co
            m_s[rs, :] = v
            c = v - mean(v)
            inv = lax.rsqrt(mean(c * c) + norm_eps)
            nv = c * inv
            n2_s[rs, :] = nv
            r2_s[rs, :] = jnp.broadcast_to(inv, (CH, LANES))
            a2_s[rs, :] = (nv * g2 + b2).astype(bf16)
        a2 = a2_s[...]
        gl = g_s[...]
        def hidden(j):
            fc = slice(j * FFC, (j + 1) * FFC)
            u_s[0, :, fc] = dot(a2, w_1[:, fc])
            da_s[0, :, fc] = dot(gl, w_2[fc, :], 1, 1)
        hidden(0)
        for j in range(FF // FFC):
            if (j + 1) * FFC < FF:
                hidden(j + 1)
            fc = slice(j * FFC, (j + 1) * FFC)
            c1 = vecs[8:9, fc]
            tot = None
            for r in range(0, ROWS, CH):
                rs = pl.ds(r, CH)
                u = u_s[0, rs, fc] + c1
                phi = 0.5 + 0.5 * lax.erf(u * 0.7071067811865476)
                dens = jnp.exp(u * u * -0.5) * 0.3989422804014327
                act_s[0, rs, fc] = (u * phi).astype(bf16)
                du = (da_s[0, rs, fc] * (phi + u * dens)).astype(bf16)
                du_s[0, rs, fc] = du
                part = colsum(du.astype(f32))
                tot = part if tot is None else tot + part
            vsum[8, :, fc] += tot
        dm_s[...] = dot(du_s[0], w_1[...], 1, 1)
        tg2 = tb2 = tco = tc2 = None
        for r in range(0, ROWS, CH):
            rs = pl.ds(r, CH)
            gw = g_s[rs, :].astype(f32)
            if r == 0:
                acc_s[:, :256] = dot(act_s[0], w_2[:, :256])
            if r == 6 * CH:
                acc_s[:, 256:] = dot(act_s[0], w_2[:, 256:])
            e2 = dm_s[rs, :]
            nv = n2_s[rs, :]
            en = e2 * nv
            eg = e2 * g2
            inv = r2_s[rs, :]
            inv = jnp.concatenate([inv, inv, inv], axis=1)
            dm = gw + inv * (eg - mean(eg) - nv * mean(en * g2))
            dm_s[rs, :] = dm
            db = dm.astype(bf16)
            db_s[rs, :] = db
            sums = (colsum(en), colsum(e2), colsum(db.astype(f32)), colsum(gw))
            if tg2 is None:
                tg2, tb2, tco, tc2 = sums
            else:
                tg2, tb2, tco, tc2 = tg2 + sums[0], tb2 + sums[1], tco + sums[2], tc2 + sums[3]
        vsum[2, :, :D] += tg2
        vsum[3, :, :D] += tb2
        vsum[6, :, :D] += tco
        vsum[7, :, :D] += tc2
        m_s[...] = m_s[...] + acc_s[...] + c2

        db = db_s[...]
        g_o[...] += dot(o_s[...], db, 0, 0)
        do_s[...] = dot(db, w_o[...], 1, 1).astype(bf16)
        def slopes(at):
            i, p = pairs[at]
            do = (do_s[pl.ds(i * TP, TP), slice(p * LANES, (p + 1) * LANES)].astype(f32) * inv_s[at]).astype(bf16)
            zero = jnp.zeros_like(do)
            dom = jnp.concatenate([jnp.where(low_half, do, zero), jnp.where(low_half, zero, do)], axis=0)
            t = of_s[at] * do.astype(f32) * -1.0
            hi = t.astype(bf16)
            lo = pltpu.roll(t - hi.astype(f32), HEAD_DIM, 1).astype(bf16)
            rest = jnp.concatenate([jnp.where(low_half, hi, lo), jnp.where(low_half, lo, hi)], axis=0)
            return dom, dot(jnp.concatenate([dom, rest], axis=1), ve_s[at], 1, 1)

        dom, dp = slopes(0)
        for at, (i, p) in enumerate(pairs):
            ir = pl.ds(i * TP, TP)
            fc = slice(at * 256, (at + 1) * 256)
            g_1[:, fc] += dot(a2_s[...], du_s[0, :, fc], 0, 0)
            e = prob_s[at]
            ds = (e.astype(f32) * dp).astype(bf16)
            dv = dot(dom, e, 0, 0).T
            dk = dot(masked_q(i, p), ds, 0, 0).T
            g_2t[:, fc] += dot(g_s[...], act_s[0, :, fc], 0, 0)
            dq2 = dot(ds, keys(i, p) * 0.125)
            dqkv_s[ir, slice(p * LANES, (p + 1) * LANES)] = jnp.where(low_half, dq2[:TP], dq2[TP:]).astype(bf16)
            dqkv_s[ir, slice(D + p * LANES, D + (p + 1) * LANES)] = dk.astype(bf16)
            vcols = slice(2 * D + p * LANES, 2 * D + (p + 1) * LANES)
            dqkv_s[pl.ds(i * TP, TP - 16), vcols] = dv[:TP - 16].astype(bf16)
            dqkv_s[pl.ds((i + 1) * TP - 16, 16), vcols] = jnp.where(tail, dv[TP - 16:], 0.0).astype(bf16)
            dom, dp = slopes(at + 1) if at + 1 < len(pairs) else (None, None)
        dqkv = dqkv_s[...]
        acc_s[...] = dot(dqkv, w_qkv[...], 1, 1)
        g_qkv[...] += dot(a1_s[...], dqkv, 0, 0)
        tg1 = tb1 = tcq = tcv = None
        for r in range(0, ROWS, CH):
            rs = pl.ds(r, CH)
            e1 = acc_s[rs, :]
            nv = n1_s[rs, :]
            en = e1 * nv
            eg = e1 * g1
            inv = r1_s[rs, :]
            inv = jnp.concatenate([inv, inv, inv], axis=1)
            dm_s[rs, :] += inv * (eg - mean(eg) - nv * mean(en * g1))
            sums = (colsum(en), colsum(e1), colsum(dqkv_s[rs, :D].astype(f32)), colsum(dqkv_s[rs, 2 * D:].astype(f32)))
            if tg1 is None:
                tg1, tb1, tcq, tcv = sums
            else:
                tg1, tb1, tcq, tcv = tg1 + sums[0], tb1 + sums[1], tcq + sums[2], tcv + sums[3]
        vsum[0, :, :D] += tg1
        vsum[1, :, :D] += tb1
        vsum[4, :, :D] += tcq
        vsum[5, :, :D] += tcv

        @pl.when(step >= 2)
        def _():
            flush(step - 2, slot, False)

        keep(step, slot, m_s, wide_o, oout)
        keep(step, slot, dm_s, wide_g, gout)
        flush(step, slot, True)
        for group in range(groups):
            @pl.when(step == last_step(group))
            def _():
                group_leaves(group)
        return carry

    lax.fori_loop(0, steps, body, 0)

    ends_copies = []
    for ref, (row, height, width) in zip((g_qkv, g_o, g_1), MATS):
        blocks = width // LANES
        for j in range(blocks):
            flat[pl.ds(row + j, height, stride=blocks), :] = ref[:, j * LANES:(j + 1) * LANES]
    row = MATS[3][0]
    for c in range(FF // LANES):
        t = g_2t[:, c * LANES:(c + 1) * LANES].T
        for j in range(3):
            flat[pl.ds(row + 3 * LANES * c + j, LANES, stride=3), :] = t[:, j * LANES:(j + 1) * LANES]
    for k in range(9):
        t = jnp.sum(vsum[k], axis=0, keepdims=True)
        for j in range(12 if k == 8 else 3):
            flat[pl.ds(VEC_ROW + 3 * k + j, 1), :] = t[:, j * LANES:(j + 1) * LANES]
    flat[pl.ds(FLAT_ROWS, flat.shape[0] - FLAT_ROWS), :] = jnp.zeros((flat.shape[0] - FLAT_ROWS, LANES), f32)
    for d in range(n):
        wbuf[places[d]] = flat[pl.ds(8 * first_tile(shard, d), rows_c), :].astype(bf16)
        copy = pltpu.make_async_copy(wbuf.at[places[d]], gbuf_h.at[places[d]], w_sem.at[d])
        copy.start()
        ends_copies.append(copy)

    @pl.when(steps >= 2)
    def _():
        flush(steps - 2, lax.rem(steps, 2), False)
    flush(steps - 1, lax.rem(steps + 1, 2), False)
    zeros_copy(False)
    for group in range(groups):
        ends_copies.extend(group_copies(group))
    for copy in ends_copies:
        copy.wait()


def flat_height(n, shard):
    return 8 * first_tile(shard, n - 1) + chunk_rows(shard)


def block_call(n, shard, cap, ends, other, images, cot, p_images, p_cot, wbuf):
    slots = images.shape[0]
    anyspace = pl.BlockSpec(memory_space=pl.ANY)
    rows_c = chunk_rows(shard)
    groups = slots // FRONT - 1
    scratch = [
        pltpu.VMEM((flat_height(n, shard), LANES), f32),
        pltpu.VMEM((D, 3 * D), bf16), pltpu.VMEM((D, D), bf16), pltpu.VMEM((D, FF), bf16), pltpu.VMEM((FF, D), bf16),
        pltpu.VMEM((16, FF), f32),
        pltpu.VMEM((D, 3 * D), f32), pltpu.VMEM((D, D), f32), pltpu.VMEM((D, FF), f32), pltpu.VMEM((D, FF), f32),
        pltpu.VMEM((9, 8, FF), f32),
        pltpu.VMEM((2, G, TOK, D), bf16), pltpu.VMEM((2, G, TOK, D), bf16),
        pltpu.VMEM((2, G, TOK, D), bf16), pltpu.VMEM((2, G, TOK, D), f32),
        pltpu.VMEM((ROWS, D), f32),
        pltpu.VMEM((ROWS, D), f32), pltpu.VMEM((ROWS, LANES), f32), pltpu.VMEM((ROWS, D), bf16),
        pltpu.VMEM((ROWS, 3 * D), bf16),
        pltpu.VMEM((G * 3, 2 * TP, TP), bf16), pltpu.VMEM((G * 3, TP, 2 * LANES), bf16),
        pltpu.VMEM((G * 3, TP, LANES), f32), pltpu.VMEM((G * 3, TP, LANES), f32),
        pltpu.VMEM((ROWS, D), bf16),
        pltpu.VMEM((ROWS, D), f32),
        pltpu.VMEM((ROWS, D), f32), pltpu.VMEM((ROWS, LANES), f32), pltpu.VMEM((ROWS, D), bf16),
        pltpu.VMEM((ROWS, D), bf16),
        pltpu.VMEM((1, ROWS, FF), f32), pltpu.VMEM((1, ROWS, FF), bf16), pltpu.VMEM((1, ROWS, FF), bf16),
        pltpu.VMEM((ROWS, D), f32),
        pltpu.VMEM((1, ROWS, FF), f32),
        pltpu.VMEM((ROWS, D), f32), pltpu.VMEM((ROWS, D), bf16), pltpu.VMEM((ROWS, D), bf16),
        pltpu.VMEM((ROWS, 3 * D), bf16),
        pltpu.VMEM((TOK, D), bf16), pltpu.VMEM((TOK, D), f32),
        pltpu.VMEM((n, rows_c, LANES), bf16),
        pltpu.VMEM((groups, D // LANES, TOK * FRONT, LANES), f32), pltpu.VMEM((groups, D // LANES, TOK * FRONT, LANES), f32),
        pltpu.VMEM((groups, D // LANES, TOK, FRONT, LANES), bf16),
        pltpu.SemaphoreType.DMA((2, G, 2)), pltpu.SemaphoreType.DMA((2, G, 2)), pltpu.SemaphoreType.DMA((2,)),
        pltpu.SemaphoreType.DMA((n,)), pltpu.SemaphoreType.DMA((groups, 2, D // LANES)),
    ]
    return pl.pallas_call(
        functools.partial(compute_kernel, n, shard, cap, slots),
        name="block",
        out_shape=(
            jax.ShapeDtypeStruct((TOK, slots, D), bf16),
            jax.ShapeDtypeStruct((TOK, slots, D), f32),
            jax.ShapeDtypeStruct((FRONT, TOK, D), bf16),
            jax.ShapeDtypeStruct((FRONT, TOK, D), f32),
            jax.ShapeDtypeStruct((cap,) + images.shape[1:], bf16),
            jax.ShapeDtypeStruct((cap,) + images.shape[1:], f32),
            jax.ShapeDtypeStruct((n, rows_c, LANES), bf16),
        ),
        in_specs=[pl.BlockSpec(memory_space=pltpu.SMEM), pl.BlockSpec(memory_space=pltpu.SMEM)] + [anyspace] * 5,
        out_specs=(anyspace,) * 7,
        scratch_shapes=scratch,
        compiler_params=pltpu.CompilerParams(vmem_limit_bytes=VMEM_LIMIT),
    )(ends, other, images, cot, p_images, p_cot, wbuf)


def chip_axes(n):
    chips = n // 2
    if chips % 16 == 0:
        rest = chips // 4
        side = 2 if rest == 4 else 4
        return (4, rest // side, side)
    return (chips, 1, 1)


class Place:
    def __init__(self, n):
        self.size = chip_axes(n)
        self.stride = (self.size[1] * self.size[2] * 2, self.size[2] * 2, 2)
        self.me = lax.axis_index("dp")
        self.core = lax.rem(self.me, 2)
        self.at = [lax.rem(self.me // self.stride[k], self.size[k]) for k in range(3)]

    def peer(self, axis, hop):
        to = lax.rem(self.at[axis] + hop, self.size[axis])
        return self.me + (to - self.at[axis]) * self.stride[axis]

    def partner(self):
        return self.me + 1 - 2 * self.core

    def slot(self, core, a, b, c):
        return ((core * self.size[1] + b) * self.size[2] + c) * self.size[0] + a

    def everyone(self):
        return [self.peer(k, h) for k in range(3) for h in range(1, self.size[k])] + [self.partner()]


def chunk_places(n):
    A, B, C = chip_axes(n)
    order = [((a * B + b) * C + c) * 2 + core for core in range(2) for b in range(B) for c in range(C) for a in range(A)]
    return [order.index(d) for d in range(n)]


def greet(place):
    barrier = pltpu.get_barrier_semaphore()
    everyone = place.everyone()
    for other in everyone:
        pl.semaphore_signal(barrier, inc=1, device_id=(other,), device_id_type=pl.DeviceIdType.MESH)
    pl.semaphore_wait(barrier, len(everyone))


class Sender:
    def __init__(self, send_sem, recv_sem):
        self.send_sem, self.recv_sem, self.all = send_sem, recv_sem, []

    def go(self, src, dst, device):
        k = len(self.all)
        copy = pltpu.make_async_remote_copy(
            src_ref=src, dst_ref=dst, send_sem=self.send_sem.at[k], recv_sem=self.recv_sem.at[k],
            device_id=(device,), device_id_type=pl.DeviceIdType.MESH)
        copy.start()
        self.all.append([copy, False])
        return copy

    def sent(self, copies):
        for entry in self.all:
            if any(entry[0] is copy for copy in copies) and not entry[1]:
                entry[0].wait_send()
                entry[1] = True

    def finish(self):
        self.sent([entry[0] for entry in self.all])


def arrive(copies):
    for copy in copies:
        copy.wait_recv()


def row_parts(rows, parts):
    tiles = rows // 16
    parts = min(parts, tiles)
    cuts = [tiles * k // parts * 16 for k in range(parts + 1)]
    return [(cuts[k], cuts[k + 1] - cuts[k]) for k in range(parts)]


PARTS = 4
SCATTER_SHARES = (7, 7, 7, 7)


def row_shares(rows, shares):
    tiles = rows // 16
    ends = [tiles * sum(shares[:k]) // sum(shares) * 16 for k in range(len(shares) + 1)]
    return [(ends[k], ends[k + 1] - ends[k]) for k in range(len(shares)) if ends[k + 1] > ends[k]]


SEMS = 192


def gather_kernel(n, cap, chunk, count, images, cot, wbuf_h, other, images_r, cot_r, p_images, p_cot,
                  wbuf, xin, wide, relay, send_sem, recv_sem, in_sem, out_sem, w_sem):
    place = Place(n)
    A, B, C = place.size
    a, b, c = place.at
    core = place.core
    loads = [pltpu.make_async_copy(src, xin.at[k], in_sem.at[k]) for k, src in enumerate((images, cot))]
    for copy in loads:
        copy.start()
    mine = place.slot(core, a, b, c)
    wbuf[mine] = chunk[...].astype(bf16)
    greet(place)
    sender = Sender(send_sem, recv_sem)
    parts = row_parts(chunk.shape[0], PARTS)
    last = len(parts) - 1
    slots = images.shape[1]
    toks = images.shape[0]

    def run(start, length, part):
        return wbuf.at[pl.ds(start, length), pl.ds(part[0], part[1]), :]

    def spread(axis, runs, part):
        return [sender.go(run(s, l, part), run(s, l, part), place.peer(axis, hop))
                for hop in range(1, place.size[axis]) for s, l in runs]

    def pass_on(runs, part):
        return [sender.go(run(s, l, part), run(s, l, part), place.partner()) for s, l in runs]

    def widen(k, t, m):
        v = xin[k, pl.ds(t, m)].reshape(m * slots, D).astype(f32)
        for j in range(D // LANES):
            wide[k, j, pl.ds(t * slots, m * slots), :] = v[:, j * LANES:(j + 1) * LANES]

    def one_slot(k, s, carry):
        for j in range(D // LANES):
            relay[k, s, :, j * LANES:(j + 1) * LANES] = wide[k, j, pl.ds(s, toks, stride=slots), :].astype(bf16)
        return carry

    def chores():
        for k in range(2):
            loads[k].wait()
            for t in range(0, toks, 100):
                widen(k, t, min(100, toks - t))
                yield
            step = -(-slots // 4)
            for s in range(0, slots, step):
                lax.fori_loop(s, min(s + step, slots), functools.partial(one_slot, k), 0)
                yield
            pair.append(sender.go(relay.at[k, pl.ds(0, cap)], (p_images, p_cot)[k], place.partner()))
            stores.append(pltpu.make_async_copy(relay.at[k], (images_r, cot_r)[k], out_sem.at[k]))
            stores[-1].start()
        while True:
            yield

    one, two, three, stores = {}, {}, {}, []
    forwards = [[] for _ in parts]
    one[0] = spread(0, [(mine, 1)], parts[0])
    pair = [sender.go(count, other, place.partner())]

    def second(k):
        arrive(one[k])
        runs = [(place.slot(core, 0, b, c), A)]
        two[k] = spread(2 if k % 2 == 0 else 1, runs, parts[k])
        forwards[k].extend(pass_on(runs, parts[k]))

    def third(k):
        arrive(two[k])
        if k % 2 == 0:
            runs = [(place.slot(core, 0, b, 0), C * A)]
            others = [(place.slot(core, 0, b, lax.rem(c + h, C)), A) for h in range(1, C)]
        else:
            runs = [(place.slot(core, 0, y, c), A) for y in range(B)]
            others = [(place.slot(core, 0, lax.rem(b + h, B), c), A) for h in range(1, B)]
        three[k] = spread(1 if k % 2 == 0 else 2, runs, parts[k])
        forwards[k].extend(pass_on(others, parts[k]))

    def ending(k):
        arrive(three[k])
        if k % 2 == 0:
            others = [(place.slot(core, 0, lax.rem(b + h, B), 0), C * A) for h in range(1, B)]
        else:
            others = [(place.slot(core, 0, y, lax.rem(c + h, C)), A) for h in range(1, C) for y in range(B)]
        forwards[k].extend(pass_on(others, parts[k]))

    chore = chores()
    next(chore)
    for k in range(len(parts)):
        sender.sent(one[k])
        if k < last:
            one[k + 1] = spread(0, [(mine, 1)], parts[k + 1])
        second(k)
        next(chore)
        if k >= 1:
            third(k - 1)
        next(chore)
    third(last)
    for _ in range(4):
        next(chore)
    for k in range(len(parts)):
        ending(k)
    for k, part in enumerate(parts):
        arrive(forwards[k])
        stores.append(pltpu.make_async_copy(wbuf.at[:, pl.ds(*part), :], wbuf_h.at[:, pl.ds(*part), :], w_sem.at[k]))
        stores[-1].start()
    arrive(pair)
    sender.finish()
    for copy in stores:
        copy.wait()


def gather_call(n, cap, chunk, count, images, cot):
    toks, slots, _ = images.shape
    anyspace = pl.BlockSpec(memory_space=pl.ANY)
    vm = pl.BlockSpec(memory_space=pltpu.VMEM)
    return pl.pallas_call(
        functools.partial(gather_kernel, n, cap),
        name="gather",
        out_shape=(
            jax.ShapeDtypeStruct((n,) + chunk.shape, bf16), jax.ShapeDtypeStruct(count.shape, jnp.int32),
            jax.ShapeDtypeStruct((slots, toks, D), bf16), jax.ShapeDtypeStruct((slots, toks, D), bf16),
            jax.ShapeDtypeStruct((cap, toks, D), bf16), jax.ShapeDtypeStruct((cap, toks, D), bf16),
        ),
        in_specs=[vm, vm, anyspace, anyspace],
        out_specs=(anyspace, vm, anyspace, anyspace, anyspace, anyspace),
        scratch_shapes=[
            pltpu.VMEM((n,) + chunk.shape, bf16),
            pltpu.VMEM((2, toks, slots, D), bf16), pltpu.VMEM((2, D // LANES, toks * slots, LANES), f32), pltpu.VMEM((2, slots, toks, D), bf16),
            pltpu.SemaphoreType.DMA((SEMS,)), pltpu.SemaphoreType.DMA((SEMS,)),
            pltpu.SemaphoreType.DMA((2,)), pltpu.SemaphoreType.DMA((2,)), pltpu.SemaphoreType.DMA((PARTS,)),
        ],
        compiler_params=pltpu.CompilerParams(collective_id=0, has_side_effects=True, vmem_limit_bytes=VMEM_LIMIT),
    )(chunk, count, images, cot)


def scatter_kernel(n, cap, gbuf, ends, other, p_out, p_grad, f_out, f_grad, total, out_h, grad_h,
                   half, got0, got1, got2, got3, r_out, r_grad, own_out, own_grad, wide, out_f, grad_f,
                   send_sem, recv_sem, in_sem, half_sem, out_sem):
    place = Place(n)
    A, B, C = place.size
    a, b, c = place.at
    core = place.core
    slots, toks, _ = f_out.shape
    loads = [pltpu.make_async_copy(src, dst, in_sem.at[k])
             for k, (src, dst) in enumerate(((f_out, own_out), (f_grad, own_grad)))]
    for copy in loads:
        copy.start()
    greet(place)
    sender = Sender(send_sem, recv_sem)
    parts = row_shares(gbuf.shape[1], SCATTER_SHARES)
    last = len(parts) - 1
    chips = n // 2
    halves = [pltpu.make_async_copy(gbuf.at[pl.ds(core * chips, chips), pl.ds(*part), :], half.at[:, pl.ds(*part), :], half_sem.at[k])
              for k, part in enumerate(parts)]
    zero = [sender.go(gbuf.at[pl.ds((1 - core) * chips, chips), pl.ds(*part), :], got0.at[:, pl.ds(*part), :], place.partner())
            for part in parts]
    back = [sender.go(p_out, r_out, place.partner()), sender.go(p_grad, r_grad, place.partner())]
    for copy in halves:
        copy.start()
    given = jnp.maximum(ends[0, MB - 1] - other[0, MB - 1], 0) // 2
    stores = []

    def shared(own, sent, k, s, carry):
        for j in range(D // LANES):
            cols = slice(j * LANES, (j + 1) * LANES)
            v = jnp.where(s < given, sent[s, :, cols], own[s, :, cols])
            wide[k, j, pl.ds(s, toks, stride=slots), :] = v.astype(f32)
        return carry

    def single(own, k, s, carry):
        for j in range(D // LANES):
            wide[k, j, pl.ds(s, toks, stride=slots), :] = own[s, :, j * LANES:(j + 1) * LANES].astype(f32)
        return carry

    def chores():
        for k, (own, sent, dst, home) in enumerate(((own_out, r_out, out_f, out_h), (own_grad, r_grad, grad_f, grad_h))):
            loads[k].wait()
            arrive(back[k:k + 1])
            lax.fori_loop(0, cap, functools.partial(shared, own, sent, k), 0)
            yield
            lax.fori_loop(cap, slots, functools.partial(single, own, k), 0)
            for j in range(D // LANES):
                dst[:, j * LANES:(j + 1) * LANES] = wide[k, j].astype(dst.dtype)
            stores.append(pltpu.make_async_copy(dst, home, out_sem.at[k]))
            stores[-1].start()
            yield
        while True:
            yield

    def rows(ref, start, length, part):
        return ref.at[pl.ds(start, length), pl.ds(*part), :]

    def slot(bb, cc):
        return (bb * C + cc) * A

    one, two, three = {}, {}, {}

    def first(k):
        arrive([zero[k]])
        halves[k].wait()
        part = parts[k]
        pr = pl.ds(*part)

        def add(i, carry):
            half[i, pr, :] = (half[i, pr, :].astype(f32) + got0[i, pr, :].astype(f32)).astype(bf16)
            return carry
        lax.fori_loop(0, chips, add, 0)
        sent = []
        if k % 2 == 0:
            for h in range(1, B):
                to = lax.rem(b + h, B)
                sent.append(sender.go(rows(half, slot(to, 0), C * A, part), rows(got1, (h - 1) * C * A, C * A, part), place.peer(1, h)))
        else:
            for h in range(1, C):
                to = lax.rem(c + h, C)
                for y in range(B):
                    sent.append(sender.go(rows(half, slot(y, to), A, part), rows(got1, ((h - 1) * B + y) * A, A, part), place.peer(2, h)))
        one[k] = sent

    def second(k):
        arrive(one[k])
        part = parts[k]
        pr = pl.ds(*part)
        sent = []
        if k % 2 == 0:
            def add(i, carry):
                v = half[slot(b, 0) + i, pr, :].astype(f32)
                for h in range(1, B):
                    v = v + got1[(h - 1) * C * A + i, pr, :].astype(f32)
                half[slot(b, 0) + i, pr, :] = v.astype(bf16)
                return carry
            lax.fori_loop(0, C * A, add, 0)
            for h in range(1, C):
                to = lax.rem(c + h, C)
                sent.append(sender.go(rows(half, slot(b, to), A, part), rows(got2, (h - 1) * A, A, part), place.peer(2, h)))
        else:
            def add(i, carry):
                y = i // A
                z = lax.rem(i, A)
                v = half[slot(y, c) + z, pr, :].astype(f32)
                for h in range(1, C):
                    v = v + got1[((h - 1) * B + y) * A + z, pr, :].astype(f32)
                half[slot(y, c) + z, pr, :] = v.astype(bf16)
                return carry
            lax.fori_loop(0, B * A, add, 0)
            for h in range(1, B):
                to = lax.rem(b + h, B)
                sent.append(sender.go(rows(half, slot(to, c), A, part), rows(got2, (h - 1) * A, A, part), place.peer(1, h)))
        two[k] = sent

    def third(k):
        arrive(two[k])
        part = parts[k]
        pr = pl.ds(*part)
        others = (C if k % 2 == 0 else B) - 1

        def add(i, carry):
            v = half[slot(b, c) + i, pr, :].astype(f32)
            for h in range(others):
                v = v + got2[h * A + i, pr, :].astype(f32)
            half[slot(b, c) + i, pr, :] = v.astype(bf16)
            return carry
        lax.fori_loop(0, A, add, 0)
        sent = []
        for h in range(1, A):
            to = lax.rem(a + h, A)
            sent.append(sender.go(rows(half, slot(b, c) + to, 1, part), rows(got3, h - 1, 1, part), place.peer(0, h)))
        three[k] = sent

    def ending(k):
        arrive(three[k])
        pr = pl.ds(*parts[k])
        v = half[slot(b, c) + a, pr, :].astype(f32)
        for h in range(A - 1):
            v = v + got3[h, pr, :].astype(f32)
        total[pr, :] = v

    chore = chores()
    first(0)
    first(1)
    next(chore)
    for k in range(0, len(parts), 2):
        pair = [j for j in (k, k + 1) if j <= last]
        nxt = [j for j in (k + 2, k + 3) if j <= last]
        for j in pair:
            second(j)
            next(chore)
        for j in nxt:
            first(j)
        next(chore)
        for j in pair:
            third(j)
            next(chore)
    for k in range(len(parts)):
        ending(k)
        if k == 0:
            for _ in range(3):
                next(chore)
    sender.finish()
    for copy in stores:
        copy.wait()


def scatter_call(n, cap, gbuf, ends, other, p_out, p_grad, f_out, f_grad):
    A, B, C = chip_axes(n)
    rows_c = gbuf.shape[1]
    slots, toks, _ = f_out.shape
    anyspace = pl.BlockSpec(memory_space=pl.ANY)
    vm = pl.BlockSpec(memory_space=pltpu.VMEM)
    sm = pl.BlockSpec(memory_space=pltpu.SMEM)
    big = max((B - 1) * C * A, (C - 1) * B * A)
    return pl.pallas_call(
        functools.partial(scatter_kernel, n, cap),
        name="scatter",
        out_shape=(jax.ShapeDtypeStruct((rows_c, LANES), f32), jax.ShapeDtypeStruct((toks * slots, D), bf16),
                   jax.ShapeDtypeStruct((toks * slots, D), f32)),
        in_specs=[anyspace, sm, sm, anyspace, anyspace, anyspace, anyspace],
        out_specs=(vm, anyspace, anyspace),
        scratch_shapes=[
            pltpu.VMEM((n // 2, rows_c, LANES), bf16), pltpu.VMEM((n // 2, rows_c, LANES), bf16),
            pltpu.VMEM((big, rows_c, LANES), bf16), pltpu.VMEM((max(B, C) * A, rows_c, LANES), bf16),
            pltpu.VMEM((A, rows_c, LANES), bf16),
            pltpu.VMEM((cap, toks, D), bf16), pltpu.VMEM((cap, toks, D), f32),
            pltpu.VMEM((slots, toks, D), bf16), pltpu.VMEM((slots, toks, D), f32),
            pltpu.VMEM((2, D // LANES, toks * slots, LANES), f32),
            pltpu.VMEM((toks * slots, D), bf16), pltpu.VMEM((toks * slots, D), f32),
            pltpu.SemaphoreType.DMA((SEMS,)), pltpu.SemaphoreType.DMA((SEMS,)),
            pltpu.SemaphoreType.DMA((2,)), pltpu.SemaphoreType.DMA((PARTS,)), pltpu.SemaphoreType.DMA((2,)),
        ],
        compiler_params=pltpu.CompilerParams(collective_id=1, has_side_effects=True, vmem_limit_bytes=VMEM_LIMIT),
    )(gbuf, ends, other, p_out, p_grad, f_out, f_grad)


def pack_shard(n, shard, values):
    me = lax.axis_index("dp")
    offset = lax.rem(shard * me, TILE)
    size = chunk_rows(shard) * LANES
    padded = jnp.pad(values, (TILE, size - shard))
    return lax.dynamic_slice_in_dim(padded, TILE - offset, size, 0).reshape(chunk_rows(shard), LANES)


def unpack_shard(n, shard, chunk):
    me = lax.axis_index("dp")
    offset = lax.rem(shard * me, TILE)
    return lax.dynamic_slice_in_dim(chunk.reshape(-1), offset, shard, 0)


CUTS = 4


def front_kernel(out_in, grad_in, out_f, grad_f, out_t, grad_t, out_v, grad_v, in_sem, out_sem):
    toks = out_f.shape[0]
    step = -(-toks // CUTS)
    moves = []
    for q in range(CUTS):
        rows = pl.ds(q * step, min(step, toks - q * step))
        for k, (src, mid, dst) in enumerate(((grad_f, grad_v, grad_t), (out_f, out_v, out_t))):
            moves.append((pltpu.make_async_copy(src.at[rows], mid.at[rows], in_sem.at[k, q]),
                          pltpu.make_async_copy(mid.at[rows], dst.at[rows, pl.ds(0, FRONT), :], out_sem.at[k, q])))
    for load, _ in moves:
        load.start()
    for load, store in moves:
        load.wait()
        store.start()
    for _, store in moves:
        store.wait()


def front_call(out_t, grad_t, out_f, grad_f):
    anyspace = pl.BlockSpec(memory_space=pl.ANY)
    return pl.pallas_call(
        front_kernel,
        name="front",
        out_shape=tuple(jax.ShapeDtypeStruct(v.shape, v.dtype) for v in (out_t, grad_t)),
        in_specs=[anyspace] * 4,
        out_specs=(anyspace, anyspace),
        scratch_shapes=[pltpu.VMEM(out_f.shape, bf16), pltpu.VMEM(grad_f.shape, f32),
                        pltpu.SemaphoreType.DMA((2, CUTS)), pltpu.SemaphoreType.DMA((2, CUTS))],
        input_output_aliases={0: 0, 1: 1},
        compiler_params=pltpu.CompilerParams(vmem_limit_bytes=VMEM_LIMIT),
    )(out_t, grad_t, out_f, grad_f)


def body(n, images, cotangent, master, moment_one, moment_two, batch_ends):
    shard = master.shape[0]
    cap = CAP
    slots, toks, _ = images.shape
    chunk = pack_shard(n, shard, master)
    wbuf, other, images_r, cot_r, p_images, p_cot = gather_call(
        n, cap, chunk, batch_ends, images.transpose(1, 0, 2), cotangent.transpose(1, 0, 2))
    out_t, grad_t, f_out, f_grad, p_out, p_grad, gbuf = block_call(
        n, shard, cap, batch_ends, other, images_r, cot_r, p_images, p_cot, wbuf)
    part, out_f, grad_f = scatter_call(n, cap, gbuf, batch_ends, other, p_out, p_grad, f_out, f_grad)
    out_t, grad_t = front_call(out_t, grad_t, out_f.reshape(toks, FRONT, D), grad_f.reshape(toks, FRONT, D))
    block_out = out_t.transpose(1, 0, 2)
    input_grad = grad_t.transpose(1, 0, 2)
    weight_grad = unpack_shard(n, shard, part)
    first_moment = beta_one * moment_one + (1.0 - beta_one) * weight_grad
    second_moment = beta_two * moment_two + (1.0 - beta_two) * weight_grad * weight_grad
    corrected_one = first_moment / (1.0 - beta_one**STEP)
    corrected_two = second_moment / (1.0 - beta_two**STEP)
    update = -learn_rate * (
        corrected_one / (jnp.sqrt(corrected_two) + adam_eps) + decay_rate * master
    )
    return (block_out, input_grad, weight_grad, first_moment, second_moment, update)


def solution(mesh):
    n = mesh.shape["dp"]
    return jax.shard_map(
        functools.partial(body, n),
        mesh=mesh,
        in_specs=(P("dp", None, None), P("dp", None, None), P("dp"), P("dp"), P("dp"), P("dp", None)),
        out_specs=(P("dp", None, None), P("dp", None, None), P("dp"), P("dp"), P("dp"), P("dp")),
        check_vma=False,
    )
```

```python
import jax, jax.numpy as jnp, functools
from jax import lax
from jax.experimental import pallas as pl
from jax.experimental.pallas import tpu as pltpu
from jax.sharding import PartitionSpec as P

D = 384
FF = 1536
HEADS = 6
HEAD_DIM = 64
TOK = 197
TP = 208
G = 2
ROWS = G * TP
MB = 3
STEP = 10
CAP = 6
FRONT = 8
CH = 32
FFC = 256

beta_one = 0.9
beta_two = 0.999
learn_rate = 0.01
decay_rate = 0.05
adam_eps = 1e-08
norm_eps = 1e-06
f32 = jnp.float32
bf16 = jnp.bfloat16

LANES = 128
TILE = 8 * LANES
MATS = ((0, D, 3 * D), (3456, D, D), (4608, D, FF), (9216, FF, D))
VEC_ROW = 13824
FLAT_ROWS = 13860
VMEM_LIMIT = 60 * 2**20


def dot(a, b, ca=1, cb=0):
    return lax.dot_general(a, b, (((ca,), (cb,)), ((), ())), preferred_element_type=f32)


def chunk_rows(shard):
    return ((shard + TILE - 1 + LANES - 1) // LANES + 15) // 16 * 16


def first_tile(shard, d):
    return (shard * d) // TILE


def compute_kernel(n, shard, cap, slots, ends, other, images, cot, p_images, p_cot, wbuf_h,
                   out_t, grad_t, f_out, f_grad, p_out, p_grad, gbuf_h,
                   flat, w_qkv, w_o, w_1, w_2, vecs, g_qkv, g_o, g_1, g_2t, vsum,
                   xin, gin, oout, gout, x_s, n1_s, r1_s, a1_s, qkv_s, prob_s, ve_s, inv_s, of_s, o_s, m_s, n2_s, r2_s, a2_s,
                   g_s, u_s, act_s, du_s, acc_s, da_s, dm_s, db_s, do_s, dqkv_s, zero_b, zero_f, wbuf, wide_o, wide_g, out16,
                   in_sem, out_sem, zero_sem, w_sem, end_sem):
    places = chunk_places(n)
    loads = [pltpu.make_async_copy(wbuf_h.at[places[d]], wbuf.at[places[d]], w_sem.at[d]) for d in range(n)]
    for copy in loads:
        copy.start()
    rows_c = wbuf.shape[1]
    live_n = ends[0, MB - 1]
    diff = live_n - other[0, MB - 1]
    own_first = jnp.clip(diff // 2, 0, cap)
    own_n = live_n - own_first
    part_n = jnp.clip((0 - diff) // 2, 0, cap)
    groups = slots // FRONT - 1
    items = own_n + part_n
    steps = (items + G - 1) // G

    def fetch(step, slot, do):
        for i in range(G):
            item = jnp.minimum(step * G + i, items - 1)
            is_own = item < own_n

            @pl.when(is_own)
            def _():
                s = own_first + item
                for k, (src, dst) in enumerate(((images, xin), (cot, gin))):
                    c = pltpu.make_async_copy(src.at[s], dst.at[slot, i], in_sem.at[slot, i, k])
                    c.start() if do else c.wait()

            @pl.when(jnp.logical_not(is_own))
            def _():
                s = item - own_n
                for k, (src, dst) in enumerate(((p_images, xin), (p_cot, gin))):
                    c = pltpu.make_async_copy(src.at[s], dst.at[slot, i], in_sem.at[slot, i, k])
                    c.start() if do else c.wait()

    def flush(step, slot, do):
        for i in range(G):
            item = step * G + i
            is_own = item < own_n
            s_own = own_first + item

            @pl.when(jnp.logical_and(is_own, s_own < FRONT))
            def _():
                for k, (dst, src) in enumerate(((f_out, oout), (f_grad, gout))):
                    c = pltpu.make_async_copy(src.at[slot, i], dst.at[s_own], out_sem.at[slot, i, k])
                    c.start() if do else c.wait()

            @pl.when(jnp.logical_and(jnp.logical_not(is_own), item < items))
            def _():
                s = item - own_n
                for k, (dst, src) in enumerate(((p_out, oout), (p_grad, gout))):
                    c = pltpu.make_async_copy(src.at[slot, i], dst.at[s], out_sem.at[slot, i, k])
                    c.start() if do else c.wait()

    def keep(step, slot, ref, wide, staged):
        for i in range(G):
            item = step * G + i
            s_own = own_first + item
            far = jnp.logical_and(item < own_n, s_own >= FRONT)

            @pl.when(far)
            def _():
                group = s_own // FRONT - 1
                for j in range(D // LANES):
                    wide[group, j, pl.ds(lax.rem(s_own, FRONT), TOK, stride=FRONT), :] = ref[pl.ds(i * TP, TOK), j * LANES:(j + 1) * LANES]

            @pl.when(jnp.logical_not(far))
            def _():
                staged[slot, i] = ref[pl.ds(i * TP, TOK), :].astype(staged.dtype)

    def zeros_copy(do):
        def one(s, carry):
            a = pltpu.make_async_copy(zero_b, f_out.at[s], zero_sem.at[0])
            b = pltpu.make_async_copy(zero_f, f_grad.at[s], zero_sem.at[1])
            a.start() if do else a.wait()
            b.start() if do else b.wait()
            return carry
        lax.fori_loop(jnp.minimum(live_n, FRONT), FRONT, one, 0)

    def zero_slot(s, carry):
        for j in range(D // LANES):
            for ref in (wide_o, wide_g):
                ref[s // FRONT - 1, j, pl.ds(lax.rem(s, FRONT), TOK, stride=FRONT), :] = jnp.zeros((TOK, LANES), f32)
        return carry

    def group_copies(group):
        first = (group + 1) * FRONT
        copies = []
        for j in range(D // LANES):
            cols = slice(j * LANES, (j + 1) * LANES)
            copies.append(pltpu.make_async_copy(
                wide_g.at[group, j].reshape(TOK, FRONT, LANES), grad_t.at[:, pl.ds(first, FRONT), cols], end_sem.at[group, 0, j]))
            copies.append(pltpu.make_async_copy(out16.at[group, j], out_t.at[:, pl.ds(first, FRONT), cols], end_sem.at[group, 1, j]))
        return copies

    def group_leaves(group):
        for j in range(D // LANES):
            out16[group, j] = wide_o[group, j].astype(bf16).reshape(TOK, FRONT, LANES)
        for copy in group_copies(group):
            copy.start()

    def last_step(group):
        by_slot = ((group + 2) * FRONT - own_first + G - 1) // G
        by_count = (own_n + G - 1) // G
        return jnp.maximum(jnp.minimum(by_slot, by_count), 1) - 1

    fetch(0, 0, True)
    zero_b[...] = jnp.zeros(zero_b.shape, bf16)
    zero_f[...] = jnp.zeros(zero_f.shape, f32)
    zeros_copy(True)
    lax.fori_loop(jnp.maximum(live_n, FRONT), slots, zero_slot, 0)
    for ref in (g_qkv, g_o, g_1, g_2t, vsum):
        ref[...] = jnp.zeros(ref.shape, f32)
    end = 0
    for d in range(n):
        at = places[d]
        loads[d].wait()
        top = 8 * first_tile(shard, d)
        if d == 0:
            flat[pl.ds(0, rows_c), :] = wbuf[at].astype(f32)
        else:
            shared = min(end - top, rows_c)
            flat[pl.ds(top, shared), :] += wbuf[at, pl.ds(0, shared), :].astype(f32)
            if shared < rows_c:
                flat[pl.ds(top + shared, rows_c - shared), :] = wbuf[at, pl.ds(shared, rows_c - shared), :].astype(f32)
        end = top + rows_c
    for ref, (row, height, width) in zip((w_qkv, w_o, w_1, w_2), MATS):
        blocks = width // LANES
        for j in range(blocks):
            ref[:, j * LANES:(j + 1) * LANES] = flat[pl.ds(row + j, height, stride=blocks), :].astype(bf16)
    for k in range(8):
        for j in range(3):
            vecs[k, j * LANES:(j + 1) * LANES] = flat[VEC_ROW + 3 * k + j, :]
    for j in range(12):
        vecs[8, j * LANES:(j + 1) * LANES] = flat[VEC_ROW + 24 + j, :]
    g_s[...] = jnp.zeros(g_s.shape, bf16)
    real = lax.broadcasted_iota(jnp.int32, (TP, LANES), 0) < TOK
    ve_s[:, :, LANES:] = jnp.broadcast_to(real.astype(f32).astype(bf16), (G * 3, TP, LANES))

    g1 = vecs[0:1, :D]
    b1 = vecs[1:2, :D]
    g2 = vecs[2:3, :D]
    b2 = vecs[3:4, :D]
    cq = vecs[4:5, :D]
    cv = vecs[5:6, :D]
    co = vecs[6:7, :D]
    c2 = vecs[7:8, :D]

    bqkv = jnp.concatenate([cq, jnp.zeros_like(cq), cv], axis=1)

    lane = lax.broadcasted_iota(jnp.int32, (1, LANES), 1)
    low_half = lane < HEAD_DIM

    def colsum(v):
        return jnp.sum(v.reshape(v.shape[0] // 8, 8, v.shape[1]), axis=0)

    def mean(v):
        return jnp.sum(v, axis=-1, keepdims=True) * (1.0 / D)

    def body(size, step, carry):
        rows = size * TP
        chunk = CH if size == G else 16
        share = FF // (3 * size)
        every = slice(0, rows)
        slot = lax.rem(step, 2)
        fetch(step, slot, False)

        @pl.when(step + 1 < steps)
        def _():
            fetch(step + 1, 1 - slot, True)

        for i in range(size):
            live = (step * G + i < items).astype(bf16)
            x = xin[slot, i].astype(f32)
            x_s[pl.ds(i * TP, TOK), :] = x
            x_s[pl.ds(i * TP + TOK, TP - TOK), :] = jnp.broadcast_to(x[TOK - 1:], (TP - TOK, D))
            g_s[pl.ds(i * TP, TOK), :] = gin[slot, i] * live
        for r in range(0, rows, chunk):
            rs = pl.ds(r, chunk)
            v = x_s[rs, :]
            c = v - mean(v)
            inv = lax.rsqrt(mean(c * c) + norm_eps)
            nv = c * inv
            n1_s[rs, :] = nv
            r1_s[rs, :] = jnp.broadcast_to(inv, (chunk, LANES))
            a1_s[rs, :] = (nv * g1 + b1).astype(bf16)
        a1 = a1_s[every, :]
        qkv_s[every, :] = (dot(a1, w_qkv[...]) + bqkv).astype(bf16)
        tail = lax.broadcasted_iota(jnp.int32, (16, 1), 0) < TOK - (TP - 16)
        pairs = [(i, p) for i in range(size) for p in range(HEADS // 2)]

        def masked_q(i, p):
            q = qkv_s[pl.ds(i * TP, TP), slice(p * LANES, (p + 1) * LANES)] * 0.125
            zero = jnp.zeros_like(q)
            return jnp.concatenate([jnp.where(low_half, q, zero), jnp.where(low_half, zero, q)], axis=0)

        def keys(i, p):
            return qkv_s[pl.ds(i * TP, TP), slice(D + p * LANES, D + (p + 1) * LANES)]

        def scores(i, p):
            return dot(masked_q(i, p), keys(i, p), 1, 1)

        s = scores(*pairs[0])
        for at, (i, p) in enumerate(pairs):
            ahead = scores(*pairs[at + 1]) if at + 1 < len(pairs) else None
            cols = slice(p * LANES, (p + 1) * LANES)
            vcols = slice(2 * D + p * LANES, 2 * D + (p + 1) * LANES)
            ve_s[at, :TP - 16, :LANES] = qkv_s[pl.ds(i * TP, TP - 16), vcols]
            last = qkv_s[pl.ds((i + 1) * TP - 16, 16), vcols]
            ve_s[at, TP - 16:, :LANES] = jnp.where(tail, last, jnp.zeros_like(last))
            e = jnp.exp(s - jnp.max(s, axis=-1, keepdims=True)).astype(bf16)
            prob_s[at] = e
            oe = dot(e, ve_s[at])
            inv = 1.0 / jnp.where(low_half, oe[:TP, LANES:], oe[TP:, LANES:])
            o = jnp.where(low_half, oe[:TP, :LANES], oe[TP:, :LANES]) * inv
            inv_s[at] = inv
            of_s[at] = o
            o_s[pl.ds(i * TP, TP), cols] = o.astype(bf16)
            s = ahead
        m_s[every, :] = dot(o_s[every, :], w_o[...])
        for r in range(0, rows, chunk):
            rs = pl.ds(r, chunk)
            v = x_s[rs, :] + m_s[rs, :] + co
            m_s[rs, :] = v
            c = v - mean(v)
            inv = lax.rsqrt(mean(c * c) + norm_eps)
            nv = c * inv
            n2_s[rs, :] = nv
            r2_s[rs, :] = jnp.broadcast_to(inv, (chunk, LANES))
            a2_s[rs, :] = (nv * g2 + b2).astype(bf16)
        a2 = a2_s[every, :]
        gl = g_s[every, :]
        def hidden(j):
            fc = slice(j * FFC, (j + 1) * FFC)
            u_s[0, every, fc] = dot(a2, w_1[:, fc])
            da_s[0, every, fc] = dot(gl, w_2[fc, :], 1, 1)
        hidden(0)
        for j in range(FF // FFC):
            if (j + 1) * FFC < FF:
                hidden(j + 1)
            fc = slice(j * FFC, (j + 1) * FFC)
            c1 = vecs[8:9, fc]
            tot = None
            for r in range(0, rows, chunk):
                rs = pl.ds(r, chunk)
                u = u_s[0, rs, fc] + c1
                phi = 0.5 + 0.5 * lax.erf(u * 0.7071067811865476)
                dens = jnp.exp(u * u * -0.5) * 0.3989422804014327
                act_s[0, rs, fc] = (u * phi).astype(bf16)
                du = (da_s[0, rs, fc] * (phi + u * dens)).astype(bf16)
                du_s[0, rs, fc] = du
                part = colsum(du.astype(f32))
                tot = part if tot is None else tot + part
            vsum[8, :, fc] += tot
        dm_s[every, :] = dot(du_s[0, every, :], w_1[...], 1, 1)
        tg2 = tb2 = tco = tc2 = None
        for r in range(0, rows, chunk):
            rs = pl.ds(r, chunk)
            gw = g_s[rs, :].astype(f32)
            if r == 0:
                acc_s[every, :256] = dot(act_s[0, every, :], w_2[:, :256])
            if r == 6 * chunk:
                acc_s[every, 256:] = dot(act_s[0, every, :], w_2[:, 256:])
            e2 = dm_s[rs, :]
            nv = n2_s[rs, :]
            en = e2 * nv
            eg = e2 * g2
            inv = r2_s[rs, :]
            inv = jnp.concatenate([inv, inv, inv], axis=1)
            dm = gw + inv * (eg - mean(eg) - nv * mean(en * g2))
            dm_s[rs, :] = dm
            db = dm.astype(bf16)
            db_s[rs, :] = db
            sums = (colsum(en), colsum(e2), colsum(db.astype(f32)), colsum(gw))
            if tg2 is None:
                tg2, tb2, tco, tc2 = sums
            else:
                tg2, tb2, tco, tc2 = tg2 + sums[0], tb2 + sums[1], tco + sums[2], tc2 + sums[3]
        vsum[2, :, :D] += tg2
        vsum[3, :, :D] += tb2
        vsum[6, :, :D] += tco
        vsum[7, :, :D] += tc2
        m_s[every, :] = m_s[every, :] + acc_s[every, :] + c2

        db = db_s[every, :]
        g_o[...] += dot(o_s[every, :], db, 0, 0)
        do_s[every, :] = dot(db, w_o[...], 1, 1).astype(bf16)
        def slopes(at):
            i, p = pairs[at]
            do = (do_s[pl.ds(i * TP, TP), slice(p * LANES, (p + 1) * LANES)].astype(f32) * inv_s[at]).astype(bf16)
            zero = jnp.zeros_like(do)
            dom = jnp.concatenate([jnp.where(low_half, do, zero), jnp.where(low_half, zero, do)], axis=0)
            t = of_s[at] * do.astype(f32) * -1.0
            hi = t.astype(bf16)
            lo = pltpu.roll(t - hi.astype(f32), HEAD_DIM, 1).astype(bf16)
            rest = jnp.concatenate([jnp.where(low_half, hi, lo), jnp.where(low_half, lo, hi)], axis=0)
            return dom, dot(jnp.concatenate([dom, rest], axis=1), ve_s[at], 1, 1)

        dom, dp = slopes(0)
        for at, (i, p) in enumerate(pairs):
            ir = pl.ds(i * TP, TP)
            fc = slice(at * share, (at + 1) * share)
            g_1[:, fc] += dot(a2_s[every, :], du_s[0, every, fc], 0, 0)
            e = prob_s[at]
            ds = (e.astype(f32) * dp).astype(bf16)
            dv = dot(dom, e, 0, 0).T
            dk = dot(masked_q(i, p), ds, 0, 0).T
            g_2t[:, fc] += dot(g_s[every, :], act_s[0, every, fc], 0, 0)
            dq2 = dot(ds, keys(i, p) * 0.125)
            dqkv_s[ir, slice(p * LANES, (p + 1) * LANES)] = jnp.where(low_half, dq2[:TP], dq2[TP:]).astype(bf16)
            dqkv_s[ir, slice(D + p * LANES, D + (p + 1) * LANES)] = dk.astype(bf16)
            vcols = slice(2 * D + p * LANES, 2 * D + (p + 1) * LANES)
            dqkv_s[pl.ds(i * TP, TP - 16), vcols] = dv[:TP - 16].astype(bf16)
            dqkv_s[pl.ds((i + 1) * TP - 16, 16), vcols] = jnp.where(tail, dv[TP - 16:], 0.0).astype(bf16)
            dom, dp = slopes(at + 1) if at + 1 < len(pairs) else (None, None)
        dqkv = dqkv_s[every, :]
        acc_s[every, :] = dot(dqkv, w_qkv[...], 1, 1)
        g_qkv[...] += dot(a1_s[every, :], dqkv, 0, 0)
        tg1 = tb1 = tcq = tcv = None
        for r in range(0, rows, chunk):
            rs = pl.ds(r, chunk)
            e1 = acc_s[rs, :]
            nv = n1_s[rs, :]
            en = e1 * nv
            eg = e1 * g1
            inv = r1_s[rs, :]
            inv = jnp.concatenate([inv, inv, inv], axis=1)
            dm_s[rs, :] += inv * (eg - mean(eg) - nv * mean(en * g1))
            sums = (colsum(en), colsum(e1), colsum(dqkv_s[rs, :D].astype(f32)), colsum(dqkv_s[rs, 2 * D:].astype(f32)))
            if tg1 is None:
                tg1, tb1, tcq, tcv = sums
            else:
                tg1, tb1, tcq, tcv = tg1 + sums[0], tb1 + sums[1], tcq + sums[2], tcv + sums[3]
        vsum[0, :, :D] += tg1
        vsum[1, :, :D] += tb1
        vsum[4, :, :D] += tcq
        vsum[5, :, :D] += tcv

        @pl.when(step >= 2)
        def _():
            flush(step - 2, slot, False)

        keep(step, slot, m_s, wide_o, oout)
        keep(step, slot, dm_s, wide_g, gout)
        flush(step, slot, True)
        for group in range(groups):
            @pl.when(step == last_step(group))
            def _():
                group_leaves(group)
        return carry

    lax.fori_loop(0, items // G, functools.partial(body, G), 0)

    @pl.when(items // G < steps)
    def _():
        body(1, steps - 1, 0)

    ends_copies = []
    for ref, (row, height, width) in zip((g_qkv, g_o, g_1), MATS):
        blocks = width // LANES
        for j in range(blocks):
            flat[pl.ds(row + j, height, stride=blocks), :] = ref[:, j * LANES:(j + 1) * LANES]
    row = MATS[3][0]
    for c in range(FF // LANES):
        t = g_2t[:, c * LANES:(c + 1) * LANES].T
        for j in range(3):
            flat[pl.ds(row + 3 * LANES * c + j, LANES, stride=3), :] = t[:, j * LANES:(j + 1) * LANES]
    for k in range(9):
        t = jnp.sum(vsum[k], axis=0, keepdims=True)
        for j in range(12 if k == 8 else 3):
            flat[pl.ds(VEC_ROW + 3 * k + j, 1), :] = t[:, j * LANES:(j + 1) * LANES]
    flat[pl.ds(FLAT_ROWS, flat.shape[0] - FLAT_ROWS), :] = jnp.zeros((flat.shape[0] - FLAT_ROWS, LANES), f32)
    for d in range(n):
        wbuf[places[d]] = flat[pl.ds(8 * first_tile(shard, d), rows_c), :].astype(bf16)
        copy = pltpu.make_async_copy(wbuf.at[places[d]], gbuf_h.at[places[d]], w_sem.at[d])
        copy.start()
        ends_copies.append(copy)

    @pl.when(steps >= 2)
    def _():
        flush(steps - 2, lax.rem(steps, 2), False)
    flush(steps - 1, lax.rem(steps + 1, 2), False)
    zeros_copy(False)
    for group in range(groups):
        ends_copies.extend(group_copies(group))
    for copy in ends_copies:
        copy.wait()


def flat_height(n, shard):
    return 8 * first_tile(shard, n - 1) + chunk_rows(shard)


def block_call(n, shard, cap, ends, other, images, cot, p_images, p_cot, wbuf):
    slots = images.shape[0]
    anyspace = pl.BlockSpec(memory_space=pl.ANY)
    rows_c = chunk_rows(shard)
    groups = slots // FRONT - 1
    scratch = [
        pltpu.VMEM((flat_height(n, shard), LANES), f32),
        pltpu.VMEM((D, 3 * D), bf16), pltpu.VMEM((D, D), bf16), pltpu.VMEM((D, FF), bf16), pltpu.VMEM((FF, D), bf16),
        pltpu.VMEM((16, FF), f32),
        pltpu.VMEM((D, 3 * D), f32), pltpu.VMEM((D, D), f32), pltpu.VMEM((D, FF), f32), pltpu.VMEM((D, FF), f32),
        pltpu.VMEM((9, 8, FF), f32),
        pltpu.VMEM((2, G, TOK, D), bf16), pltpu.VMEM((2, G, TOK, D), bf16),
        pltpu.VMEM((2, G, TOK, D), bf16), pltpu.VMEM((2, G, TOK, D), f32),
        pltpu.VMEM((ROWS, D), f32),
        pltpu.VMEM((ROWS, D), f32), pltpu.VMEM((ROWS, LANES), f32), pltpu.VMEM((ROWS, D), bf16),
        pltpu.VMEM((ROWS, 3 * D), bf16),
        pltpu.VMEM((G * 3, 2 * TP, TP), bf16), pltpu.VMEM((G * 3, TP, 2 * LANES), bf16),
        pltpu.VMEM((G * 3, TP, LANES), f32), pltpu.VMEM((G * 3, TP, LANES), f32),
        pltpu.VMEM((ROWS, D), bf16),
        pltpu.VMEM((ROWS, D), f32),
        pltpu.VMEM((ROWS, D), f32), pltpu.VMEM((ROWS, LANES), f32), pltpu.VMEM((ROWS, D), bf16),
        pltpu.VMEM((ROWS, D), bf16),
        pltpu.VMEM((1, ROWS, FF), f32), pltpu.VMEM((1, ROWS, FF), bf16), pltpu.VMEM((1, ROWS, FF), bf16),
        pltpu.VMEM((ROWS, D), f32),
        pltpu.VMEM((1, ROWS, FF), f32),
        pltpu.VMEM((ROWS, D), f32), pltpu.VMEM((ROWS, D), bf16), pltpu.VMEM((ROWS, D), bf16),
        pltpu.VMEM((ROWS, 3 * D), bf16),
        pltpu.VMEM((TOK, D), bf16), pltpu.VMEM((TOK, D), f32),
        pltpu.VMEM((n, rows_c, LANES), bf16),
        pltpu.VMEM((groups, D // LANES, TOK * FRONT, LANES), f32), pltpu.VMEM((groups, D // LANES, TOK * FRONT, LANES), f32),
        pltpu.VMEM((groups, D // LANES, TOK, FRONT, LANES), bf16),
        pltpu.SemaphoreType.DMA((2, G, 2)), pltpu.SemaphoreType.DMA((2, G, 2)), pltpu.SemaphoreType.DMA((2,)),
        pltpu.SemaphoreType.DMA((n,)), pltpu.SemaphoreType.DMA((groups, 2, D // LANES)),
    ]
    return pl.pallas_call(
        functools.partial(compute_kernel, n, shard, cap, slots),
        name="block",
        out_shape=(
            jax.ShapeDtypeStruct((TOK, slots, D), bf16),
            jax.ShapeDtypeStruct((TOK, slots, D), f32),
            jax.ShapeDtypeStruct((FRONT, TOK, D), bf16),
            jax.ShapeDtypeStruct((FRONT, TOK, D), f32),
            jax.ShapeDtypeStruct((cap,) + images.shape[1:], bf16),
            jax.ShapeDtypeStruct((cap,) + images.shape[1:], f32),
            jax.ShapeDtypeStruct((n, rows_c, LANES), bf16),
        ),
        in_specs=[pl.BlockSpec(memory_space=pltpu.SMEM), pl.BlockSpec(memory_space=pltpu.SMEM)] + [anyspace] * 5,
        out_specs=(anyspace,) * 7,
        scratch_shapes=scratch,
        compiler_params=pltpu.CompilerParams(vmem_limit_bytes=VMEM_LIMIT),
    )(ends, other, images, cot, p_images, p_cot, wbuf)


def chip_axes(n):
    chips = n // 2
    if chips % 16 == 0:
        rest = chips // 4
        side = 2 if rest == 4 else 4
        return (4, rest // side, side)
    return (chips, 1, 1)


class Place:
    def __init__(self, n):
        self.size = chip_axes(n)
        self.stride = (self.size[1] * self.size[2] * 2, self.size[2] * 2, 2)
        self.me = lax.axis_index("dp")
        self.core = lax.rem(self.me, 2)
        self.at = [lax.rem(self.me // self.stride[k], self.size[k]) for k in range(3)]

    def peer(self, axis, hop):
        to = lax.rem(self.at[axis] + hop, self.size[axis])
        return self.me + (to - self.at[axis]) * self.stride[axis]

    def partner(self):
        return self.me + 1 - 2 * self.core

    def slot(self, core, a, b, c):
        return ((core * self.size[1] + b) * self.size[2] + c) * self.size[0] + a

    def everyone(self):
        return [self.peer(k, h) for k in range(3) for h in range(1, self.size[k])] + [self.partner()]


def chunk_places(n):
    A, B, C = chip_axes(n)
    order = [((a * B + b) * C + c) * 2 + core for core in range(2) for b in range(B) for c in range(C) for a in range(A)]
    return [order.index(d) for d in range(n)]


def greet(place):
    barrier = pltpu.get_barrier_semaphore()
    everyone = place.everyone()
    for other in everyone:
        pl.semaphore_signal(barrier, inc=1, device_id=(other,), device_id_type=pl.DeviceIdType.MESH)
    pl.semaphore_wait(barrier, len(everyone))


class Sender:
    def __init__(self, send_sem, recv_sem):
        self.send_sem, self.recv_sem, self.all = send_sem, recv_sem, []

    def go(self, src, dst, device):
        k = len(self.all)
        copy = pltpu.make_async_remote_copy(
            src_ref=src, dst_ref=dst, send_sem=self.send_sem.at[k], recv_sem=self.recv_sem.at[k],
            device_id=(device,), device_id_type=pl.DeviceIdType.MESH)
        copy.start()
        self.all.append([copy, False])
        return copy

    def sent(self, copies):
        for entry in self.all:
            if any(entry[0] is copy for copy in copies) and not entry[1]:
                entry[0].wait_send()
                entry[1] = True

    def finish(self):
        self.sent([entry[0] for entry in self.all])


def arrive(copies):
    for copy in copies:
        copy.wait_recv()


def row_parts(rows, parts):
    tiles = rows // 16
    parts = min(parts, tiles)
    cuts = [tiles * k // parts * 16 for k in range(parts + 1)]
    return [(cuts[k], cuts[k + 1] - cuts[k]) for k in range(parts)]


PARTS = 4
SCATTER_SHARES = (7, 7, 7, 7)


def row_shares(rows, shares):
    tiles = rows // 16
    ends = [tiles * sum(shares[:k]) // sum(shares) * 16 for k in range(len(shares) + 1)]
    return [(ends[k], ends[k + 1] - ends[k]) for k in range(len(shares)) if ends[k + 1] > ends[k]]


SEMS = 192


def gather_kernel(n, cap, chunk, count, images, cot, wbuf_h, other, images_r, cot_r, p_images, p_cot,
                  wbuf, xin, wide, relay, send_sem, recv_sem, in_sem, out_sem, w_sem):
    place = Place(n)
    A, B, C = place.size
    a, b, c = place.at
    core = place.core
    loads = [pltpu.make_async_copy(src, xin.at[k], in_sem.at[k]) for k, src in enumerate((images, cot))]
    for copy in loads:
        copy.start()
    mine = place.slot(core, a, b, c)
    wbuf[mine] = chunk[...].astype(bf16)
    greet(place)
    sender = Sender(send_sem, recv_sem)
    parts = row_parts(chunk.shape[0], PARTS)
    last = len(parts) - 1
    slots = images.shape[1]
    toks = images.shape[0]

    def run(start, length, part):
        return wbuf.at[pl.ds(start, length), pl.ds(part[0], part[1]), :]

    def spread(axis, runs, part):
        return [sender.go(run(s, l, part), run(s, l, part), place.peer(axis, hop))
                for hop in range(1, place.size[axis]) for s, l in runs]

    def pass_on(runs, part):
        return [sender.go(run(s, l, part), run(s, l, part), place.partner()) for s, l in runs]

    def widen(k, t, m):
        v = xin[k, pl.ds(t, m)].reshape(m * slots, D).astype(f32)
        for j in range(D // LANES):
            wide[k, j, pl.ds(t * slots, m * slots), :] = v[:, j * LANES:(j + 1) * LANES]

    def one_slot(k, s, carry):
        for j in range(D // LANES):
            relay[k, s, :, j * LANES:(j + 1) * LANES] = wide[k, j, pl.ds(s, toks, stride=slots), :].astype(bf16)
        return carry

    def chores():
        for k in range(2):
            loads[k].wait()
            for t in range(0, toks, 100):
                widen(k, t, min(100, toks - t))
                yield
            step = -(-slots // 4)
            for s in range(0, slots, step):
                lax.fori_loop(s, min(s + step, slots), functools.partial(one_slot, k), 0)
                yield
            pair.append(sender.go(relay.at[k, pl.ds(0, cap)], (p_images, p_cot)[k], place.partner()))
            stores.append(pltpu.make_async_copy(relay.at[k], (images_r, cot_r)[k], out_sem.at[k]))
            stores[-1].start()
        while True:
            yield

    one, two, three, stores = {}, {}, {}, []
    forwards = [[] for _ in parts]
    one[0] = spread(0, [(mine, 1)], parts[0])
    pair = [sender.go(count, other, place.partner())]

    def second(k):
        arrive(one[k])
        runs = [(place.slot(core, 0, b, c), A)]
        two[k] = spread(2 if k % 2 == 0 else 1, runs, parts[k])
        forwards[k].extend(pass_on(runs, parts[k]))

    def third(k):
        arrive(two[k])
        if k % 2 == 0:
            runs = [(place.slot(core, 0, b, 0), C * A)]
            others = [(place.slot(core, 0, b, lax.rem(c + h, C)), A) for h in range(1, C)]
        else:
            runs = [(place.slot(core, 0, y, c), A) for y in range(B)]
            others = [(place.slot(core, 0, lax.rem(b + h, B), c), A) for h in range(1, B)]
        three[k] = spread(1 if k % 2 == 0 else 2, runs, parts[k])
        forwards[k].extend(pass_on(others, parts[k]))

    def ending(k):
        arrive(three[k])
        if k % 2 == 0:
            others = [(place.slot(core, 0, lax.rem(b + h, B), 0), C * A) for h in range(1, B)]
        else:
            others = [(place.slot(core, 0, y, lax.rem(c + h, C)), A) for h in range(1, C) for y in range(B)]
        forwards[k].extend(pass_on(others, parts[k]))

    chore = chores()
    next(chore)
    for k in range(len(parts)):
        sender.sent(one[k])
        if k < last:
            one[k + 1] = spread(0, [(mine, 1)], parts[k + 1])
        second(k)
        next(chore)
        if k >= 1:
            third(k - 1)
        next(chore)
    third(last)
    for _ in range(4):
        next(chore)
    for k in range(len(parts)):
        ending(k)
    for k, part in enumerate(parts):
        arrive(forwards[k])
        stores.append(pltpu.make_async_copy(wbuf.at[:, pl.ds(*part), :], wbuf_h.at[:, pl.ds(*part), :], w_sem.at[k]))
        stores[-1].start()
    arrive(pair)
    sender.finish()
    for copy in stores:
        copy.wait()


def gather_call(n, cap, chunk, count, images, cot):
    toks, slots, _ = images.shape
    anyspace = pl.BlockSpec(memory_space=pl.ANY)
    vm = pl.BlockSpec(memory_space=pltpu.VMEM)
    return pl.pallas_call(
        functools.partial(gather_kernel, n, cap),
        name="gather",
        out_shape=(
            jax.ShapeDtypeStruct((n,) + chunk.shape, bf16), jax.ShapeDtypeStruct(count.shape, jnp.int32),
            jax.ShapeDtypeStruct((slots, toks, D), bf16), jax.ShapeDtypeStruct((slots, toks, D), bf16),
            jax.ShapeDtypeStruct((cap, toks, D), bf16), jax.ShapeDtypeStruct((cap, toks, D), bf16),
        ),
        in_specs=[vm, vm, anyspace, anyspace],
        out_specs=(anyspace, vm, anyspace, anyspace, anyspace, anyspace),
        scratch_shapes=[
            pltpu.VMEM((n,) + chunk.shape, bf16),
            pltpu.VMEM((2, toks, slots, D), bf16), pltpu.VMEM((2, D // LANES, toks * slots, LANES), f32), pltpu.VMEM((2, slots, toks, D), bf16),
            pltpu.SemaphoreType.DMA((SEMS,)), pltpu.SemaphoreType.DMA((SEMS,)),
            pltpu.SemaphoreType.DMA((2,)), pltpu.SemaphoreType.DMA((2,)), pltpu.SemaphoreType.DMA((PARTS,)),
        ],
        compiler_params=pltpu.CompilerParams(collective_id=0, has_side_effects=True, vmem_limit_bytes=VMEM_LIMIT),
    )(chunk, count, images, cot)


def scatter_kernel(n, cap, gbuf, ends, other, p_out, p_grad, f_out, f_grad, total, out_h, grad_h,
                   half, got0, got1, got2, got3, r_out, r_grad, own_out, own_grad, wide, out_f, grad_f,
                   send_sem, recv_sem, in_sem, half_sem, out_sem):
    place = Place(n)
    A, B, C = place.size
    a, b, c = place.at
    core = place.core
    slots, toks, _ = f_out.shape
    loads = [pltpu.make_async_copy(src, dst, in_sem.at[k])
             for k, (src, dst) in enumerate(((f_out, own_out), (f_grad, own_grad)))]
    for copy in loads:
        copy.start()
    greet(place)
    sender = Sender(send_sem, recv_sem)
    parts = row_shares(gbuf.shape[1], SCATTER_SHARES)
    last = len(parts) - 1
    chips = n // 2
    halves = [pltpu.make_async_copy(gbuf.at[pl.ds(core * chips, chips), pl.ds(*part), :], half.at[:, pl.ds(*part), :], half_sem.at[k])
              for k, part in enumerate(parts)]
    zero = [sender.go(gbuf.at[pl.ds((1 - core) * chips, chips), pl.ds(*part), :], got0.at[:, pl.ds(*part), :], place.partner())
            for part in parts]
    back = [sender.go(p_out, r_out, place.partner()), sender.go(p_grad, r_grad, place.partner())]
    for copy in halves:
        copy.start()
    given = jnp.maximum(ends[0, MB - 1] - other[0, MB - 1], 0) // 2
    stores = []

    def shared(own, sent, k, s, carry):
        for j in range(D // LANES):
            cols = slice(j * LANES, (j + 1) * LANES)
            v = jnp.where(s < given, sent[s, :, cols], own[s, :, cols])
            wide[k, j, pl.ds(s, toks, stride=slots), :] = v.astype(f32)
        return carry

    def single(own, k, s, carry):
        for j in range(D // LANES):
            wide[k, j, pl.ds(s, toks, stride=slots), :] = own[s, :, j * LANES:(j + 1) * LANES].astype(f32)
        return carry

    def chores():
        for k, (own, sent, dst, home) in enumerate(((own_out, r_out, out_f, out_h), (own_grad, r_grad, grad_f, grad_h))):
            loads[k].wait()
            arrive(back[k:k + 1])
            lax.fori_loop(0, cap, functools.partial(shared, own, sent, k), 0)
            yield
            lax.fori_loop(cap, slots, functools.partial(single, own, k), 0)
            for j in range(D // LANES):
                dst[:, j * LANES:(j + 1) * LANES] = wide[k, j].astype(dst.dtype)
            stores.append(pltpu.make_async_copy(dst, home, out_sem.at[k]))
            stores[-1].start()
            yield
        while True:
            yield

    def rows(ref, start, length, part):
        return ref.at[pl.ds(start, length), pl.ds(*part), :]

    def slot(bb, cc):
        return (bb * C + cc) * A

    one, two, three = {}, {}, {}

    def first(k):
        arrive([zero[k]])
        halves[k].wait()
        part = parts[k]
        pr = pl.ds(*part)

        def add(i, carry):
            half[i, pr, :] = (half[i, pr, :].astype(f32) + got0[i, pr, :].astype(f32)).astype(bf16)
            return carry
        lax.fori_loop(0, chips, add, 0, unroll=4)
        sent = []
        if k % 2 == 0:
            for h in range(1, B):
                to = lax.rem(b + h, B)
                sent.append(sender.go(rows(half, slot(to, 0), C * A, part), rows(got1, (h - 1) * C * A, C * A, part), place.peer(1, h)))
        else:
            for h in range(1, C):
                to = lax.rem(c + h, C)
                for y in range(B):
                    sent.append(sender.go(rows(half, slot(y, to), A, part), rows(got1, ((h - 1) * B + y) * A, A, part), place.peer(2, h)))
        one[k] = sent

    def second(k):
        arrive(one[k])
        part = parts[k]
        pr = pl.ds(*part)
        sent = []
        if k % 2 == 0:
            def add(i, carry):
                v = half[slot(b, 0) + i, pr, :].astype(f32)
                for h in range(1, B):
                    v = v + got1[(h - 1) * C * A + i, pr, :].astype(f32)
                half[slot(b, 0) + i, pr, :] = v.astype(bf16)
                return carry
            lax.fori_loop(0, C * A, add, 0, unroll=4)
            for h in range(1, C):
                to = lax.rem(c + h, C)
                sent.append(sender.go(rows(half, slot(b, to), A, part), rows(got2, (h - 1) * A, A, part), place.peer(2, h)))
        else:
            def add(i, carry):
                y = i // A
                z = lax.rem(i, A)
                v = half[slot(y, c) + z, pr, :].astype(f32)
                for h in range(1, C):
                    v = v + got1[((h - 1) * B + y) * A + z, pr, :].astype(f32)
                half[slot(y, c) + z, pr, :] = v.astype(bf16)
                return carry
            lax.fori_loop(0, B * A, add, 0, unroll=4)
            for h in range(1, B):
                to = lax.rem(b + h, B)
                sent.append(sender.go(rows(half, slot(to, c), A, part), rows(got2, (h - 1) * A, A, part), place.peer(1, h)))
        two[k] = sent

    def third(k):
        arrive(two[k])
        part = parts[k]
        pr = pl.ds(*part)
        others = (C if k % 2 == 0 else B) - 1

        def add(i, carry):
            v = half[slot(b, c) + i, pr, :].astype(f32)
            for h in range(others):
                v = v + got2[h * A + i, pr, :].astype(f32)
            half[slot(b, c) + i, pr, :] = v.astype(bf16)
            return carry
        lax.fori_loop(0, A, add, 0, unroll=4)
        sent = []
        for h in range(1, A):
            to = lax.rem(a + h, A)
            sent.append(sender.go(rows(half, slot(b, c) + to, 1, part), rows(got3, h - 1, 1, part), place.peer(0, h)))
        three[k] = sent

    def ending(k):
        arrive(three[k])
        pr = pl.ds(*parts[k])
        v = half[slot(b, c) + a, pr, :].astype(f32)
        for h in range(A - 1):
            v = v + got3[h, pr, :].astype(f32)
        total[pr, :] = v

    chore = chores()
    first(0)
    first(1)
    next(chore)
    for k in range(0, len(parts), 2):
        pair = [j for j in (k, k + 1) if j <= last]
        nxt = [j for j in (k + 2, k + 3) if j <= last]
        for j in pair:
            second(j)
        for j in nxt:
            first(j)
        for j in pair:
            third(j)
        for _ in range(3):
            next(chore)
    for k in range(len(parts)):
        ending(k)
        if k == 0:
            for _ in range(3):
                next(chore)
    sender.finish()
    for copy in stores:
        copy.wait()


def scatter_call(n, cap, gbuf, ends, other, p_out, p_grad, f_out, f_grad):
    A, B, C = chip_axes(n)
    rows_c = gbuf.shape[1]
    slots, toks, _ = f_out.shape
    anyspace = pl.BlockSpec(memory_space=pl.ANY)
    vm = pl.BlockSpec(memory_space=pltpu.VMEM)
    sm = pl.BlockSpec(memory_space=pltpu.SMEM)
    big = max((B - 1) * C * A, (C - 1) * B * A)
    return pl.pallas_call(
        functools.partial(scatter_kernel, n, cap),
        name="scatter",
        out_shape=(jax.ShapeDtypeStruct((rows_c, LANES), f32), jax.ShapeDtypeStruct((toks * slots, D), bf16),
                   jax.ShapeDtypeStruct((toks * slots, D), f32)),
        in_specs=[anyspace, sm, sm, anyspace, anyspace, anyspace, anyspace],
        out_specs=(vm, anyspace, anyspace),
        scratch_shapes=[
            pltpu.VMEM((n // 2, rows_c, LANES), bf16), pltpu.VMEM((n // 2, rows_c, LANES), bf16),
            pltpu.VMEM((big, rows_c, LANES), bf16), pltpu.VMEM((max(B, C) * A, rows_c, LANES), bf16),
            pltpu.VMEM((A, rows_c, LANES), bf16),
            pltpu.VMEM((cap, toks, D), bf16), pltpu.VMEM((cap, toks, D), f32),
            pltpu.VMEM((slots, toks, D), bf16), pltpu.VMEM((slots, toks, D), f32),
            pltpu.VMEM((2, D // LANES, toks * slots, LANES), f32),
            pltpu.VMEM((toks * slots, D), bf16), pltpu.VMEM((toks * slots, D), f32),
            pltpu.SemaphoreType.DMA((SEMS,)), pltpu.SemaphoreType.DMA((SEMS,)),
            pltpu.SemaphoreType.DMA((2,)), pltpu.SemaphoreType.DMA((PARTS,)), pltpu.SemaphoreType.DMA((2,)),
        ],
        compiler_params=pltpu.CompilerParams(collective_id=1, has_side_effects=True, vmem_limit_bytes=VMEM_LIMIT),
    )(gbuf, ends, other, p_out, p_grad, f_out, f_grad)


def pack_shard(n, shard, values):
    me = lax.axis_index("dp")
    offset = lax.rem(shard * me, TILE)
    size = chunk_rows(shard) * LANES
    padded = jnp.pad(values, (TILE, size - shard))
    return lax.dynamic_slice_in_dim(padded, TILE - offset, size, 0).reshape(chunk_rows(shard), LANES)


def unpack_shard(n, shard, chunk):
    me = lax.axis_index("dp")
    offset = lax.rem(shard * me, TILE)
    return lax.dynamic_slice_in_dim(chunk.reshape(-1), offset, shard, 0)


CUTS = 4


def front_kernel(out_in, grad_in, out_f, grad_f, out_t, grad_t, out_v, grad_v, in_sem, out_sem):
    toks = out_f.shape[0]
    step = -(-toks // CUTS)
    moves = []
    for q in range(CUTS):
        rows = pl.ds(q * step, min(step, toks - q * step))
        for k, (src, mid, dst) in enumerate(((grad_f, grad_v, grad_t), (out_f, out_v, out_t))):
            moves.append((pltpu.make_async_copy(src.at[rows], mid.at[rows], in_sem.at[k, q]),
                          pltpu.make_async_copy(mid.at[rows], dst.at[rows, pl.ds(0, FRONT), :], out_sem.at[k, q])))
    for load, _ in moves:
        load.start()
    for load, store in moves:
        load.wait()
        store.start()
    for _, store in moves:
        store.wait()


def front_call(out_t, grad_t, out_f, grad_f):
    anyspace = pl.BlockSpec(memory_space=pl.ANY)
    return pl.pallas_call(
        front_kernel,
        name="front",
        out_shape=tuple(jax.ShapeDtypeStruct(v.shape, v.dtype) for v in (out_t, grad_t)),
        in_specs=[anyspace] * 4,
        out_specs=(anyspace, anyspace),
        scratch_shapes=[pltpu.VMEM(out_f.shape, bf16), pltpu.VMEM(grad_f.shape, f32),
                        pltpu.SemaphoreType.DMA((2, CUTS)), pltpu.SemaphoreType.DMA((2, CUTS))],
        input_output_aliases={0: 0, 1: 1},
        compiler_params=pltpu.CompilerParams(vmem_limit_bytes=VMEM_LIMIT),
    )(out_t, grad_t, out_f, grad_f)


def body(n, images, cotangent, master, moment_one, moment_two, batch_ends):
    shard = master.shape[0]
    cap = CAP
    slots, toks, _ = images.shape
    chunk = pack_shard(n, shard, master)
    wbuf, other, images_r, cot_r, p_images, p_cot = gather_call(
        n, cap, chunk, batch_ends, images.transpose(1, 0, 2), cotangent.transpose(1, 0, 2))
    out_t, grad_t, f_out, f_grad, p_out, p_grad, gbuf = block_call(
        n, shard, cap, batch_ends, other, images_r, cot_r, p_images, p_cot, wbuf)
    part, out_f, grad_f = scatter_call(n, cap, gbuf, batch_ends, other, p_out, p_grad, f_out, f_grad)
    out_t, grad_t = front_call(out_t, grad_t, out_f.reshape(toks, FRONT, D), grad_f.reshape(toks, FRONT, D))
    block_out = out_t.transpose(1, 0, 2)
    input_grad = grad_t.transpose(1, 0, 2)
    weight_grad = unpack_shard(n, shard, part)
    first_moment = beta_one * moment_one + (1.0 - beta_one) * weight_grad
    second_moment = beta_two * moment_two + (1.0 - beta_two) * weight_grad * weight_grad
    corrected_one = first_moment / (1.0 - beta_one**STEP)
    corrected_two = second_moment / (1.0 - beta_two**STEP)
    update = -learn_rate * (
        corrected_one / (jnp.sqrt(corrected_two) + adam_eps) + decay_rate * master
    )
    return (block_out, input_grad, weight_grad, first_moment, second_moment, update)


def solution(mesh):
    n = mesh.shape["dp"]
    return jax.shard_map(
        functools.partial(body, n),
        mesh=mesh,
        in_specs=(P("dp", None, None), P("dp", None, None), P("dp"), P("dp"), P("dp"), P("dp", None)),
        out_specs=(P("dp", None, None), P("dp", None, None), P("dp"), P("dp"), P("dp"), P("dp")),
        check_vma=False,
    )
```
